32 devices in a mesh: leaf: 8 (over z, y), front: 4 (over x, core).
Axes of the slice: x: 2, y: 2, z: 4, core: 2. Of those that a mesh axis runs over, the one named last changes fastest.
Arguments:
- leaf_fronts: float32 [8, 1, 2048, 2048], P('leaf', None, 'front'), may hold values from -40 to 40, as said below
- screen_weights: float32 [8, 1, 2048], P('leaf', None, 'front'), may hold values from 0.1 to 2
- parent_tile_index: int32 [8, 1, 12], replicated, may hold values from 0 to 31, as said below
Outputs:
- leaf_panel: float32 [8, 1, 2048, 512], P('leaf', None, 'front')
- parent_panel: float32 [8, 1, 2048, 128], P('leaf', None, 'front')
- parent_update: float32 [8, 1, 2048, 3968], P('leaf', None, 'front')
The draws below stay inside these ranges and needn't reach their ends.
Inputs may be any that keep to these rules, and one draw needn't show every extreme that they name: `leaf_fronts`: each first-level front is symmetric positive definite. `parent_tile_index`: entry [i, g, a] is the tile of parent (i // 2, g) that receives contribution tile t = 4 * (a // 3) + a % 3 + 1 of front (i, g); tile p covers rows p * 128 to (p + 1) * 128 - 1. The entries of one front are distinct, tile 1 always goes to parent tile 0, and p * 128 // 1024 == t * 128 // 512.
All inputs are finite; a program needn't handle non-finite values.
Results may differ from the reference program's by a relative error of at most 0.00013.
Values sent between devices are 32-bit elements; how exact they have to be, the bound alone decides.
No kernel may reach another device: no remote copies, remote signals or barrier semaphores. Data moves between devices by JAX's collectives and lax.ppermute only.
A program may use at most 128 MiB of HBM per device.

```python
import math
import jax
import jax.numpy as jnp
from jax import lax

SEPARATOR_ONE = 512
SEP2 = 1024
PANEL_WIDTH = 128
FRONTS_PER_LEVEL = 1
FRONT_ORDER_M1 = 2048
M2 = 4096
LEAVES = 8
ROWS1 = 512
ROWS2 = 512
FRONT_TILES_ONE = 16
ELIMINATED_TILES = 4
N_FRONT = 4


def draw_leaf_fronts(key, part):
    first, second, third = jax.random.split(key, 3)
    shape = (LEAVES, FRONTS_PER_LEVEL, FRONT_ORDER_M1, FRONT_ORDER_M1)
    raw = jnp.clip(jax.random.normal(first, shape, jnp.float32), -4.0, 4.0) * (1.15 / math.sqrt(FRONT_ORDER_M1))
    diagonal = 2.5 + jax.random.uniform(second, (LEAVES, FRONTS_PER_LEVEL, FRONT_ORDER_M1), jnp.float32)
    coupling = jnp.clip(jax.random.normal(third, (LEAVES, FRONTS_PER_LEVEL, FRONT_ORDER_M1, PANEL_WIDTH), jnp.float32), -4.0, 4.0)
    coupling = coupling * (1.5 / math.sqrt(PANEL_WIDTH))
    symmetric = 0.5 * (raw + jnp.swapaxes(raw, 2, 3))
    row_ids = lax.broadcasted_iota(jnp.int32, (1, 1, FRONT_ORDER_M1, FRONT_ORDER_M1), 2)
    col_ids = lax.broadcasted_iota(jnp.int32, (1, 1, FRONT_ORDER_M1, FRONT_ORDER_M1), 3)
    base = jnp.where(row_ids == col_ids, diagonal[:, :, :, None], symmetric)
    return base + jnp.einsum('lgnp,lgmp->lgnm', coupling, coupling, precision=lax.Precision.HIGHEST)


def draw_parent_tile_index(key, part):
    blocks = FRONT_ORDER_M1 // ROWS1
    count = ROWS1 // PANEL_WIDTH
    slots = 2 * count
    shape = (LEAVES, FRONTS_PER_LEVEL, blocks, slots)
    scores = jax.random.randint(key, shape, 0, 2 ** 24)
    slot_ids = lax.broadcasted_iota(jnp.int32, shape, 3)
    block_ids = lax.broadcasted_iota(jnp.int32, shape, 2)
    leaf_ids = lax.broadcasted_iota(jnp.int32, shape, 0)
    member_ids = lax.broadcasted_iota(jnp.int32, shape, 1)
    forced_zero = (block_ids == 0) & (slot_ids == 0)
    forced_last = (leaf_ids == 0) & (member_ids == 0) & (block_ids == blocks - 1) & (slot_ids == slots - 1)
    scores = jnp.where(forced_zero | forced_last, -1, scores)
    ranked = scores * 64 + slot_ids
    order = jnp.argsort(ranked, axis=3)[:, :, :, :count].astype(jnp.int32)
    shifted = jnp.concatenate([order[:, :, :, :1], order[:, :, :, :count - 1]], axis=3)
    reversed_order = jnp.flip(order, axis=3)
    first_block = lax.broadcasted_iota(jnp.int32, (LEAVES, FRONTS_PER_LEVEL, blocks, count), 2) == 0
    assigned = jnp.where(first_block, shifted, reversed_order)
    block_base = lax.broadcasted_iota(jnp.int32, (LEAVES, FRONTS_PER_LEVEL, blocks, count), 2) * slots
    full = (block_base + assigned).reshape(LEAVES, FRONTS_PER_LEVEL, blocks * count // 4, 4)
    kept_block = full[:, :, :, 1:]
    return kept_block.reshape(LEAVES, FRONTS_PER_LEVEL, 3 * (blocks * count // 4)).astype(jnp.int32)


def shard_levels(rng, dims, pieces, least, high):
    def one(position, shards_of):
        steps = jax.random.uniform(jax.random.fold_in(jax.random.fold_in(rng, 6), position), (shards_of,), jnp.float32, least / len(pieces), high / len(pieces))
        return jnp.repeat(jnp.exp(steps), dims[position] // shards_of).reshape((-1,) + (1,) * (len(dims) - position - 1))

    gain = one(*pieces[0])
    for cut in pieces[1:]:
        gain = gain * one(*cut)
    return gain


def setup_inputs(seed: int = 0) -> dict:
    splits = jax.random.split(jax.random.key(seed), 4)
    leaf_fronts = draw_leaf_fronts(jax.random.fold_in(splits[3], 71), 0)
    screen_weights = jnp.clip(jnp.exp(math.log(2.0) - 2.9957323 * jax.random.uniform(splits[1], (LEAVES, FRONTS_PER_LEVEL, M2 // 2), jnp.float32) ** shard_levels(splits[1], (LEAVES, FRONTS_PER_LEVEL, M2 // 2), ((0, 8), (2, 4)), -0.2, 0.2)), 0.1, 2.0)
    parent_tile_index = draw_parent_tile_index(jax.random.fold_in(splits[3], 71), 0)
    return dict(leaf_fronts=leaf_fronts, screen_weights=screen_weights, parent_tile_index=parent_tile_index)


def invert_block(corner_block):
    factor = jnp.linalg.cholesky(corner_block)
    identity = jnp.eye(corner_block.shape[-1], dtype=jnp.float32)
    return jax.scipy.linalg.solve_triangular(factor, identity, lower=True)

def factor_leaf(front_matrix):
    column_block = front_matrix.reshape(FRONT_ORDER_M1, ELIMINATED_TILES, 4, PANEL_WIDTH)[:, :, 0, :].reshape(FRONT_ORDER_M1, SEPARATOR_ONE)
    corner_block = column_block.reshape(ELIMINATED_TILES, 4, PANEL_WIDTH, SEPARATOR_ONE)[:, 0].reshape(SEPARATOR_ONE, SEPARATOR_ONE)
    inverse = invert_block(corner_block)
    return jnp.dot(column_block, inverse.T, precision=lax.Precision.HIGHEST)

def factor_parent(parent):
    inverse = invert_block(parent[:PANEL_WIDTH, :PANEL_WIDTH])
    return jnp.dot(parent[:, :PANEL_WIDTH], inverse.T, precision=lax.Precision.HIGHEST)

def parent_base(weights_natural):
    row_ids = lax.broadcasted_iota(jnp.int32, (M2, M2), 0)
    col_ids = lax.broadcasted_iota(jnp.int32, (M2, M2), 1)
    inside = row_ids < SEP2
    diagonal = jnp.where(row_ids == col_ids, weights_natural[:, None] + jnp.where(inside, 4.0, 0.0), 0.0)
    neighbour = jnp.where(inside & (col_ids < SEP2) & (jnp.abs(row_ids - col_ids) == 1), 1.0, 0.0)
    return diagonal - neighbour

def contribution(schur_update):
    kept_block = 3 * SEPARATOR_ONE
    row_block = schur_update.reshape(ELIMINATED_TILES, 4, PANEL_WIDTH, FRONT_ORDER_M1)[:, 1:].reshape(kept_block, FRONT_ORDER_M1)
    return row_block.reshape(kept_block, ELIMINATED_TILES, 4, PANEL_WIDTH)[:, :, 1:].reshape(kept_block, kept_block)

def add_child(parent, schur_update, child_map):
    tile_blocks = 3 * ELIMINATED_TILES
    count = M2 // PANEL_WIDTH
    inner = contribution(schur_update).reshape(tile_blocks, PANEL_WIDTH, tile_blocks, PANEL_WIDTH).transpose(0, 2, 1, 3)
    grid = parent.reshape(count, PANEL_WIDTH, count, PANEL_WIDTH).transpose(0, 2, 1, 3)
    grid = grid.at[child_map[:, None], child_map[None, :]].add(inner)
    return grid.transpose(0, 2, 1, 3).reshape(M2, M2)

def device_rows(matrix):
    width = matrix.shape[1]
    split = matrix.reshape(N_FRONT, 2, ROWS2, width).transpose(1, 0, 2, 3)
    return split.reshape(2, N_FRONT * ROWS2, width)

def one_pair(inputs):
    pair_fronts, pair_weights, pair_maps = inputs
    leaf_list, panel_list, update_list = ([], [], [])
    for member in range(FRONTS_PER_LEVEL):
        panels = []
        schurs = []
        for child in range(2):
            front_matrix = pair_fronts[child, member]
            panel = factor_leaf(front_matrix)
            panels.append(panel)
            schurs.append(front_matrix - jnp.dot(panel, panel.T, precision=lax.Precision.HIGHEST))
        natural = pair_weights[:, member].reshape(2, N_FRONT, ROWS2).transpose(1, 0, 2).reshape(M2)
        parent = parent_base(natural)
        parent = add_child(parent, schurs[0], pair_maps[0, member])
        parent = add_child(parent, schurs[1], pair_maps[1, member])
        panel_two = factor_parent(parent)
        update = parent[:, PANEL_WIDTH:] - jnp.dot(panel_two, panel_two[PANEL_WIDTH:, :].T, precision=lax.Precision.HIGHEST)
        leaf_list.append(jnp.stack(panels))
        panel_list.append(device_rows(panel_two))
        update_list.append(device_rows(update))
    return (jnp.stack(leaf_list, 1), jnp.stack(panel_list, 1), jnp.stack(update_list, 1))

def reference(leaf_fronts, screen_weights, parent_tile_index):
    front_pairs = LEAVES // 2
    fronts_paired = leaf_fronts.reshape(front_pairs, 2, FRONTS_PER_LEVEL, FRONT_ORDER_M1, FRONT_ORDER_M1)
    weights_paired = screen_weights.reshape(front_pairs, 2, FRONTS_PER_LEVEL, M2 // 2)
    paired_tile_maps = parent_tile_index.reshape(front_pairs, 2, FRONTS_PER_LEVEL, FRONT_TILES_ONE - ELIMINATED_TILES)
    leaf_all, panel_all, update_all = lax.map(one_pair, (fronts_paired, weights_paired, paired_tile_maps))
    leaf_panel = leaf_all.reshape(LEAVES, FRONTS_PER_LEVEL, FRONT_ORDER_M1, SEPARATOR_ONE)
    parent_panel = panel_all.reshape(LEAVES, FRONTS_PER_LEVEL, M2 // 2, PANEL_WIDTH)
    parent_update = update_all.reshape(LEAVES, FRONTS_PER_LEVEL, M2 // 2, M2 - PANEL_WIDTH)
    return (leaf_panel, parent_panel, parent_update)
```

```python
import functools

import jax
import jax.numpy as jnp
from jax import lax
from jax.experimental import pallas as pl
from jax.experimental.pallas import tpu as pltpu
from jax.sharding import PartitionSpec as P

SEP2 = 1024
PANEL_WIDTH = 128
M2 = 4096
GROUP_TILES = 4
SLAB = 8
GROUP = 32
EXACT = lax.Precision.HIGHEST
VMEM_BYTES = 60 * 2**20

TILE = PANEL_WIDTH
LAST = ((1,), (1,))
PLAIN = ((1,), (0,))
FIRST = ((0,), (0,))


def from_front(value, distance):
    pairs = [(source, source ^ distance) for source in range(lax.axis_size("front"))]
    return lax.ppermute(value, "front", pairs)


def from_sibling(value):
    pairs = [(source, source ^ 1) for source in range(lax.axis_size("leaf"))]
    return lax.ppermute(value, "leaf", pairs)


def slot_of(offset, count):
    slot, bit, weight = 0, 1, count // 2
    while weight:
        slot = slot + jnp.where((offset & bit) != 0, weight, 0)
        bit, weight = bit * 2, weight // 2
    return slot


def offset_of(slot, count):
    offset, bit, weight = 0, 1, count // 2
    while weight:
        offset += bit if slot & weight else 0
        bit, weight = bit * 2, weight // 2
    return offset


def gather_front(value):
    held = value[None]
    distance = lax.axis_size("front") // 2
    while distance:
        held = jnp.concatenate([held, from_front(held, distance)], axis=0)
        distance //= 2
    return held


def exact_dot(left, right, contract):
    return lax.dot_general(
        left, right, (contract, ((), ())), precision=EXACT, preferred_element_type=jnp.float32
    )


def halves(value):
    high = value.astype(jnp.bfloat16)
    return high, (value - high.astype(jnp.float32)).astype(jnp.bfloat16)


def split_dot(left, right, contract=LAST):
    dot = functools.partial(
        lax.dot_general, dimension_numbers=(contract, ((), ())), preferred_element_type=jnp.float32
    )
    return dot(left[0], right[0]) + (dot(left[0], right[1]) + dot(left[1], right[0]))


def lane(row, index):
    return jnp.broadcast_to(row[:, index : index + 1], row.shape)


def sum_tree(terms):
    while len(terms) > 1:
        terms = [sum(terms[i : i + 2]) for i in range(0, len(terms), 2)]
    return terms[0]


def factor_slab(rows, extra, first):
    entry = {}
    for i in range(SLAB):
        for j in range(i + 1):
            entry[i, j] = lane(rows[i], first + j)
    for j in range(SLAB):
        scale = lax.rsqrt(entry[j, j])
        rows[j] = rows[j] * scale
        extra[j] = extra[j] * scale
        for i in range(j + 1, SLAB):
            entry[i, j] = entry[i, j] * scale
        for i in range(j + 1, SLAB):
            for k in range(j + 1, i + 1):
                entry[i, k] = entry[i, k] - entry[i, j] * entry[k, j]
        for i in range(j + 1, SLAB):
            rows[i] = rows[i] - entry[i, j] * rows[j]
            extra[i] = extra[i] - entry[i, j] * extra[j]


def factor_tile(a, b, fronts):
    row_ids = lax.broadcasted_iota(jnp.int32, (fronts * TILE, TILE), 0)
    col_ids = lax.broadcasted_iota(jnp.int32, (fronts * TILE, TILE), 1) * fronts
    b[...] = ((row_ids >= col_ids) & (row_ids < col_ids + fronts)).astype(jnp.float32)

    def at(i):
        return pl.ds(fronts * i, fronts)

    for start in range(0, TILE, GROUP):
        stop = start + GROUP
        rows = [a[at(i), :] for i in range(start, stop)]
        extra = [b[at(i), :] for i in range(start, stop)]
        for s in range(0, GROUP, SLAB):
            head, head_extra = rows[s : s + SLAB], extra[s : s + SLAB]
            factor_slab(head, head_extra, start + s)
            rows[s : s + SLAB], extra[s : s + SLAB] = head, head_extra
            for i in range(s + SLAB, GROUP):
                factors = [lane(row, start + i) for row in head]
                rows[i] = rows[i] - sum_tree([f * r for f, r in zip(factors, head)])
                extra[i] = extra[i] - sum_tree([f * r for f, r in zip(factors, head_extra)])
        for i in range(GROUP):
            a[at(start + i), :] = rows[i]
            b[at(start + i), :] = extra[i]
        if stop < TILE:
            for q in range(fronts):
                done = pl.ds(fronts * start + q, GROUP, stride=fronts)
                rest = pl.ds(fronts * stop + q, TILE - stop, stride=fronts)
                upper, inverse = a[done, :], b[done, :]
                both = exact_dot(upper, jnp.concatenate([upper, inverse], axis=1), FIRST)[stop:]
                a[rest, :] = a[rest, :] - both[:, :TILE]
                b[rest, :] = b[rest, :] - both[:, TILE:]


def corner_kernel(*refs, order, first, last):
    tiles = order // TILE
    if first == 0:
        slots, slabs, work, out, a, b = refs
    else:
        old_work, old_out, out, work, a, b = refs
    fronts = out.shape[0]
    if first == 0:
        for e in range(tiles):
            for q in range(fronts):
                work[q, e * TILE : (e + 1) * TILE, :] = slabs[slots[e], q, :TILE, :]
    else:
        work[...] = old_work[...]
        out[...] = old_out[...]

    def step(k, carry):
        block = pl.ds(pl.multiple_of(k * TILE, TILE), TILE)
        for q in range(fronts):
            a[pl.ds(q, TILE, stride=fronts), :] = work[q, block, block]
        factor_tile(a, b, fronts)
        for q in range(fronts):
            out[q, block, block] = b[pl.ds(q, TILE, stride=fronts), :]
        for fixed in range(first, last):

            @pl.when(k == fixed)
            def _():
                here = slice(fixed * TILE, (fixed + 1) * TILE)
                low, rest = slice(0, fixed * TILE), slice((fixed + 1) * TILE, order)
                for q in range(fronts):
                    corner = out[q, here, here]
                    if fixed:
                        chain = exact_dot(work[q, here, low], out[q, low, low], PLAIN)
                        out[q, here, low] = -exact_dot(corner, chain, PLAIN)
                    if fixed + 1 < tiles:
                        out[q, here, rest] = jnp.zeros((TILE, order - (fixed + 1) * TILE), jnp.float32)
                        below = exact_dot(work[q, rest, here], corner, LAST)
                        work[q, rest, here] = below
                        work[q, rest, rest] = work[q, rest, rest] - exact_dot(below, below, LAST)

        return carry

    lax.fori_loop(first, last, step, 0)


def invert_corners(slots, slabs, order):
    fronts = slabs.shape[1]
    vmem, smem = pl.BlockSpec(memory_space=pltpu.VMEM), pl.BlockSpec(memory_space=pltpu.SMEM)
    state = jax.ShapeDtypeStruct((fronts, order, order), jnp.float32)
    tile = pltpu.VMEM((fronts * TILE, TILE), jnp.float32)
    middle = order // TILE // 2
    params = pltpu.CompilerParams(vmem_limit_bytes=VMEM_BYTES)
    cost = pl.CostEstimate(flops=15 * 10**9, bytes_accessed=2**23, transcendentals=0)
    work, out = pl.pallas_call(
        functools.partial(corner_kernel, order=order, first=0, last=middle),
        out_shape=(state, state),
        in_specs=[smem, vmem],
        out_specs=(vmem, vmem),
        scratch_shapes=[tile, tile],
        compiler_params=params,
        cost_estimate=cost,
        name="corner_first",
    )(slots, slabs)
    return pl.pallas_call(
        functools.partial(corner_kernel, order=order, first=middle, last=order // TILE),
        out_shape=state,
        in_specs=[vmem, vmem],
        out_specs=vmem,
        scratch_shapes=[pltpu.VMEM((fronts, order, order), jnp.float32), tile, tile],
        compiler_params=params,
        cost_estimate=cost,
        name="corner_second",
    )(work, out)


def parent_kernel(
    place, maps, fronts_here, far, slab, edge, inverse, weights,
    leaf_panel, parent_panel, parent_update,
    panel_high, panel_low, column, two_high, two_low, a, b, *, count, skip, width, devices,
):
    front, half = place[0], place[1]
    sent = count - skip
    separator = width // GROUP_TILES
    rows = count * TILE
    first_row = pl.multiple_of((front * 2 + half) * rows, TILE)
    tiles = width // TILE

    def at(tile):
        return pl.ds(pl.multiple_of(tile * TILE, TILE), TILE)

    for i in range(2):
        turned = halves(inverse[i])
        if skip and i == 0:
            leaf_panel[:TILE, :] = split_dot(halves(slab[:TILE, :]), turned)
        for s in range(devices):
            panel = split_dot(halves(edge[s, i, :, :separator]), turned)
            if s == 0 and i == 0:
                leaf_panel[skip * TILE :, :] = panel
            panel_high[i, s], panel_low[i, s] = halves(panel)

    column[...] = jnp.zeros_like(column)
    row_ids = lax.broadcasted_iota(jnp.int32, (TILE, TILE), 0)
    col_ids = lax.broadcasted_iota(jnp.int32, (TILE, TILE), 1)
    near = jnp.where(jnp.abs(row_ids - col_ids) == 1, 1.0, 0.0)
    column[:TILE, :] = jnp.where(row_ids == col_ids, weights[0:1, :TILE] + 4.0, 0.0) - near
    column[TILE : 2 * TILE, :] = -jnp.where((row_ids == 0) & (col_ids == TILE - 1), 1.0, 0.0)
    tile_one = (1 - skip) * TILE
    for i in range(2):
        slot = place[2]
        one = (
            panel_high[i, slot, tile_one : tile_one + TILE, :],
            panel_low[i, slot, tile_one : tile_one + TILE, :],
        )
        for s in range(devices):
            piece = edge[s, i, :, separator:] - split_dot((panel_high[i, s], panel_low[i, s]), one)
            owner = front ^ offset_of(s, devices)
            for t in range(sent):
                target = maps[i, owner * count + skip + t]

                @pl.when(target >= 0)
                def _():
                    column[at(target), :] += piece[t * TILE : (t + 1) * TILE, :]

    a[...] = column[:TILE, :]
    factor_tile(a, b, 1)
    turned = halves(b[...])
    for start in range(0, M2, 1024):
        block = slice(start, start + 1024)
        panel = split_dot(halves(column[block, :]), turned)
        column[block, :] = panel
        two_high[block, :], two_low[block, :] = halves(panel)
    mine = pl.ds(first_row, rows)
    parent_panel[...] = column[mine, :]

    own = two_high[mine, :], two_low[mine, :]
    weight = jnp.transpose(jnp.broadcast_to(weights[1:2, :rows], (TILE, rows)))
    for start in range(TILE, M2, 1024):
        stop = min(start + 1024, M2)
        product = split_dot(own, (two_high[start:stop, :], two_low[start:stop, :]))
        parent_update[:, start - TILE : stop - TILE] = -product
    inside = first_row < SEP2
    diagonal = jnp.where(inside, 4.0, 0.0)
    for j in range(count):
        here = (front * 2 + half) * count + j
        line = slice(j * TILE, (j + 1) * TILE)

        @pl.when(here > 0)
        def _():
            middle = jnp.where(row_ids == col_ids, weight[line, :] + diagonal, 0.0) - jnp.where(inside, near, 0.0)
            parent_update[line, at(here - 1)] += middle

        @pl.when((here > 1) & inside)
        def _():
            parent_update[line, at(here - 2)] -= jnp.where((row_ids == 0) & (col_ids == TILE - 1), 1.0, 0.0)

        @pl.when((here + 1) * TILE < SEP2)
        def _():
            parent_update[line, at(here)] -= jnp.where((row_ids == TILE - 1) & (col_ids == 0), 1.0, 0.0)

    for i in range(2):
        for t in range(sent):
            target = maps[i, front * count + skip + t] - (front * 2 + half) * count

            @pl.when((target >= 0) & (target < count))
            def _():
                line = slice(t * TILE, (t + 1) * TILE)
                left = panel_high[i, 0, line, :], panel_low[i, 0, line, :]
                for s in range(devices):
                    product = split_dot(left, (panel_high[i, s], panel_low[i, s]))
                    owner = front ^ offset_of(s, devices)
                    for c in range(sent):
                        tile = owner * count + skip + c
                        goal = maps[i, tile]

                        @pl.when(goal > 0)
                        def _():
                            if i == 0:
                                source = fronts_here[(skip + t) * TILE : (skip + t + 1) * TILE, at(tile)]
                            else:
                                group = tile // GROUP_TILES
                                source = far[line, at(tile - group - 2)]
                            parent_update[at(target), at(goal - 1)] += (
                                source - product[:, c * TILE : (c + 1) * TILE]
                            )


def full_map(child_map):
    grouped = child_map.reshape(-1, GROUP_TILES - 1)
    opening = jnp.full((grouped.shape[0], 1), -1, jnp.int32)
    return jnp.concatenate([opening, grouped], axis=1).reshape(-1)


def one_front(matrix, weights, own_map, sibling_map, front, half):
    rows, width = matrix.shape
    devices = lax.axis_size("front")
    count, tiles = rows // TILE, width // TILE
    skip = 1 if count % GROUP_TILES == 0 else 0
    separator = width // GROUP_TILES
    sent = (count - skip) * TILE
    others = jnp.arange(devices, dtype=jnp.int32)
    slots = slot_of(front ^ others, devices)

    def columns(block, chosen):
        return jnp.concatenate([block[:, t * TILE : (t + 1) * TILE] for t in chosen], axis=1)

    corner = list(range(0, tiles, GROUP_TILES))
    rest = [t for t in range(tiles) if t % GROUP_TILES and t != 1]
    weight_row = jnp.pad(weights[None], ((0, SLAB - 1), (0, separator - rows)))
    slab = jnp.concatenate([columns(matrix[:TILE], corner), weight_row], axis=0)
    far_slab = from_sibling(slab)
    slabs = gather_front(jnp.stack([slab, far_slab]))
    body = matrix[skip * TILE :]
    edge = columns(body, corner + [1])
    far_edge = from_sibling(edge)
    far = from_sibling(columns(body, rest))
    edges = gather_front(jnp.stack([edge, far_edge]))

    corner_owner = jnp.arange(GROUP_TILES, dtype=jnp.int32) * GROUP_TILES // count
    corner_slots = slot_of(front ^ corner_owner, devices)
    inverse = invert_corners(corner_slots, slabs, separator)

    first = lax.dynamic_index_in_dim(slabs, slots[0], 0, keepdims=False)[:, TILE, :]
    head = jnp.where(half == 0, first[0], first[1])
    two_weights = jnp.pad(jnp.stack([head, weight_row[0]]), ((0, SLAB - 2), (0, 0)))
    place = jnp.concatenate([jnp.stack([front, half]), slots]).astype(jnp.int32)
    maps = jnp.stack([own_map, sibling_map])
    vmem, smem = pl.BlockSpec(memory_space=pltpu.VMEM), pl.BlockSpec(memory_space=pltpu.SMEM)
    f32, bf16 = jnp.float32, jnp.bfloat16
    return pl.pallas_call(
        functools.partial(parent_kernel, count=count, skip=skip, width=width, devices=devices),
        out_shape=(
            jax.ShapeDtypeStruct((rows, separator), f32),
            jax.ShapeDtypeStruct((rows, TILE), f32),
            jax.ShapeDtypeStruct((rows, M2 - TILE), f32),
        ),
        in_specs=[smem, smem] + [vmem] * 6,
        out_specs=(vmem, vmem, vmem),
        scratch_shapes=[
            pltpu.VMEM((2, devices, sent, separator), bf16),
            pltpu.VMEM((2, devices, sent, separator), bf16),
            pltpu.VMEM((M2, TILE), f32),
            pltpu.VMEM((M2, TILE), bf16),
            pltpu.VMEM((M2, TILE), bf16),
            pltpu.VMEM((TILE, TILE), f32),
            pltpu.VMEM((TILE, TILE), f32),
        ],
        compiler_params=pltpu.CompilerParams(vmem_limit_bytes=VMEM_BYTES),
        cost_estimate=pl.CostEstimate(flops=15 * 10**9, bytes_accessed=2**25, transcendentals=0),
        name="parent",
    )(place, maps, matrix, far, slab, edges, inverse, two_weights)


def on_device(leaf_fronts, screen_weights, parent_tile_index):
    front = lax.axis_index("front")
    leaf = lax.axis_index("leaf")
    half = leaf % 2
    own = lax.dynamic_index_in_dim(parent_tile_index, leaf, 0, keepdims=False)
    sibling = lax.dynamic_index_in_dim(parent_tile_index, leaf ^ 1, 0, keepdims=False)
    results = [
        one_front(leaf_fronts[0, g], screen_weights[0, g], full_map(own[g]), full_map(sibling[g]), front, half)
        for g in range(leaf_fronts.shape[1])
    ]
    return tuple(jnp.stack(parts)[None] for parts in zip(*results))


def solution(mesh):
    in_specs = (P("leaf", None, "front", None), P("leaf", None, "front"), P())
    out_specs = (
        P("leaf", None, "front", None),
        P("leaf", None, "front", None),
        P("leaf", None, "front", None),
    )
    return jax.shard_map(
        on_device, mesh=mesh, in_specs=in_specs, out_specs=out_specs, check_vma=False
    )
```

```python
import functools

import jax
import jax.numpy as jnp
from jax import lax
from jax.experimental import pallas as pl
from jax.experimental.pallas import tpu as pltpu
from jax.sharding import PartitionSpec as P

SEP2 = 1024
PANEL_WIDTH = 128
M2 = 4096
GROUP_TILES = 4
SLAB = 8
EXACT = lax.Precision.HIGHEST
VMEM_BYTES = 60 * 2**20

TILE = PANEL_WIDTH
LAST = ((1,), (1,))
PLAIN = ((1,), (0,))


def from_front(value, distance):
    pairs = [(source, source ^ distance) for source in range(lax.axis_size("front"))]
    return lax.ppermute(value, "front", pairs)


def from_sibling(value):
    pairs = [(source, source ^ 1) for source in range(lax.axis_size("leaf"))]
    return lax.ppermute(value, "leaf", pairs)


def after(value, *events):
    return lax.optimization_barrier((value, *events))[0]


def slot_of(offset, count):
    slot, bit, weight = 0, 1, count // 2
    while weight:
        slot = slot + jnp.where((offset & bit) != 0, weight, 0)
        bit, weight = bit * 2, weight // 2
    return slot


def offset_of(slot, count):
    offset, bit, weight = 0, 1, count // 2
    while weight:
        offset += bit if slot & weight else 0
        bit, weight = bit * 2, weight // 2
    return offset


def exact_dot(left, right, contract):
    return lax.dot_general(
        left, right, (contract, ((), ())), precision=EXACT, preferred_element_type=jnp.float32
    )


def plain_dot(left, right):
    return lax.dot_general(left, right, (LAST, ((), ())), preferred_element_type=jnp.float32)


def halves(value):
    high = value.astype(jnp.bfloat16)
    return high, (value - high.astype(jnp.float32)).astype(jnp.bfloat16)


def split_dot(left, right):
    return plain_dot(left[0], right[0]) + (plain_dot(left[0], right[1]) + plain_dot(left[1], right[0]))


def lane(row, index):
    return jnp.broadcast_to(row[:, index : index + 1], row.shape)


def sum_tree(terms):
    while len(terms) > 1:
        terms = [sum(terms[i : i + 2]) for i in range(0, len(terms), 2)]
    return terms[0]


def factor_slab(block, first, inside, lanes):
    rows = [jnp.broadcast_to(block[i : i + 1, :], block.shape) for i in range(SLAB)]
    entry = {(i, j): lane(rows[i], first + j) for i in range(SLAB) for j in range(i + 1)}
    rows = [
        jnp.where(inside, jnp.where(lanes == first + i, 1.0, 0.0), row) for i, row in enumerate(rows)
    ]
    done = []
    for p in range(0, SLAB, 2):
        r = p + 1
        one, mixed, two = entry[p, p], entry[r, p], entry[r, r]
        inverse_one = pl.reciprocal(one, approx=True)
        inverse_two = pl.reciprocal(one * two - mixed * mixed, approx=True) * one
        factor = {i: entry[i, p] * inverse_one for i in range(r, SLAB)}
        rows[r] = rows[r] - factor[r] * rows[p]
        for i in range(p + 2, SLAB):
            entry[i, r] = entry[i, r] - factor[i] * mixed
        for i in range(p + 2, SLAB):
            second = entry[i, r] * inverse_two
            for k in range(p + 2, i + 1):
                entry[i, k] = (entry[i, k] - factor[i] * entry[k, p]) - second * entry[k, r]
            rows[i] = (rows[i] - factor[i] * rows[p]) - second * rows[r]
        done.append(rows[p] * lax.rsqrt(one))
        done.append(rows[r] * (inverse_two * lax.rsqrt(inverse_two)))
    return done


def factor_steps(a, fronts):
    sublanes = lax.broadcasted_iota(jnp.int32, (SLAB, TILE), 0)
    lanes = lax.broadcasted_iota(jnp.int32, (SLAB, TILE), 1)
    for start in range(0, TILE, SLAB):
        inside = (lanes >= start) & (lanes < start + SLAB)
        for q in range(fronts):
            rows = factor_slab(a[q, start : start + SLAB, :], start, inside, lanes)
            for low in range(start + SLAB, TILE, SLAB):
                chosen = sublanes + low
                terms = [jnp.take_along_axis(row, chosen, axis=1) * row for row in rows]
                block = a[q, low : low + SLAB, :]
                a[q, low : low + SLAB, :] = jnp.where(inside, 0.0, block) - sum_tree(terms)
            block = rows[0]
            for i in range(1, SLAB):
                block = jnp.where(sublanes == i, rows[i], block)
            a[q, start : start + SLAB, :] = block
        yield


def place():
    leaf, front = lax.axis_index("leaf"), lax.axis_index("front")
    return leaf, front, leaf & 1


def corner_kernel(*refs, order, first, last, count, devices):
    tiles = order // TILE
    if first == 0:
        near, other, work, out, heads, a = refs
    else:
        old_work, old_out, out, work, a = refs
    fronts = out.shape[0]
    if first == 0:
        front = place()[1]
        pieces = devices // 2

        def copy(owner, q, take):
            slot = slot_of(front ^ owner, devices)
            for held, low in ((near, 0), (other, pieces)):

                @pl.when((slot >= low) & (slot < low + pieces))
                def _():
                    take(held.at[q * pieces + slot - low])

        for q in range(fronts):
            for e in range(tiles):

                def take_tile(slab):
                    work[q, e * TILE : (e + 1) * TILE, :] = slab[:TILE, :]

                copy(e * GROUP_TILES // count, q, take_tile)

            def take_head(slab):
                heads[q] = slab[TILE:, :]

            copy(0, q, take_head)
    else:
        work[...] = old_work[...]
        out[...] = old_out[...]

    def step(k, carry):
        block = pl.ds(pl.multiple_of(k * TILE, TILE), TILE)
        for q in range(fronts):
            a[q] = work[q, block, block]
        for _ in factor_steps(a, fronts):
            pass
        kept = lax.broadcasted_iota(jnp.int32, (TILE, TILE), 0) >= lax.broadcasted_iota(jnp.int32, (TILE, TILE), 1)
        for q in range(fronts):
            out[q, block, block] = jnp.where(kept, a[q], 0.0)
        for fixed in range(first, last):

            @pl.when(k == fixed)
            def _():
                here = slice(fixed * TILE, (fixed + 1) * TILE)
                low, rest = slice(0, fixed * TILE), slice((fixed + 1) * TILE, order)
                for q in range(fronts):
                    corner = out[q, here, here]
                    if fixed:
                        chain = exact_dot(work[q, here, low], out[q, low, low], PLAIN)
                        out[q, here, low] = -exact_dot(corner, chain, PLAIN)
                    if fixed + 1 < tiles:
                        out[q, here, rest] = jnp.zeros((TILE, order - (fixed + 1) * TILE), jnp.float32)
                        below = exact_dot(work[q, rest, here], corner, LAST)
                        work[q, rest, here] = below
                        work[q, rest, rest] = work[q, rest, rest] - exact_dot(below, below, LAST)

        return carry

    lax.fori_loop(first, last, step, 0)


def parent_kernel(*refs, count, skip, width, devices):
    pieces = 2 * devices
    table, heads, weights, slab, inverse, fronts_here, far = refs[:7]
    edges = refs[7 : 7 + pieces]
    leaf_out, panel_out, update_out = refs[7 + pieces : 10 + pieces]
    (
        edge, here, beyond, leaf_panel, own_panel, panel_high, panel_low, column,
        two_left, two_right, total, a, edge_done, rows_done, out_done,
    ) = refs[10 + pieces :]
    leaf, front, half = place()
    sent = count - skip
    separator = width // GROUP_TILES
    rows = count * TILE
    first_row = pl.multiple_of((front * 2 + half) * rows, TILE)

    def at(tile):
        return pl.ds(pl.multiple_of(tile * TILE, TILE), TILE)

    def goal_of(i, tile):
        entry = 3 * (tile >> 2) + (tile & 3) - 1
        return jnp.where((tile & 3) == 0, -1, table[leaf ^ i, jnp.maximum(entry, 0)])

    copies = [
        pltpu.make_async_copy(edges[k], edge.at[k // devices, k % devices], edge_done.at[k]) for k in range(pieces)
    ]
    copies += [
        pltpu.make_async_copy(fronts_here.at[skip * TILE :, :], here, rows_done.at[0]),
        pltpu.make_async_copy(far, beyond, rows_done.at[1]),
    ]
    for copy in copies:
        copy.start()

    total[...] = jnp.zeros_like(total)
    column[...] = jnp.zeros_like(column)
    row_ids = lax.broadcasted_iota(jnp.int32, (TILE, TILE), 0)
    col_ids = lax.broadcasted_iota(jnp.int32, (TILE, TILE), 1)
    near = jnp.where(jnp.abs(row_ids - col_ids) == 1, 1.0, 0.0)
    before = jnp.where((row_ids == 0) & (col_ids == TILE - 1), 1.0, 0.0)
    behind = jnp.where((row_ids == TILE - 1) & (col_ids == 0), 1.0, 0.0)
    first_weights = jnp.where(half == 0, heads[0, 0:1, :TILE], heads[1, 0:1, :TILE])
    column[:TILE, :] = jnp.where(row_ids == col_ids, first_weights + 4.0, 0.0) - near
    column[TILE : 2 * TILE, :] = -before
    inside = first_row < SEP2
    weight = jnp.transpose(jnp.broadcast_to(weights[...], (TILE, rows)))
    for j in range(count):
        mine = (front * 2 + half) * count + j
        line = slice(j * TILE, (j + 1) * TILE)
        total[line, at(mine)] = jnp.where(
            row_ids == col_ids, weight[line, :] + jnp.where(inside, 4.0, 0.0), 0.0
        ) - jnp.where(inside, near, 0.0)

        @pl.when((mine > 0) & inside)
        def _():
            total[line, at(mine - 1)] = -before

        @pl.when((mine + 1) * TILE < SEP2)
        def _():
            total[line, at(mine + 1)] = -behind

    leaf_copy = pltpu.make_async_copy(leaf_panel, leaf_out, out_done.at[0])
    for i in range(2):
        turned = halves(inverse[i])
        cut = separator // 2
        top = tuple(part[:cut, :cut] for part in turned)
        bottom = tuple(part[cut:, :] for part in turned)

        def panel_of(block):
            full = halves(block)
            return jnp.concatenate(
                [split_dot(tuple(part[:, :cut] for part in full), top), split_dot(full, bottom)], axis=1
            )

        for s in range(devices):
            copies[i * devices + s].wait()
            panel = panel_of(edge[i, s, :, :separator])
            if s == 0 and i == 0:
                leaf_panel[skip * TILE :, :] = panel
                if skip:
                    leaf_panel[:TILE, :] = panel_of(slab[:TILE, :])
                leaf_copy.start()
            panel_high[i, s], panel_low[i, s] = halves(panel)

    tile_one = slice((1 - skip) * TILE, (2 - skip) * TILE)
    slot = slot_of(front, devices)
    for i in range(2):
        one = panel_high[i, slot, tile_one, :], panel_low[i, slot, tile_one, :]
        for s in range(devices):
            piece = edge[i, s, :, separator:] - split_dot((panel_high[i, s], panel_low[i, s]), one)
            owner = front ^ offset_of(s, devices)
            for t in range(sent):
                target = goal_of(i, owner * count + skip + t)

                @pl.when(target >= 0)
                def _():
                    column[at(target), :] += piece[t * TILE : (t + 1) * TILE, :]

    copies[-2].wait()
    copies[-1].wait()

    def contribution(i, s):
        product = split_dot((panel_high[i, 0], panel_low[i, 0]), (panel_high[i, s], panel_low[i, s]))
        for c in range(sent):
            tile = (front ^ offset_of(s, devices)) * count + skip + c
            goal = jnp.maximum(goal_of(i, tile), 0)
            for t in range(sent):
                target = goal_of(i, front * count + skip + t) - (front * 2 + half) * count
                target = jnp.where((target >= 0) & (target < count), target, count)
                line = slice(t * TILE, (t + 1) * TILE)
                if i == 0:
                    source = here[line, at(tile)]
                else:
                    source = beyond[line, at(jnp.maximum(tile - (tile >> 2) - 2, 0))]
                total[at(target), at(goal)] += source - product[line, c * TILE : (c + 1) * TILE]

    work = [functools.partial(contribution, i, s) for i in range(2) for s in range(devices)]
    a[0] = column[:TILE, :]
    steps = TILE // SLAB
    for k, _ in enumerate(factor_steps(a, 1)):
        while work and len(work) * steps >= (steps - k) * (2 * devices):
            work.pop(0)()
    for task in work:
        task()

    turned = halves(jnp.where(row_ids >= col_ids, a[0], 0.0))
    for start in range(0, M2, 1024):
        block = slice(start, start + 1024)
        panel = split_dot(halves(column[block, :]), turned)
        column[block, :] = panel
        high, low = halves(panel)
        two_left[block, :] = jnp.concatenate([high, high, low], axis=1)
        two_right[block, :] = jnp.concatenate([high, low, high], axis=1)
    mine = pl.ds(first_row, rows)
    own_panel[...] = column[mine, :]
    panel_copy = pltpu.make_async_copy(own_panel, panel_out, out_done.at[1])
    panel_copy.start()
    own = two_left[mine, :]
    sends = [leaf_copy, panel_copy]
    for start in range(TILE, M2, 512):
        stop = min(start + 512, M2)
        total[:rows, start:stop] = total[:rows, start:stop] - plain_dot(own, two_right[start:stop, :])
        send = pltpu.make_async_copy(
            total.at[:rows, start:stop],
            update_out.at[:, start - TILE : stop - TILE],
            out_done.at[len(sends)],
        )
        send.start()
        sends.append(send)
    for send in sends:
        send.wait()


def one_front(matrix, weights, table):
    rows, width = matrix.shape
    devices = lax.axis_size("front")
    count, tiles = rows // TILE, width // TILE
    skip = 1 if count % GROUP_TILES == 0 else 0
    separator = width // GROUP_TILES
    sent = (count - skip) * TILE
    distances = []
    while 2 ** (len(distances) + 1) < devices:
        distances.insert(0, 2 ** (len(distances) + 1))

    def columns(block, chosen):
        return jnp.concatenate([block[:, t * TILE : (t + 1) * TILE] for t in chosen], axis=1)

    def spread(pieces):
        for distance in distances:
            pieces = pieces + [from_front(piece, distance) for piece in pieces]
        return pieces

    corner = list(range(0, tiles, GROUP_TILES))
    rest = [t for t in range(tiles) if t % GROUP_TILES and t != 1]
    weight_rows = jnp.pad(weights[None], ((0, SLAB - 1), (0, separator - rows)))
    slab = jnp.concatenate([columns(matrix[:TILE], corner), weight_rows], axis=0)
    body = matrix[skip * TILE :]
    far_slab = from_sibling(slab)
    slabs = spread([slab])
    edge = columns(body, corner + [1])
    far_body = columns(body, rest)
    far_slabs = spread([far_slab])
    held = jnp.stack(slabs + far_slabs)
    other = from_front(held, 1)
    far_edge = from_sibling(after(edge, far_slab))
    far = from_sibling(after(far_body, far_slab))
    near_edges = spread([after(edge, *far_slabs)])

    vmem = pl.BlockSpec(memory_space=pltpu.VMEM)
    smem = pl.BlockSpec(memory_space=pltpu.SMEM)
    anywhere = pl.BlockSpec(memory_space=pl.ANY)
    f32, bf16 = jnp.float32, jnp.bfloat16
    state = jax.ShapeDtypeStruct((2, separator, separator), f32)
    scratch = pltpu.VMEM((2, TILE, TILE), f32)
    params = pltpu.CompilerParams(vmem_limit_bytes=VMEM_BYTES)
    cost = pl.CostEstimate(flops=12 * 10**9, bytes_accessed=2**23, transcendentals=0)
    middle = separator // TILE // 2
    half_kernel = functools.partial(corner_kernel, order=separator, count=count, devices=devices)
    state_one, state_two, heads = pl.pallas_call(
        functools.partial(half_kernel, first=0, last=middle),
        out_shape=(state, state, jax.ShapeDtypeStruct((2, SLAB, separator), f32)),
        in_specs=[vmem, vmem],
        out_specs=(vmem, vmem, vmem),
        scratch_shapes=[scratch],
        compiler_params=params,
        cost_estimate=cost,
        name="corner_first",
    )(held, other)

    other_edges = [from_front(after(piece, heads), 1) for piece in near_edges]
    far_edges = spread([after(far_edge, heads)])
    inverse = pl.pallas_call(
        functools.partial(half_kernel, first=middle, last=separator // TILE),
        out_shape=state,
        in_specs=[vmem, vmem],
        out_specs=vmem,
        scratch_shapes=[pltpu.VMEM((2, separator, separator), f32), scratch],
        compiler_params=params,
        cost_estimate=cost,
        name="corner_second",
    )(after(state_one, far_edge), state_two)
    other_far_edges = [from_front(piece, 1) for piece in far_edges]

    edges = near_edges + other_edges + far_edges + other_far_edges
    return pl.pallas_call(
        functools.partial(parent_kernel, count=count, skip=skip, width=width, devices=devices),
        out_shape=(
            jax.ShapeDtypeStruct((rows, separator), f32),
            jax.ShapeDtypeStruct((rows, TILE), f32),
            jax.ShapeDtypeStruct((rows, M2 - TILE), f32),
        ),
        in_specs=[smem, vmem, vmem, vmem, vmem] + [anywhere] * (2 + len(edges)),
        out_specs=(anywhere, anywhere, anywhere),
        scratch_shapes=[
            pltpu.VMEM((2, devices) + edge.shape, f32),
            pltpu.VMEM((sent, width), f32),
            pltpu.VMEM(far.shape, f32),
            pltpu.VMEM((rows, separator), f32),
            pltpu.VMEM((rows, TILE), f32),
            pltpu.VMEM((2, devices, sent, separator), bf16),
            pltpu.VMEM((2, devices, sent, separator), bf16),
            pltpu.VMEM((M2, TILE), f32),
            pltpu.VMEM((M2, 3 * TILE), bf16),
            pltpu.VMEM((M2, 3 * TILE), bf16),
            pltpu.VMEM((rows + TILE, M2), f32),
            pltpu.VMEM((1, TILE, TILE), f32),
            pltpu.SemaphoreType.DMA((len(edges),)),
            pltpu.SemaphoreType.DMA((2,)),
            pltpu.SemaphoreType.DMA((2 + M2 // 512,)),
        ],
        compiler_params=params,
        cost_estimate=pl.CostEstimate(flops=15 * 10**9, bytes_accessed=2**25, transcendentals=0),
        name="parent",
    )(table, heads, weights[None], slab, inverse, matrix, far, *edges)


def on_device(leaf_fronts, screen_weights, parent_tile_index):
    results = [
        one_front(leaf_fronts[0, g], screen_weights[0, g], parent_tile_index[:, g])
        for g in range(leaf_fronts.shape[1])
    ]
    return tuple(jnp.stack(parts)[None] for parts in zip(*results))


def solution(mesh):
    in_specs = (P("leaf", None, "front", None), P("leaf", None, "front"), P())
    out_specs = (
        P("leaf", None, "front", None),
        P("leaf", None, "front", None),
        P("leaf", None, "front", None),
    )
    return jax.shard_map(
        on_device, mesh=mesh, in_specs=in_specs, out_specs=out_specs, check_vma=False
    )
```

```python
import functools

import jax
import jax.numpy as jnp
from jax import lax
from jax.experimental import pallas as pl
from jax.experimental.pallas import tpu as pltpu
from jax.sharding import PartitionSpec as P

SEP2 = 1024
PANEL_WIDTH = 128
M2 = 4096
GROUP_TILES = 4
SLAB = 8
GROUP = 32
EXACT = lax.Precision.HIGHEST
VMEM_BYTES = 60 * 2**20

TILE = PANEL_WIDTH
LAST = ((1,), (1,))
PLAIN = ((1,), (0,))
FIRST = ((0,), (0,))


def from_front(value, distance):
    pairs = [(source, source ^ distance) for source in range(lax.axis_size("front"))]
    return lax.ppermute(value, "front", pairs)


def from_sibling(value):
    pairs = [(source, source ^ 1) for source in range(lax.axis_size("leaf"))]
    return lax.ppermute(value, "leaf", pairs)


def after(value, *events):
    return lax.optimization_barrier((value, *events))[0]


def slot_of(offset, count):
    slot, bit, weight = 0, 1, count // 2
    while weight:
        slot = slot + jnp.where((offset & bit) != 0, weight, 0)
        bit, weight = bit * 2, weight // 2
    return slot


def offset_of(slot, count):
    offset, bit, weight = 0, 1, count // 2
    while weight:
        offset += bit if slot & weight else 0
        bit, weight = bit * 2, weight // 2
    return offset


def exact_dot(left, right, contract):
    return lax.dot_general(
        left, right, (contract, ((), ())), precision=EXACT, preferred_element_type=jnp.float32
    )


def plain_dot(left, right):
    return lax.dot_general(left, right, (LAST, ((), ())), preferred_element_type=jnp.float32)


def halves(value):
    high = value.astype(jnp.bfloat16)
    return high, (value - high.astype(jnp.float32)).astype(jnp.bfloat16)


def split_dot(left, right):
    return plain_dot(left[0], right[0]) + (plain_dot(left[0], right[1]) + plain_dot(left[1], right[0]))


def lane(row, index):
    return jnp.broadcast_to(row[:, index : index + 1], row.shape)


def sum_tree(terms):
    while len(terms) > 1:
        terms = [sum(terms[i : i + 2]) for i in range(0, len(terms), 2)]
    return terms[0]


def factor_slab(rows, first, inside, lanes):
    entry = {(i, j): lane(rows[i], first + j) for i in range(SLAB) for j in range(i + 1)}
    rows = [jnp.where(inside, jnp.where(lanes == first + i, 1.0, 0.0), row) for i, row in enumerate(rows)]
    done = []
    for p in range(0, SLAB, 2):
        r = p + 1
        one, mixed, two = entry[p, p], entry[r, p], entry[r, r]
        inverse_one = pl.reciprocal(one, approx=True)
        inverse_two = pl.reciprocal(one * two - mixed * mixed, approx=True) * one
        factor = {i: entry[i, p] * inverse_one for i in range(r, SLAB)}
        rows[r] = rows[r] - factor[r] * rows[p]
        for i in range(p + 2, SLAB):
            entry[i, r] = entry[i, r] - factor[i] * mixed
        for i in range(p + 2, SLAB):
            second = entry[i, r] * inverse_two
            for k in range(p + 2, i + 1):
                entry[i, k] = (entry[i, k] - factor[i] * entry[k, p]) - second * entry[k, r]
            rows[i] = (rows[i] - factor[i] * rows[p]) - second * rows[r]
        done.append(rows[p] * lax.rsqrt(one))
        done.append(rows[r] * (inverse_two * lax.rsqrt(inverse_two)))
    return done


def factor_steps(a, fronts):
    lanes = lax.broadcasted_iota(jnp.int32, (fronts, TILE), 1)
    columns = lax.broadcasted_iota(jnp.int32, (TILE, TILE), 1)
    settled = (lax.broadcasted_iota(jnp.int32, (GROUP, TILE), 0) & -SLAB) + SLAB

    def at(i):
        return pl.ds(fronts * i, fronts)

    for start in range(0, TILE, GROUP):
        stop = start + GROUP
        rows = [a[at(i), :] for i in range(start, stop)]
        for s in range(0, GROUP, SLAB):
            first = start + s
            inside = (lanes >= first) & (lanes < first + SLAB)
            head = factor_slab(rows[s : s + SLAB], first, inside, lanes)
            for i in range(SLAB):
                a[at(first + i), :] = head[i]
            for i in range(s + SLAB, GROUP):
                terms = [lane(row, start + i) * row for row in head]
                rows[i] = jnp.where(inside, 0.0, rows[i]) - sum_tree(terms)
            if s + SLAB < GROUP:
                yield
        if stop < TILE:
            for q in range(fronts):
                upper = a[pl.ds(fronts * start + q, GROUP, stride=fronts), :]
                rest = pl.ds(fronts * stop + q, TILE - stop, stride=fronts)
                inverse = jnp.where((columns[:GROUP] >= start + settled) & (columns[:GROUP] < stop), 0.0, upper)
                product = exact_dot(upper, inverse, FIRST)[stop:]
                group = columns[stop:]
                kept = jnp.where((group >= start) & (group < stop), 0.0, a[rest, :])
                a[rest, :] = kept - product
        yield


def place():
    leaf, front = lax.axis_index("leaf"), lax.axis_index("front")
    return leaf, front, leaf & 1


def corner_kernel(*refs, order, first, last, count, devices):
    tiles = order // TILE
    pieces = 2 * devices
    if first == 0:
        slabs, (work, out, heads, a) = refs[:pieces], refs[pieces:]
    else:
        old_work, old_out, out, work, a = refs
    fronts = out.shape[0]
    if first == 0:
        front = place()[1]

        def copy(owner, q, take):
            slot = slot_of(front ^ owner, devices)
            for s in range(devices):

                @pl.when(slot == s)
                def _():
                    take(slabs[q * devices + s])

        for q in range(fronts):
            for e in range(tiles):

                def take_tile(slab):
                    work[q, e * TILE : (e + 1) * TILE, :] = slab[:TILE, :]

                copy(e * GROUP_TILES // count, q, take_tile)

            def take_head(slab):
                heads[q] = slab[TILE:, :]

            copy(0, q, take_head)
    else:
        work[...] = old_work[...]
        out[...] = old_out[...]

    def step(k, carry):
        block = pl.ds(pl.multiple_of(k * TILE, TILE), TILE)
        for q in range(fronts):
            a[pl.ds(q, TILE, stride=fronts), :] = work[q, block, block]
        for _ in factor_steps(a, fronts):
            pass
        kept = lax.broadcasted_iota(jnp.int32, (TILE, TILE), 0) >= lax.broadcasted_iota(jnp.int32, (TILE, TILE), 1)
        for q in range(fronts):
            out[q, block, block] = jnp.where(kept, a[pl.ds(q, TILE, stride=fronts), :], 0.0)
        for fixed in range(first, last):

            @pl.when(k == fixed)
            def _():
                here = slice(fixed * TILE, (fixed + 1) * TILE)
                low, rest = slice(0, fixed * TILE), slice((fixed + 1) * TILE, order)
                for q in range(fronts):
                    corner = out[q, here, here]
                    if fixed:
                        chain = exact_dot(work[q, here, low], out[q, low, low], PLAIN)
                        out[q, here, low] = -exact_dot(corner, chain, PLAIN)
                    if fixed + 1 < tiles:
                        out[q, here, rest] = jnp.zeros((TILE, order - (fixed + 1) * TILE), jnp.float32)
                        below = exact_dot(work[q, rest, here], corner, LAST)
                        work[q, rest, here] = below
                        work[q, rest, rest] = work[q, rest, rest] - exact_dot(below, below, LAST)

        return carry

    lax.fori_loop(first, last, step, 0)


def parent_kernel(*refs, count, skip, width, devices):
    pieces = 2 * devices
    table, heads, weights, slab, inverse, fronts_here, far = refs[:7]
    edges = refs[7 : 7 + pieces]
    leaf_out, panel_out, update_out = refs[7 + pieces : 10 + pieces]
    (
        edge, here, beyond, leaf_panel, own_panel, panel_high, panel_low, column,
        two_left, two_right, total, a, edge_done, rows_done, out_done,
    ) = refs[10 + pieces :]
    leaf, front, half = place()
    sent = count - skip
    separator = width // GROUP_TILES
    rows = count * TILE
    first_row = pl.multiple_of((front * 2 + half) * rows, TILE)

    def at(tile):
        return pl.ds(pl.multiple_of(tile * TILE, TILE), TILE)

    def goal_of(i, tile):
        entry = 3 * (tile >> 2) + (tile & 3) - 1
        return jnp.where((tile & 3) == 0, -1, table[leaf ^ i, jnp.maximum(entry, 0)])

    copies = [
        pltpu.make_async_copy(edges[k], edge.at[k // devices, k % devices], edge_done.at[k]) for k in range(pieces)
    ]
    copies += [
        pltpu.make_async_copy(fronts_here.at[skip * TILE :, :], here, rows_done.at[0]),
        pltpu.make_async_copy(far, beyond, rows_done.at[1]),
    ]
    for copy in copies:
        copy.start()

    total[...] = jnp.zeros_like(total)
    column[...] = jnp.zeros_like(column)
    row_ids = lax.broadcasted_iota(jnp.int32, (TILE, TILE), 0)
    col_ids = lax.broadcasted_iota(jnp.int32, (TILE, TILE), 1)
    near = jnp.where(jnp.abs(row_ids - col_ids) == 1, 1.0, 0.0)
    before = jnp.where((row_ids == 0) & (col_ids == TILE - 1), 1.0, 0.0)
    behind = jnp.where((row_ids == TILE - 1) & (col_ids == 0), 1.0, 0.0)
    first_weights = jnp.where(half == 0, heads[0, 0:1, :TILE], heads[1, 0:1, :TILE])
    column[:TILE, :] = jnp.where(row_ids == col_ids, first_weights + 4.0, 0.0) - near
    column[TILE : 2 * TILE, :] = -before
    inside = first_row < SEP2
    weight = jnp.transpose(jnp.broadcast_to(weights[...], (TILE, rows)))
    for j in range(count):
        mine = (front * 2 + half) * count + j
        line = slice(j * TILE, (j + 1) * TILE)
        total[line, at(mine)] = jnp.where(
            row_ids == col_ids, weight[line, :] + jnp.where(inside, 4.0, 0.0), 0.0
        ) - jnp.where(inside, near, 0.0)

        @pl.when((mine > 0) & inside)
        def _():
            total[line, at(mine - 1)] = -before

        @pl.when((mine + 1) * TILE < SEP2)
        def _():
            total[line, at(mine + 1)] = -behind

    leaf_copy = pltpu.make_async_copy(leaf_panel, leaf_out, out_done.at[0])
    for i in range(2):
        turned = halves(inverse[i])
        cut = separator // 2
        top = tuple(part[:cut, :cut] for part in turned)
        bottom = tuple(part[cut:, :] for part in turned)

        def panel_of(block):
            full = halves(block)
            return jnp.concatenate(
                [split_dot(tuple(part[:, :cut] for part in full), top), split_dot(full, bottom)], axis=1
            )

        for s in range(devices):
            copies[i * devices + s].wait()
            panel = panel_of(edge[i, s, :, :separator])
            if s == 0 and i == 0:
                leaf_panel[skip * TILE :, :] = panel
                if skip:
                    leaf_panel[:TILE, :] = panel_of(slab[:TILE, :])
                leaf_copy.start()
            panel_high[i, s], panel_low[i, s] = halves(panel)

    tile_one = slice((1 - skip) * TILE, (2 - skip) * TILE)
    slot = slot_of(front, devices)
    for i in range(2):
        one = panel_high[i, slot, tile_one, :], panel_low[i, slot, tile_one, :]
        for s in range(devices):
            piece = edge[i, s, :, separator:] - split_dot((panel_high[i, s], panel_low[i, s]), one)
            owner = front ^ offset_of(s, devices)
            for t in range(sent):
                target = goal_of(i, owner * count + skip + t)

                @pl.when(target >= 0)
                def _():
                    column[at(target), :] += piece[t * TILE : (t + 1) * TILE, :]

    copies[-2].wait()
    copies[-1].wait()

    def contribution(i, s):
        product = split_dot((panel_high[i, 0], panel_low[i, 0]), (panel_high[i, s], panel_low[i, s]))
        for c in range(sent):
            tile = (front ^ offset_of(s, devices)) * count + skip + c
            goal = jnp.maximum(goal_of(i, tile), 0)
            for t in range(sent):
                target = goal_of(i, front * count + skip + t) - (front * 2 + half) * count
                target = jnp.where((target >= 0) & (target < count), target, count)
                line = slice(t * TILE, (t + 1) * TILE)
                if i == 0:
                    source = here[line, at(tile)]
                else:
                    source = beyond[line, at(jnp.maximum(tile - (tile >> 2) - 2, 0))]
                total[at(target), at(goal)] += source - product[line, c * TILE : (c + 1) * TILE]

    work = [functools.partial(contribution, i, s) for i in range(2) for s in range(devices)]
    a[...] = column[:TILE, :]
    steps = TILE // SLAB
    for k, _ in enumerate(factor_steps(a, 1)):
        while work and len(work) * steps >= (steps - k) * (2 * devices):
            work.pop(0)()
    for task in work:
        task()

    turned = halves(jnp.where(row_ids >= col_ids, a[...], 0.0))
    for start in range(0, M2, 1024):
        block = slice(start, start + 1024)
        panel = split_dot(halves(column[block, :]), turned)
        column[block, :] = panel
        high, low = halves(panel)
        two_left[block, :] = jnp.concatenate([high, high, low], axis=1)
        two_right[block, :] = jnp.concatenate([high, low, high], axis=1)
    mine = pl.ds(first_row, rows)
    own_panel[...] = column[mine, :]
    panel_copy = pltpu.make_async_copy(own_panel, panel_out, out_done.at[1])
    panel_copy.start()
    own = two_left[mine, :]
    sends = [leaf_copy, panel_copy]
    for start in range(TILE, M2, 512):
        stop = min(start + 512, M2)
        total[:rows, start:stop] = total[:rows, start:stop] - plain_dot(own, two_right[start:stop, :])
        send = pltpu.make_async_copy(
            total.at[:rows, start:stop],
            update_out.at[:, start - TILE : stop - TILE],
            out_done.at[len(sends)],
        )
        send.start()
        sends.append(send)
    for send in sends:
        send.wait()


def slab_kernel(matrix, weights, slab, done, *, chosen):
    copies = [
        pltpu.make_async_copy(
            matrix.at[:TILE, t * TILE : (t + 1) * TILE], slab.at[:TILE, k * TILE : (k + 1) * TILE], done.at[k]
        )
        for k, t in enumerate(chosen)
    ]
    for copy in copies:
        copy.start()
    slab[TILE:, :] = jnp.zeros_like(slab[TILE:, :])
    slab[TILE : TILE + 1, : weights.shape[1]] = weights[...]
    for copy in copies:
        copy.wait()


def body_kernel(matrix, edge, far, done, *, skip, chosen, rest):
    copies = []
    for target, tiles in ((edge, chosen), (far, rest)):
        filled = 0
        while filled < len(tiles):
            stop = filled + 1
            while stop < len(tiles) and tiles[stop] == tiles[stop - 1] + 1:
                stop += 1
            copies.append(
                pltpu.make_async_copy(
                    matrix.at[skip * TILE :, tiles[filled] * TILE : (tiles[stop - 1] + 1) * TILE],
                    target.at[:, filled * TILE : stop * TILE],
                    done.at[len(copies)],
                )
            )
            filled = stop
    for copy in copies:
        copy.start()
    for copy in copies:
        copy.wait()


def one_front(matrix, weights, table):
    rows, width = matrix.shape
    devices = lax.axis_size("front")
    count, tiles = rows // TILE, width // TILE
    skip = 1 if count % GROUP_TILES == 0 else 0
    separator = width // GROUP_TILES
    sent = (count - skip) * TILE
    distances = []
    while 2 ** (len(distances) + 1) < devices:
        distances.insert(0, 2 ** (len(distances) + 1))

    def spread(pieces):
        for distance in distances:
            pieces = pieces + [from_front(piece, distance) for piece in pieces]
        return pieces

    vmem = pl.BlockSpec(memory_space=pltpu.VMEM)
    smem = pl.BlockSpec(memory_space=pltpu.SMEM)
    anywhere = pl.BlockSpec(memory_space=pl.ANY)
    f32, bf16 = jnp.float32, jnp.bfloat16
    params = pltpu.CompilerParams(vmem_limit_bytes=VMEM_BYTES)
    small = pltpu.CompilerParams(vmem_limit_bytes=VMEM_BYTES // 3)

    corner = list(range(0, tiles, GROUP_TILES))
    rest = [t for t in range(tiles) if t % GROUP_TILES and t != 1]
    slab = pl.pallas_call(
        functools.partial(slab_kernel, chosen=corner),
        out_shape=jax.ShapeDtypeStruct((TILE + SLAB, separator), f32),
        in_specs=[anywhere, vmem],
        out_specs=vmem,
        scratch_shapes=[pltpu.SemaphoreType.DMA((len(corner),))],
        compiler_params=params,
        cost_estimate=pl.CostEstimate(flops=0, bytes_accessed=2**19, transcendentals=0),
        name="slab",
    )(matrix, weights[None])
    far_slab = from_sibling(slab)
    slabs = spread([slab])
    edge, far_body = pl.pallas_call(
        functools.partial(body_kernel, skip=skip, chosen=corner + [1], rest=rest),
        out_shape=(
            jax.ShapeDtypeStruct((sent, (len(corner) + 1) * TILE), f32),
            jax.ShapeDtypeStruct((sent, len(rest) * TILE), f32),
        ),
        in_specs=[anywhere],
        out_specs=(anywhere, anywhere),
        scratch_shapes=[pltpu.SemaphoreType.DMA((2 * tiles,))],
        compiler_params=params,
        cost_estimate=pl.CostEstimate(flops=0, bytes_accessed=2**23, transcendentals=0),
        name="body",
    )(after(matrix, slab))
    far_slabs = spread([after(far_slab, edge)])
    other_slabs = [from_front(piece, 1) for piece in slabs]
    other_far_slabs = [from_front(piece, 1) for piece in far_slabs]
    far_edge = from_sibling(after(edge, far_slab))
    far = from_sibling(after(far_body, far_slab))
    near_edges = spread([after(edge, *far_slabs)])

    state = jax.ShapeDtypeStruct((2, separator, separator), f32)
    scratch = pltpu.VMEM((2 * TILE, TILE), f32)
    cost = pl.CostEstimate(flops=12 * 10**9, bytes_accessed=2**23, transcendentals=0)
    middle = separator // TILE // 2
    half_kernel = functools.partial(corner_kernel, order=separator, count=count, devices=devices)
    state_one, state_two, heads = pl.pallas_call(
        functools.partial(half_kernel, first=0, last=middle),
        out_shape=(state, state, jax.ShapeDtypeStruct((2, SLAB, separator), f32)),
        in_specs=[vmem] * (2 * devices),
        out_specs=(vmem, vmem, vmem),
        scratch_shapes=[scratch],
        compiler_params=small,
        cost_estimate=cost,
        name="corner_first",
    )(*slabs, *other_slabs, *far_slabs, *other_far_slabs)

    other_edges = [from_front(after(piece, heads), 1) for piece in near_edges]
    far_edges = spread([after(far_edge, heads)])
    inverse = pl.pallas_call(
        functools.partial(half_kernel, first=middle, last=separator // TILE),
        out_shape=state,
        in_specs=[vmem, vmem],
        out_specs=vmem,
        scratch_shapes=[pltpu.VMEM((2, separator, separator), f32), scratch],
        compiler_params=small,
        cost_estimate=cost,
        name="corner_second",
    )(after(state_one, far_edge), state_two)
    other_far_edges = [from_front(after(piece, inverse), 1) for piece in far_edges]

    edges = near_edges + other_edges + far_edges + other_far_edges
    return pl.pallas_call(
        functools.partial(parent_kernel, count=count, skip=skip, width=width, devices=devices),
        out_shape=(
            jax.ShapeDtypeStruct((rows, separator), f32),
            jax.ShapeDtypeStruct((rows, TILE), f32),
            jax.ShapeDtypeStruct((rows, M2 - TILE), f32),
        ),
        in_specs=[smem, vmem, vmem, vmem, vmem] + [anywhere] * (2 + len(edges)),
        out_specs=(anywhere, anywhere, anywhere),
        scratch_shapes=[
            pltpu.VMEM((2, devices) + edge.shape, f32),
            pltpu.VMEM((sent, width), f32),
            pltpu.VMEM(far.shape, f32),
            pltpu.VMEM((rows, separator), f32),
            pltpu.VMEM((rows, TILE), f32),
            pltpu.VMEM((2, devices, sent, separator), bf16),
            pltpu.VMEM((2, devices, sent, separator), bf16),
            pltpu.VMEM((M2, TILE), f32),
            pltpu.VMEM((M2, 3 * TILE), bf16),
            pltpu.VMEM((M2, 3 * TILE), bf16),
            pltpu.VMEM((rows + TILE, M2), f32),
            pltpu.VMEM((TILE, TILE), f32),
            pltpu.SemaphoreType.DMA((len(edges),)),
            pltpu.SemaphoreType.DMA((2,)),
            pltpu.SemaphoreType.DMA((2 + M2 // 512,)),
        ],
        compiler_params=pltpu.CompilerParams(vmem_limit_bytes=VMEM_BYTES * 3 // 4),
        cost_estimate=pl.CostEstimate(flops=15 * 10**9, bytes_accessed=2**25, transcendentals=0),
        name="parent",
    )(table, heads, weights[None], slab, inverse, matrix, far, *edges)


def on_device(leaf_fronts, screen_weights, parent_tile_index):
    results = [
        one_front(leaf_fronts[0, g], screen_weights[0, g], parent_tile_index[:, g])
        for g in range(leaf_fronts.shape[1])
    ]
    return tuple(jnp.stack(parts)[None] for parts in zip(*results))


def solution(mesh):
    in_specs = (P("leaf", None, "front", None), P("leaf", None, "front"), P())
    out_specs = (
        P("leaf", None, "front", None),
        P("leaf", None, "front", None),
        P("leaf", None, "front", None),
    )
    return jax.shard_map(
        on_device, mesh=mesh, in_specs=in_specs, out_specs=out_specs, check_vma=False
    )
```

```python
import functools

import jax
import jax.numpy as jnp
from jax import lax
from jax.experimental import pallas as pl
from jax.experimental.pallas import tpu as pltpu
from jax.sharding import PartitionSpec as P

SEP2 = 1024
PANEL_WIDTH = 128
M2 = 4096
GROUP_TILES = 4
SLAB = 8
GROUP = 32
EXACT = lax.Precision.HIGHEST
VMEM_BYTES = 60 * 2**20

TILE = PANEL_WIDTH
LAST = ((1,), (1,))
PLAIN = ((1,), (0,))
FIRST = ((0,), (0,))


def from_front(value, distance):
    pairs = [(source, source ^ distance) for source in range(lax.axis_size("front"))]
    return lax.ppermute(value, "front", pairs)


def from_sibling(value):
    pairs = [(source, source ^ 1) for source in range(lax.axis_size("leaf"))]
    return lax.ppermute(value, "leaf", pairs)


def after(value, *events):
    return lax.optimization_barrier((value, *events))[0]


def slot_of(offset, count):
    slot, bit, weight = 0, 1, count // 2
    while weight:
        slot = slot + jnp.where((offset & bit) != 0, weight, 0)
        bit, weight = bit * 2, weight // 2
    return slot


def offset_of(slot, count):
    offset, bit, weight = 0, 1, count // 2
    while weight:
        offset += bit if slot & weight else 0
        bit, weight = bit * 2, weight // 2
    return offset


def exact_dot(left, right, contract):
    return lax.dot_general(
        left, right, (contract, ((), ())), precision=EXACT, preferred_element_type=jnp.float32
    )


def plain_dot(left, right):
    return lax.dot_general(left, right, (LAST, ((), ())), preferred_element_type=jnp.float32)


def halves(value):
    high = value.astype(jnp.bfloat16)
    return high, (value - high.astype(jnp.float32)).astype(jnp.bfloat16)


def split_dot(left, right):
    return plain_dot(left[0], right[0]) + (plain_dot(left[0], right[1]) + plain_dot(left[1], right[0]))


def lane(row, index):
    return jnp.broadcast_to(row[:, index : index + 1], row.shape)


def sum_tree(terms):
    while len(terms) > 1:
        terms = [sum(terms[i : i + 2]) for i in range(0, len(terms), 2)]
    return terms[0]


def factor_slab(rows, first, inside, lanes):
    entry = {(i, j): lane(rows[i], first + j) for i in range(SLAB) for j in range(i + 1)}
    rows = [jnp.where(inside, jnp.where(lanes == first + i, 1.0, 0.0), row) for i, row in enumerate(rows)]
    done = []
    for p in range(0, SLAB, 2):
        r = p + 1
        one, mixed, two = entry[p, p], entry[r, p], entry[r, r]
        inverse_one = pl.reciprocal(one, approx=True)
        inverse_two = pl.reciprocal(one * two - mixed * mixed, approx=True) * one
        factor = {i: entry[i, p] * inverse_one for i in range(r, SLAB)}
        rows[r] = rows[r] - factor[r] * rows[p]
        for i in range(p + 2, SLAB):
            entry[i, r] = entry[i, r] - factor[i] * mixed
        for i in range(p + 2, SLAB):
            second = entry[i, r] * inverse_two
            for k in range(p + 2, i + 1):
                entry[i, k] = (entry[i, k] - factor[i] * entry[k, p]) - second * entry[k, r]
            rows[i] = (rows[i] - factor[i] * rows[p]) - second * rows[r]
        done.append(rows[p] * lax.rsqrt(one))
        done.append(rows[r] * (inverse_two * lax.rsqrt(inverse_two)))
    return done


def factor_steps(a, fronts):
    lanes = lax.broadcasted_iota(jnp.int32, (fronts, TILE), 1)
    columns = lax.broadcasted_iota(jnp.int32, (TILE, TILE), 1)
    settled = (lax.broadcasted_iota(jnp.int32, (GROUP, TILE), 0) & -SLAB) + SLAB

    def at(i):
        return pl.ds(fronts * i, fronts)

    for start in range(0, TILE, GROUP):
        stop = start + GROUP
        rows = [a[at(i), :] for i in range(start, stop)]
        for s in range(0, GROUP, SLAB):
            first = start + s
            inside = (lanes >= first) & (lanes < first + SLAB)
            head = factor_slab(rows[s : s + SLAB], first, inside, lanes)
            for i in range(SLAB):
                a[at(first + i), :] = head[i]
            for i in range(s + SLAB, GROUP):
                terms = [lane(row, start + i) * row for row in head]
                rows[i] = jnp.where(inside, 0.0, rows[i]) - sum_tree(terms)
            if s + SLAB < GROUP:
                yield
        if stop < TILE:
            for q in range(fronts):
                upper = a[pl.ds(fronts * start + q, GROUP, stride=fronts), :]
                rest = pl.ds(fronts * stop + q, TILE - stop, stride=fronts)
                inverse = jnp.where((columns[:GROUP] >= start + settled) & (columns[:GROUP] < stop), 0.0, upper)
                product = exact_dot(upper, inverse, FIRST)[stop:]
                group = columns[stop:]
                kept = jnp.where((group >= start) & (group < stop), 0.0, a[rest, :])
                a[rest, :] = kept - product
        yield


def place():
    leaf, front = lax.axis_index("leaf"), lax.axis_index("front")
    return leaf, front, leaf & 1


def corner_kernel(*refs, order, first, last, count, devices):
    tiles = order // TILE
    pieces = 2 * devices
    if first == 0:
        slabs, (work, out, heads, a) = refs[:pieces], refs[pieces:]
    else:
        old_work, old_out, out, work, a = refs
    fronts = out.shape[0]
    if first == 0:
        front = place()[1]

        def copy(owner, q, take):
            slot = slot_of(front ^ owner, devices)
            for s in range(devices):

                @pl.when(slot == s)
                def _():
                    take(slabs[q * devices + s])

        for q in range(fronts):
            for e in range(tiles):

                def take_tile(slab):
                    work[q, e * TILE : (e + 1) * TILE, :] = slab[:TILE, :]

                copy(e * GROUP_TILES // count, q, take_tile)

            def take_head(slab):
                heads[q] = slab[TILE:, :]

            copy(0, q, take_head)
    else:
        work[...] = old_work[...]
        out[...] = old_out[...]

    def step(k, carry):
        block = pl.ds(pl.multiple_of(k * TILE, TILE), TILE)
        for q in range(fronts):
            a[pl.ds(q, TILE, stride=fronts), :] = work[q, block, block]
        for _ in factor_steps(a, fronts):
            pass
        kept = lax.broadcasted_iota(jnp.int32, (TILE, TILE), 0) >= lax.broadcasted_iota(jnp.int32, (TILE, TILE), 1)
        for q in range(fronts):
            out[q, block, block] = jnp.where(kept, a[pl.ds(q, TILE, stride=fronts), :], 0.0)
        for fixed in range(first, last):

            @pl.when(k == fixed)
            def _():
                here = slice(fixed * TILE, (fixed + 1) * TILE)
                low, rest = slice(0, fixed * TILE), slice((fixed + 1) * TILE, order)
                for q in range(fronts):
                    corner = out[q, here, here]
                    if fixed:
                        chain = exact_dot(work[q, here, low], out[q, low, low], PLAIN)
                        out[q, here, low] = -exact_dot(corner, chain, PLAIN)
                    if fixed + 1 < tiles:
                        out[q, here, rest] = jnp.zeros((TILE, order - (fixed + 1) * TILE), jnp.float32)
                        below = exact_dot(work[q, rest, here], corner, LAST)
                        work[q, rest, here] = below
                        work[q, rest, rest] = work[q, rest, rest] - exact_dot(below, below, LAST)

        return carry

    lax.fori_loop(first, last, step, 0)


def at(tile):
    return pl.ds(pl.multiple_of(tile * TILE, TILE), TILE)


def goal_of(table, i, tile):
    entry = 3 * (tile >> 2) + (tile & 3) - 1
    return jnp.where((tile & 3) == 0, -1, table[place()[0] ^ i, jnp.maximum(entry, 0)])


def panel_of(inverse):
    turned = halves(inverse)
    cut = inverse.shape[0] // 2
    top = tuple(part[:cut, :cut] for part in turned)
    bottom = tuple(part[cut:, :] for part in turned)

    def product(block):
        full = halves(block)
        left = split_dot(tuple(part[:, :cut] for part in full), top)
        return jnp.concatenate([left, split_dot(full, bottom)], axis=1)

    return product


def add_columns(table, i, edge, panel_high, panel_low, column, *, count, skip, devices):
    front = place()[1]
    separator = panel_high.shape[2]
    first = slice((1 - skip) * TILE, (2 - skip) * TILE)
    slot = slot_of(front, devices)
    one = panel_high[slot, first, :], panel_low[slot, first, :]
    for s in range(devices):
        piece = edge[s, :, separator:] - split_dot((panel_high[s], panel_low[s]), one)
        owner = front ^ offset_of(s, devices)
        for t in range(count - skip):
            target = goal_of(table, i, owner * count + skip + t)

            @pl.when(target >= 0)
            def _():
                column[at(target), :] += piece[t * TILE : (t + 1) * TILE, :]


def own_kernel(*refs, count, skip, width, devices):
    table, heads, weights, slab, inverse, fronts_here = refs[:6]
    edges = refs[6 : 6 + devices]
    leaf_panel, column, total_out = refs[6 + devices : 9 + devices]
    edge, here, panel_high, panel_low, total, edge_done, done = refs[9 + devices :]
    leaf, front, half = place()
    sent = count - skip
    separator = width // GROUP_TILES
    rows = count * TILE
    first_row = (front * 2 + half) * rows

    copies = [pltpu.make_async_copy(edges[s], edge.at[s], edge_done.at[s]) for s in range(devices)]
    copies.append(pltpu.make_async_copy(fronts_here.at[skip * TILE :, :], here, done.at[0]))
    for copy in copies:
        copy.start()

    total[...] = jnp.zeros_like(total)
    column[...] = jnp.zeros_like(column)
    row_ids = lax.broadcasted_iota(jnp.int32, (TILE, TILE), 0)
    col_ids = lax.broadcasted_iota(jnp.int32, (TILE, TILE), 1)
    near = jnp.where(jnp.abs(row_ids - col_ids) == 1, 1.0, 0.0)
    before = jnp.where((row_ids == 0) & (col_ids == TILE - 1), 1.0, 0.0)
    behind = jnp.where((row_ids == TILE - 1) & (col_ids == 0), 1.0, 0.0)
    first_weights = jnp.where(half == 0, heads[0, 0:1, :TILE], heads[1, 0:1, :TILE])
    column[:TILE, :] = jnp.where(row_ids == col_ids, first_weights + 4.0, 0.0) - near
    column[TILE : 2 * TILE, :] = -before
    inside = first_row < SEP2
    weight = jnp.transpose(jnp.broadcast_to(weights[...], (TILE, rows)))
    for j in range(count):
        mine = (front * 2 + half) * count + j
        line = slice(j * TILE, (j + 1) * TILE)
        total[line, at(mine)] = jnp.where(
            row_ids == col_ids, weight[line, :] + jnp.where(inside, 4.0, 0.0), 0.0
        ) - jnp.where(inside, near, 0.0)

        @pl.when((mine > 0) & inside)
        def _():
            total[line, at(mine - 1)] = -before

        @pl.when((mine + 1) * TILE < SEP2)
        def _():
            total[line, at(mine + 1)] = -behind

    panel_from = panel_of(inverse[0])
    if skip:
        leaf_panel[:TILE, :] = panel_from(slab[:TILE, :])
    for s in range(devices):
        copies[s].wait()
        panel = panel_from(edge[s, :, :separator])
        if s == 0:
            leaf_panel[skip * TILE :, :] = panel
        panel_high[s], panel_low[s] = halves(panel)
    add_columns(table, 0, edge, panel_high, panel_low, column, count=count, skip=skip, devices=devices)

    copies[-1].wait()
    for s in range(devices):
        product = split_dot((panel_high[0], panel_low[0]), (panel_high[s], panel_low[s]))
        for c in range(sent):
            tile = (front ^ offset_of(s, devices)) * count + skip + c
            goal = jnp.maximum(goal_of(table, 0, tile), 0)
            for t in range(sent):
                target = goal_of(table, 0, front * count + skip + t) - (front * 2 + half) * count
                target = jnp.where((target >= 0) & (target < count), target, count)
                line = slice(t * TILE, (t + 1) * TILE)
                total[at(target), at(goal)] += here[line, at(tile)] - product[line, c * TILE : (c + 1) * TILE]
    send = pltpu.make_async_copy(total.at[:rows, TILE:], total_out, done.at[1])
    send.start()
    send.wait()


def parent_kernel(*refs, count, skip, width, devices):
    table, inverse, column_in, total_in = refs[:4]
    edges = refs[4 : 4 + devices]
    panel_out, update_out, far_high, far_low = refs[4 + devices : 8 + devices]
    edge, panel_high, panel_low, column, two_left, two_right, total, a, edge_done, done = refs[8 + devices :]
    leaf, front, half = place()
    separator = width // GROUP_TILES
    rows = count * TILE
    first_row = pl.multiple_of((front * 2 + half) * rows, TILE)

    copies = [pltpu.make_async_copy(edges[s], edge.at[s], edge_done.at[s]) for s in range(devices)]
    copies.append(pltpu.make_async_copy(column_in, column, done.at[0]))
    copies.append(pltpu.make_async_copy(total_in, total, done.at[1]))
    for copy in copies:
        copy.start()

    panel_from = panel_of(inverse[1])
    for s in range(devices):
        copies[s].wait()
        panel_high[s], panel_low[s] = halves(panel_from(edge[s, :, :separator]))
    sends = [
        pltpu.make_async_copy(panel_high, far_high, done.at[2]),
        pltpu.make_async_copy(panel_low, far_low, done.at[3]),
    ]
    for send in sends:
        send.start()
    copies[devices].wait()
    add_columns(table, 1, edge, panel_high, panel_low, column, count=count, skip=skip, devices=devices)

    a[...] = column[:TILE, :]
    for _ in factor_steps(a, 1):
        pass
    row_ids = lax.broadcasted_iota(jnp.int32, (TILE, TILE), 0)
    col_ids = lax.broadcasted_iota(jnp.int32, (TILE, TILE), 1)
    turned = halves(jnp.where(row_ids >= col_ids, a[...], 0.0))
    for start in range(0, M2, 1024):
        block = slice(start, start + 1024)
        panel = split_dot(halves(column[block, :]), turned)
        column[block, :] = panel
        high, low = halves(panel)
        two_left[block, :] = jnp.concatenate([high, high, low], axis=1)
        two_right[block, :] = jnp.concatenate([high, low, high], axis=1)
    mine = pl.ds(first_row, rows)
    panel_out[...] = column[mine, :]
    own = two_left[mine, :]
    copies[-1].wait()
    for start in range(TILE, M2, 512):
        stop = min(start + 512, M2)
        here = slice(start - TILE, stop - TILE)
        total[:, here] = total[:, here] - plain_dot(own, two_right[start:stop, :])
        send = pltpu.make_async_copy(total.at[:, here], update_out.at[:, here], done.at[2 + len(sends)])
        send.start()
        sends.append(send)
    for send in sends:
        send.wait()


def far_kernel(table, high, low, far, update, out, panel_high, panel_low, beyond, tiles, loaded, got, put, *, count, skip, devices):
    leaf, front, half = place()
    sent = count - skip
    loads = [
        pltpu.make_async_copy(high, panel_high, loaded.at[0]),
        pltpu.make_async_copy(low, panel_low, loaded.at[1]),
        pltpu.make_async_copy(far, beyond, loaded.at[2]),
    ]
    for load in loads:
        load.start()

    def each(s, t, c):
        tile = (front ^ offset_of(s, devices)) * count + skip + c
        goal = goal_of(table, 1, tile)
        target = goal_of(table, 1, front * count + skip + t) - (front * 2 + half) * count
        valid = (goal > 0) & (target >= 0) & (target < count)
        index = (s * sent + t) * sent + c
        lies = out.at[at(jnp.clip(target, 0, count - 1)), at(jnp.maximum(goal - 1, 0))]
        return tile, index, valid, lies

    def fetch(index, lies):
        return pltpu.make_async_copy(lies, tiles.at[index], got.at[index])

    def store(index, lies):
        return pltpu.make_async_copy(tiles.at[index], lies, put.at[index])

    for s in range(devices):
        for t in range(sent):
            for c in range(sent):
                _, index, valid, lies = each(s, t, c)

                @pl.when(valid)
                def _():
                    fetch(index, lies).start()

    for load in loads:
        load.wait()
    for s in range(devices):
        product = split_dot((panel_high[0], panel_low[0]), (panel_high[s], panel_low[s]))
        for t in range(sent):
            line = slice(t * TILE, (t + 1) * TILE)
            for c in range(sent):
                tile, index, valid, lies = each(s, t, c)

                @pl.when(valid)
                def _():
                    source = beyond[line, at(jnp.maximum(tile - (tile >> 2) - 2, 0))]
                    fetch(index, lies).wait()
                    tiles[index] += source - product[line, c * TILE : (c + 1) * TILE]
                    store(index, lies).start()

    for s in range(devices):
        for t in range(sent):
            for c in range(sent):
                _, index, valid, lies = each(s, t, c)

                @pl.when(valid)
                def _():
                    store(index, lies).wait()


def slab_kernel(matrix, weights, slab, done, *, chosen):
    copies = [
        pltpu.make_async_copy(
            matrix.at[:TILE, t * TILE : (t + 1) * TILE], slab.at[:TILE, k * TILE : (k + 1) * TILE], done.at[k]
        )
        for k, t in enumerate(chosen)
    ]
    for copy in copies:
        copy.start()
    slab[TILE:, :] = jnp.zeros_like(slab[TILE:, :])
    slab[TILE : TILE + 1, : weights.shape[1]] = weights[...]
    for copy in copies:
        copy.wait()


def body_kernel(matrix, edge, far, done, *, skip, chosen, rest):
    copies = []
    for target, tiles in ((edge, chosen), (far, rest)):
        filled = 0
        while filled < len(tiles):
            stop = filled + 1
            while stop < len(tiles) and tiles[stop] == tiles[stop - 1] + 1:
                stop += 1
            copies.append(
                pltpu.make_async_copy(
                    matrix.at[skip * TILE :, tiles[filled] * TILE : (tiles[stop - 1] + 1) * TILE],
                    target.at[:, filled * TILE : stop * TILE],
                    done.at[len(copies)],
                )
            )
            filled = stop
    for copy in copies:
        copy.start()
    for copy in copies:
        copy.wait()


def one_front(matrix, weights, table):
    rows, width = matrix.shape
    devices = lax.axis_size("front")
    count, tiles = rows // TILE, width // TILE
    skip = 1 if count % GROUP_TILES == 0 else 0
    separator = width // GROUP_TILES
    sent = (count - skip) * TILE
    distances = []
    while 2 ** (len(distances) + 1) < devices:
        distances.insert(0, 2 ** (len(distances) + 1))

    def spread(pieces):
        for distance in distances:
            pieces = pieces + [from_front(piece, distance) for piece in pieces]
        return pieces

    vmem = pl.BlockSpec(memory_space=pltpu.VMEM)
    smem = pl.BlockSpec(memory_space=pltpu.SMEM)
    anywhere = pl.BlockSpec(memory_space=pl.ANY)
    f32, bf16 = jnp.float32, jnp.bfloat16
    params = pltpu.CompilerParams(vmem_limit_bytes=VMEM_BYTES)
    small = pltpu.CompilerParams(vmem_limit_bytes=VMEM_BYTES // 3)

    corner = list(range(0, tiles, GROUP_TILES))
    rest = [t for t in range(tiles) if t % GROUP_TILES and t != 1]
    slab = pl.pallas_call(
        functools.partial(slab_kernel, chosen=corner),
        out_shape=jax.ShapeDtypeStruct((TILE + SLAB, separator), f32),
        in_specs=[anywhere, vmem],
        out_specs=vmem,
        scratch_shapes=[pltpu.SemaphoreType.DMA((len(corner),))],
        compiler_params=params,
        cost_estimate=pl.CostEstimate(flops=0, bytes_accessed=2**19, transcendentals=0),
        name="slab",
    )(matrix, weights[None])
    far_slab = from_sibling(slab)
    slabs = spread([slab])
    edge, far_body = pl.pallas_call(
        functools.partial(body_kernel, skip=skip, chosen=corner + [1], rest=rest),
        out_shape=(
            jax.ShapeDtypeStruct((sent, (len(corner) + 1) * TILE), f32),
            jax.ShapeDtypeStruct((sent, len(rest) * TILE), f32),
        ),
        in_specs=[anywhere],
        out_specs=(vmem, vmem),
        scratch_shapes=[pltpu.SemaphoreType.DMA((2 * tiles,))],
        compiler_params=params,
        cost_estimate=pl.CostEstimate(flops=0, bytes_accessed=2**23, transcendentals=0),
        name="body",
    )(after(matrix, slab))
    far_slabs = spread([after(far_slab, edge)])
    other_slabs = [from_front(piece, 1) for piece in slabs]
    other_far_slabs = [from_front(piece, 1) for piece in far_slabs]
    far_edge = from_sibling(after(edge, far_slab))
    far = from_sibling(after(far_body, far_slab))
    near_edges = spread([after(edge, *far_slabs)])

    state = jax.ShapeDtypeStruct((2, separator, separator), f32)
    scratch = pltpu.VMEM((2 * TILE, TILE), f32)
    cost = pl.CostEstimate(flops=3 * 10**9, bytes_accessed=2**22, transcendentals=0)
    middle = separator // TILE // 2
    half_kernel = functools.partial(corner_kernel, order=separator, count=count, devices=devices)
    state_one, state_two, heads = pl.pallas_call(
        functools.partial(half_kernel, first=0, last=middle),
        out_shape=(state, state, jax.ShapeDtypeStruct((2, SLAB, separator), f32)),
        in_specs=[vmem] * (2 * devices),
        out_specs=(vmem, vmem, vmem),
        scratch_shapes=[scratch],
        compiler_params=small,
        cost_estimate=cost,
        name="corner_first",
    )(*slabs, *other_slabs, *far_slabs, *other_far_slabs)

    other_edges = [from_front(after(piece, heads), 1) for piece in near_edges]
    far_edges = spread([after(far_edge, heads)])
    inverse = pl.pallas_call(
        functools.partial(half_kernel, first=middle, last=separator // TILE),
        out_shape=state,
        in_specs=[vmem, vmem],
        out_specs=vmem,
        scratch_shapes=[pltpu.VMEM((2, separator, separator), f32), scratch],
        compiler_params=small,
        cost_estimate=cost,
        name="corner_second",
    )(after(state_one, far_edge), state_two)
    other_far_edges = [from_front(after(piece, inverse), 1) for piece in far_edges]

    sizes = dict(count=count, skip=skip, devices=devices)
    edge_space = pltpu.VMEM((devices,) + edge.shape, f32)
    panel_space = pltpu.VMEM((devices, sent, separator), bf16)
    update_shape = jax.ShapeDtypeStruct((rows, M2 - TILE), f32)
    panel_shape = jax.ShapeDtypeStruct((devices, sent, separator), bf16)
    large = pltpu.CompilerParams(vmem_limit_bytes=VMEM_BYTES * 3 // 4)
    leaf_panel, column, total = pl.pallas_call(
        functools.partial(own_kernel, width=width, **sizes),
        out_shape=(
            jax.ShapeDtypeStruct((rows, separator), f32),
            jax.ShapeDtypeStruct((M2, TILE), f32),
            update_shape,
        ),
        in_specs=[smem, vmem, vmem, vmem, vmem] + [anywhere] * (1 + devices),
        out_specs=(vmem, vmem, anywhere),
        scratch_shapes=[
            edge_space,
            pltpu.VMEM((sent, width), f32),
            panel_space,
            panel_space,
            pltpu.VMEM((rows + TILE, M2), f32),
            pltpu.SemaphoreType.DMA((devices,)),
            pltpu.SemaphoreType.DMA((2,)),
        ],
        compiler_params=large,
        cost_estimate=pl.CostEstimate(flops=2 * 10**9, bytes_accessed=2**22, transcendentals=0),
        name="own",
    )(table, heads, weights[None], slab, inverse, matrix, *near_edges, *other_edges)
    parent_panel, update, far_high, far_low = pl.pallas_call(
        functools.partial(parent_kernel, width=width, **sizes),
        out_shape=(jax.ShapeDtypeStruct((rows, TILE), f32), update_shape, panel_shape, panel_shape),
        in_specs=[smem, vmem] + [anywhere] * (2 + devices),
        out_specs=(vmem, anywhere, anywhere, anywhere),
        scratch_shapes=[
            edge_space,
            panel_space,
            panel_space,
            pltpu.VMEM((M2, TILE), f32),
            pltpu.VMEM((M2, 3 * TILE), bf16),
            pltpu.VMEM((M2, 3 * TILE), bf16),
            pltpu.VMEM(update_shape.shape, f32),
            pltpu.VMEM((TILE, TILE), f32),
            pltpu.SemaphoreType.DMA((devices,)),
            pltpu.SemaphoreType.DMA((4 + M2 // 512,)),
        ],
        compiler_params=large,
        cost_estimate=pl.CostEstimate(flops=3 * 10**9, bytes_accessed=2**22, transcendentals=0),
        name="parent",
    )(table, inverse, column, total, *far_edges, *other_far_edges)
    update = pl.pallas_call(
        functools.partial(far_kernel, **sizes),
        out_shape=update_shape,
        in_specs=[smem] + [anywhere] * 4,
        out_specs=anywhere,
        scratch_shapes=[
            panel_space,
            panel_space,
            pltpu.VMEM(far.shape, f32),
            pltpu.VMEM((devices * (count - skip) ** 2, TILE, TILE), f32),
            pltpu.SemaphoreType.DMA((3,)),
            pltpu.SemaphoreType.DMA((devices * (count - skip) ** 2,)),
            pltpu.SemaphoreType.DMA((devices * (count - skip) ** 2,)),
        ],
        input_output_aliases={4: 0},
        compiler_params=large,
        cost_estimate=pl.CostEstimate(flops=10**9, bytes_accessed=2**21, transcendentals=0),
        name="far",
    )(table, far_high, far_low, far, update)
    return leaf_panel, parent_panel, update


def on_device(leaf_fronts, screen_weights, parent_tile_index):
    results = [
        one_front(leaf_fronts[0, g], screen_weights[0, g], parent_tile_index[:, g])
        for g in range(leaf_fronts.shape[1])
    ]
    return tuple(jnp.stack(parts)[None] for parts in zip(*results))


def solution(mesh):
    in_specs = (P("leaf", None, "front", None), P("leaf", None, "front"), P())
    out_specs = (
        P("leaf", None, "front", None),
        P("leaf", None, "front", None),
        P("leaf", None, "front", None),
    )
    return jax.shard_map(
        on_device, mesh=mesh, in_specs=in_specs, out_specs=out_specs, check_vma=False
    )
```

```python
import functools

import jax
import jax.numpy as jnp
from jax import lax
from jax.experimental import pallas as pl
from jax.experimental.pallas import tpu as pltpu
from jax.sharding import PartitionSpec as P

SEP2 = 1024
PANEL_WIDTH = 128
M2 = 4096
GROUP_TILES = 4
SLAB = 8
GROUP = 32
EXACT = lax.Precision.HIGHEST
VMEM_BYTES = 60 * 2**20

TILE = PANEL_WIDTH
LAST = ((1,), (1,))
PLAIN = ((1,), (0,))
FIRST = ((0,), (0,))


def from_front(value, distance):
    pairs = [(source, source ^ distance) for source in range(lax.axis_size("front"))]
    return lax.ppermute(value, "front", pairs)


def from_sibling(value):
    pairs = [(source, source ^ 1) for source in range(lax.axis_size("leaf"))]
    return lax.ppermute(value, "leaf", pairs)


def after(value, *events):
    return lax.optimization_barrier((value, *events))[0]


def slot_of(offset, count):
    slot, bit, weight = 0, 1, count // 2
    while weight:
        slot = slot + jnp.where((offset & bit) != 0, weight, 0)
        bit, weight = bit * 2, weight // 2
    return slot


def offset_of(slot, count):
    offset, bit, weight = 0, 1, count // 2
    while weight:
        offset += bit if slot & weight else 0
        bit, weight = bit * 2, weight // 2
    return offset


def exact_dot(left, right, contract):
    return lax.dot_general(
        left, right, (contract, ((), ())), precision=EXACT, preferred_element_type=jnp.float32
    )


def plain_dot(left, right):
    return lax.dot_general(left, right, (LAST, ((), ())), preferred_element_type=jnp.float32)


def halves(value):
    high = value.astype(jnp.bfloat16)
    return high, (value - high.astype(jnp.float32)).astype(jnp.bfloat16)


def split_dot(left, right):
    return plain_dot(left[0], right[0]) + (plain_dot(left[0], right[1]) + plain_dot(left[1], right[0]))


def lane(row, index):
    return jnp.broadcast_to(row[:, index : index + 1], row.shape)


def sum_tree(terms):
    while len(terms) > 1:
        terms = [sum(terms[i : i + 2]) for i in range(0, len(terms), 2)]
    return terms[0]


def factor_slab(rows, first, inside, lanes):
    entry = {(i, j): lane(rows[i], first + j) for i in range(SLAB) for j in range(i + 1)}
    rows = [jnp.where(inside, jnp.where(lanes == first + i, 1.0, 0.0), row) for i, row in enumerate(rows)]
    done = []
    for p in range(0, SLAB, 2):
        r = p + 1
        one, mixed, two = entry[p, p], entry[r, p], entry[r, r]
        inverse_one = pl.reciprocal(one, approx=True)
        inverse_two = pl.reciprocal(one * two - mixed * mixed, approx=True) * one
        factor = {i: entry[i, p] * inverse_one for i in range(r, SLAB)}
        rows[r] = rows[r] - factor[r] * rows[p]
        for i in range(p + 2, SLAB):
            entry[i, r] = entry[i, r] - factor[i] * mixed
        for i in range(p + 2, SLAB):
            second = entry[i, r] * inverse_two
            for k in range(p + 2, i + 1):
                entry[i, k] = (entry[i, k] - factor[i] * entry[k, p]) - second * entry[k, r]
            rows[i] = (rows[i] - factor[i] * rows[p]) - second * rows[r]
        done.append(rows[p] * lax.rsqrt(one))
        done.append(rows[r] * (inverse_two * lax.rsqrt(inverse_two)))
    return done


def factor_steps(a, fronts):
    lanes = lax.broadcasted_iota(jnp.int32, (fronts, TILE), 1)
    columns = lax.broadcasted_iota(jnp.int32, (TILE, TILE), 1)
    settled = (lax.broadcasted_iota(jnp.int32, (GROUP, TILE), 0) & -SLAB) + SLAB

    def at(i):
        return pl.ds(fronts * i, fronts)

    for start in range(0, TILE, GROUP):
        stop = start + GROUP
        rows = [a[at(i), :] for i in range(start, stop)]
        for s in range(0, GROUP, SLAB):
            first = start + s
            inside = (lanes >= first) & (lanes < first + SLAB)
            head = factor_slab(rows[s : s + SLAB], first, inside, lanes)
            for i in range(SLAB):
                a[at(first + i), :] = head[i]
            for i in range(s + SLAB, GROUP):
                terms = [lane(row, start + i) * row for row in head]
                rows[i] = jnp.where(inside, 0.0, rows[i]) - sum_tree(terms)
            if s + SLAB < GROUP:
                yield
        if stop < TILE:
            for q in range(fronts):
                upper = a[pl.ds(fronts * start + q, GROUP, stride=fronts), :]
                rest = pl.ds(fronts * stop + q, TILE - stop, stride=fronts)
                inverse = jnp.where((columns[:GROUP] >= start + settled) & (columns[:GROUP] < stop), 0.0, upper)
                product = exact_dot(upper, inverse, FIRST)[stop:]
                group = columns[stop:]
                kept = jnp.where((group >= start) & (group < stop), 0.0, a[rest, :])
                a[rest, :] = kept - product
        yield


def place():
    leaf, front = lax.axis_index("leaf"), lax.axis_index("front")
    return leaf, front, leaf & 1


def corner_kernel(*refs, order, first, last, count, devices):
    tiles = order // TILE
    pieces = 2 * devices
    if first == 0:
        slabs, (work, out, heads, a) = refs[:pieces], refs[pieces:]
    else:
        old_work, old_out, out, work, a = refs
    fronts = out.shape[0]
    if first == 0:
        front = place()[1]

        def copy(owner, q, take):
            slot = slot_of(front ^ owner, devices)
            for s in range(devices):

                @pl.when(slot == s)
                def _():
                    take(slabs[q * devices + s])

        for q in range(fronts):
            for e in range(tiles):

                def take_tile(slab):
                    work[q, e * TILE : (e + 1) * TILE, :] = slab[:TILE, :]

                copy(e * GROUP_TILES // count, q, take_tile)

            def take_head(slab):
                heads[q] = slab[TILE:, :]

            copy(0, q, take_head)
    else:
        work[...] = old_work[...]
        out[...] = old_out[...]

    def step(k, carry):
        block = pl.ds(pl.multiple_of(k * TILE, TILE), TILE)
        for q in range(fronts):
            a[pl.ds(q, TILE, stride=fronts), :] = work[q, block, block]
        for _ in factor_steps(a, fronts):
            pass
        kept = lax.broadcasted_iota(jnp.int32, (TILE, TILE), 0) >= lax.broadcasted_iota(jnp.int32, (TILE, TILE), 1)
        for q in range(fronts):
            out[q, block, block] = jnp.where(kept, a[pl.ds(q, TILE, stride=fronts), :], 0.0)
        for fixed in range(first, last):

            @pl.when(k == fixed)
            def _():
                here = slice(fixed * TILE, (fixed + 1) * TILE)
                low, rest = slice(0, fixed * TILE), slice((fixed + 1) * TILE, order)
                for q in range(fronts):
                    corner = out[q, here, here]
                    if fixed:
                        chain = exact_dot(work[q, here, low], out[q, low, low], PLAIN)
                        out[q, here, low] = -exact_dot(corner, chain, PLAIN)
                    if fixed + 1 < tiles:
                        out[q, here, rest] = jnp.zeros((TILE, order - (fixed + 1) * TILE), jnp.float32)
                        below = exact_dot(work[q, rest, here], corner, LAST)
                        work[q, rest, here] = below
                        work[q, rest, rest] = work[q, rest, rest] - exact_dot(below, below, LAST)

        return carry

    lax.fori_loop(first, last, step, 0)


def at(tile):
    return pl.ds(pl.multiple_of(tile * TILE, TILE), TILE)


def goal_of(table, i, tile):
    entry = 3 * (tile >> 2) + (tile & 3) - 1
    return jnp.where((tile & 3) == 0, -1, table[place()[0] ^ i, jnp.maximum(entry, 0)])


def panel_of(inverse):
    turned = halves(inverse)
    cut = inverse.shape[0] // 2
    top = tuple(part[:cut, :cut] for part in turned)
    bottom = tuple(part[cut:, :] for part in turned)

    def product(block):
        full = halves(block)
        left = split_dot(tuple(part[:, :cut] for part in full), top)
        return jnp.concatenate([left, split_dot(full, bottom)], axis=1)

    return product


def add_columns(table, i, edges, panel_high, panel_low, column, *, count, skip, devices):
    front = place()[1]
    separator = panel_high.shape[2]
    first = slice((1 - skip) * TILE, (2 - skip) * TILE)
    slot = slot_of(front, devices)
    one = panel_high[slot, first, :], panel_low[slot, first, :]
    for s in range(devices):
        piece = edges[s][:, separator:] - split_dot((panel_high[s], panel_low[s]), one)
        owner = front ^ offset_of(s, devices)
        for t in range(count - skip):
            target = goal_of(table, i, owner * count + skip + t)

            @pl.when(target >= 0)
            def _():
                column[at(target), :] += piece[t * TILE : (t + 1) * TILE, :]


def own_kernel(*refs, count, skip, width, devices):
    table, heads, weights, slab, inverse, fronts_here = refs[:6]
    edges = refs[6 : 6 + devices]
    leaf_panel, column, total, panel_high, panel_low = refs[6 + devices :]
    leaf, front, half = place()
    sent = count - skip
    separator = width // GROUP_TILES
    rows = count * TILE
    first_row = (front * 2 + half) * rows

    total[...] = jnp.zeros_like(total)
    column[...] = jnp.zeros_like(column)
    row_ids = lax.broadcasted_iota(jnp.int32, (TILE, TILE), 0)
    col_ids = lax.broadcasted_iota(jnp.int32, (TILE, TILE), 1)
    near = jnp.where(jnp.abs(row_ids - col_ids) == 1, 1.0, 0.0)
    before = jnp.where((row_ids == 0) & (col_ids == TILE - 1), 1.0, 0.0)
    behind = jnp.where((row_ids == TILE - 1) & (col_ids == 0), 1.0, 0.0)
    first_weights = jnp.where(half == 0, heads[0, 0:1, :TILE], heads[1, 0:1, :TILE])
    column[:TILE, :] = jnp.where(row_ids == col_ids, first_weights + 4.0, 0.0) - near
    column[TILE : 2 * TILE, :] = -before
    inside = first_row < SEP2
    weight = jnp.transpose(jnp.broadcast_to(weights[...], (TILE, rows)))
    for j in range(count):
        mine = (front * 2 + half) * count + j
        line = slice(j * TILE, (j + 1) * TILE)
        total[line, at(mine)] = jnp.where(
            row_ids == col_ids, weight[line, :] + jnp.where(inside, 4.0, 0.0), 0.0
        ) - jnp.where(inside, near, 0.0)

        @pl.when((mine > 0) & inside)
        def _():
            total[line, at(mine - 1)] = -before

        @pl.when((mine + 1) * TILE < SEP2)
        def _():
            total[line, at(mine + 1)] = -behind

    panel_from = panel_of(inverse[0])
    if skip:
        leaf_panel[:TILE, :] = panel_from(slab[:TILE, :])
    for s in range(devices):
        panel = panel_from(edges[s][:, :separator])
        if s == 0:
            leaf_panel[skip * TILE :, :] = panel
        panel_high[s], panel_low[s] = halves(panel)
    add_columns(table, 0, edges, panel_high, panel_low, column, count=count, skip=skip, devices=devices)

    for s in range(devices):
        product = split_dot((panel_high[0], panel_low[0]), (panel_high[s], panel_low[s]))
        for c in range(sent):
            tile = (front ^ offset_of(s, devices)) * count + skip + c
            goal = jnp.maximum(goal_of(table, 0, tile), 0)
            for t in range(sent):
                target = goal_of(table, 0, front * count + skip + t) - (front * 2 + half) * count
                target = jnp.where((target >= 0) & (target < count), target, count)
                line = slice(t * TILE, (t + 1) * TILE)
                source = fronts_here[(skip + t) * TILE : (skip + t + 1) * TILE, at(tile)]
                total[at(target), at(goal)] += source - product[line, c * TILE : (c + 1) * TILE]


def parent_kernel(*refs, count, skip, width, devices):
    table, inverse, column_in, total = refs[:4]
    edges = refs[4 : 4 + devices]
    panel_out, update_out, panel_high, panel_low = refs[4 + devices : 8 + devices]
    column, two_left, two_right, update, a, done = refs[8 + devices :]
    leaf, front, half = place()
    separator = width // GROUP_TILES
    rows = count * TILE
    first_row = pl.multiple_of((front * 2 + half) * rows, TILE)

    column[...] = column_in[...]
    panel_from = panel_of(inverse[1])
    for s in range(devices):
        panel_high[s], panel_low[s] = halves(panel_from(edges[s][:, :separator]))
    add_columns(table, 1, edges, panel_high, panel_low, column, count=count, skip=skip, devices=devices)

    a[...] = column[:TILE, :]
    for _ in factor_steps(a, 1):
        pass
    row_ids = lax.broadcasted_iota(jnp.int32, (TILE, TILE), 0)
    col_ids = lax.broadcasted_iota(jnp.int32, (TILE, TILE), 1)
    turned = halves(jnp.where(row_ids >= col_ids, a[...], 0.0))
    for start in range(0, M2, 1024):
        block = slice(start, start + 1024)
        panel = split_dot(halves(column[block, :]), turned)
        column[block, :] = panel
        high, low = halves(panel)
        two_left[block, :] = jnp.concatenate([high, high, low], axis=1)
        two_right[block, :] = jnp.concatenate([high, low, high], axis=1)
    mine = pl.ds(first_row, rows)
    panel_out[...] = column[mine, :]
    own = two_left[mine, :]
    sends = []
    for start in range(TILE, M2, 512):
        stop = min(start + 512, M2)
        here = slice(start - TILE, stop - TILE)
        update[:, here] = total[:rows, start:stop] - plain_dot(own, two_right[start:stop, :])
        send = pltpu.make_async_copy(update.at[:, here], update_out.at[:, here], done.at[len(sends)])
        send.start()
        sends.append(send)
    for send in sends:
        send.wait()


def far_kernel(table, panel_high, panel_low, *refs, count, skip, devices, cut):
    beyond, (update, out, tiles, got, put) = refs[:2], refs[2:]
    leaf, front, half = place()
    sent = count - skip

    def each(s, t, c):
        tile = (front ^ offset_of(s, devices)) * count + skip + c
        goal = goal_of(table, 1, tile)
        target = goal_of(table, 1, front * count + skip + t) - (front * 2 + half) * count
        valid = (goal > 0) & (target >= 0) & (target < count)
        index = (s * sent + t) * sent + c
        lies = out.at[at(jnp.clip(target, 0, count - 1)), at(jnp.maximum(goal - 1, 0))]
        return tile, index, valid, lies

    def fetch(index, lies):
        return pltpu.make_async_copy(lies, tiles.at[index], got.at[index])

    def store(index, lies):
        return pltpu.make_async_copy(tiles.at[index], lies, put.at[index])

    for s in range(devices):
        for t in range(sent):
            for c in range(sent):
                _, index, valid, lies = each(s, t, c)

                @pl.when(valid)
                def _():
                    fetch(index, lies).start()

    for s in range(devices):
        product = split_dot((panel_high[0], panel_low[0]), (panel_high[s], panel_low[s]))
        for t in range(sent):
            line = slice(t * TILE, (t + 1) * TILE)
            for c in range(sent):
                tile, index, valid, lies = each(s, t, c)

                source = jnp.maximum(tile - (tile >> 2) - 2, 0)

                @pl.when(valid)
                def _():
                    fetch(index, lies).wait()
                    tiles[index] += -product[line, c * TILE : (c + 1) * TILE]

                @pl.when(valid & (source < cut))
                def _():
                    tiles[index] += beyond[0][line, at(jnp.minimum(source, cut - 1))]

                @pl.when(valid & (source >= cut))
                def _():
                    tiles[index] += beyond[1][line, at(jnp.maximum(source - cut, 0))]

                @pl.when(valid)
                def _():
                    store(index, lies).start()

    for s in range(devices):
        for t in range(sent):
            for c in range(sent):
                _, index, valid, lies = each(s, t, c)

                @pl.when(valid)
                def _():
                    store(index, lies).wait()


def slab_kernel(matrix, weights, slab, kept, done, *, chosen):
    copies = [
        pltpu.make_async_copy(
            matrix.at[:TILE, t * TILE : (t + 1) * TILE], slab.at[:TILE, k * TILE : (k + 1) * TILE], done.at[k]
        )
        for k, t in enumerate(chosen)
    ]
    for copy in copies:
        copy.start()
    slab[TILE:, :] = jnp.zeros_like(slab[TILE:, :])
    slab[TILE : TILE + 1, : weights.shape[1]] = weights[...]
    for copy in copies:
        copy.wait()
    kept[...] = slab[...]


def body_kernel(matrix, edge, *refs, skip, chosen, rest):
    parts, done = refs[:-1], refs[-1]
    copies = []
    for target, tiles in ((edge, chosen), *zip(parts, rest)):
        filled = 0
        while filled < len(tiles):
            stop = filled + 1
            while stop < len(tiles) and tiles[stop] == tiles[stop - 1] + 1:
                stop += 1
            copies.append(
                pltpu.make_async_copy(
                    matrix.at[skip * TILE :, tiles[filled] * TILE : (tiles[stop - 1] + 1) * TILE],
                    target.at[:, filled * TILE : stop * TILE],
                    done.at[len(copies)],
                )
            )
            filled = stop
    for copy in copies:
        copy.start()
    for copy in copies:
        copy.wait()


def one_front(matrix, weights, table):
    rows, width = matrix.shape
    devices = lax.axis_size("front")
    count, tiles = rows // TILE, width // TILE
    skip = 1 if count % GROUP_TILES == 0 else 0
    separator = width // GROUP_TILES
    sent = (count - skip) * TILE
    distances = []
    while 2 ** (len(distances) + 1) < devices:
        distances.insert(0, 2 ** (len(distances) + 1))

    def spread(pieces):
        for distance in distances:
            pieces = pieces + [from_front(piece, distance) for piece in pieces]
        return pieces

    vmem = pl.BlockSpec(memory_space=pltpu.VMEM)
    smem = pl.BlockSpec(memory_space=pltpu.SMEM)
    hbm = pl.BlockSpec(memory_space=pl.ANY)
    f32, bf16 = jnp.float32, jnp.bfloat16
    params = pltpu.CompilerParams(vmem_limit_bytes=VMEM_BYTES)
    small = pltpu.CompilerParams(vmem_limit_bytes=VMEM_BYTES // 3)

    corner = list(range(0, tiles, GROUP_TILES))
    rest = [t for t in range(tiles) if t % GROUP_TILES and t != 1]
    slab, kept = pl.pallas_call(
        functools.partial(slab_kernel, chosen=corner),
        out_shape=(jax.ShapeDtypeStruct((TILE + SLAB, separator), f32),) * 2,
        in_specs=[hbm, vmem],
        out_specs=(vmem, vmem),
        scratch_shapes=[pltpu.SemaphoreType.DMA((len(corner),))],
        compiler_params=params,
        cost_estimate=pl.CostEstimate(flops=0, bytes_accessed=2**19, transcendentals=0),
        name="slab",
    )(matrix, weights[None])
    far_slab = from_sibling(slab)
    slabs = spread([slab])
    cut = len(rest) * 3 // 11
    rest = (rest[:cut], rest[cut:])
    edge, *bodies = pl.pallas_call(
        functools.partial(body_kernel, skip=skip, chosen=corner + [1], rest=rest),
        out_shape=(
            jax.ShapeDtypeStruct((sent, (len(corner) + 1) * TILE), f32),
            *(jax.ShapeDtypeStruct((sent, len(part) * TILE), f32) for part in rest),
        ),
        in_specs=[hbm],
        out_specs=(vmem, vmem, vmem),
        scratch_shapes=[pltpu.SemaphoreType.DMA((2 * tiles,))],
        compiler_params=params,
        cost_estimate=pl.CostEstimate(flops=0, bytes_accessed=2**23, transcendentals=0),
        name="body",
    )(after(matrix, slab))
    far_slabs = spread([after(far_slab, edge, *slabs)])
    other_slabs = [from_front(piece, 1) for piece in slabs]
    other_far_slabs = [from_front(piece, 1) for piece in far_slabs]
    far_edge = from_sibling(after(edge, far_slab))
    far = [from_sibling(after(bodies[0], far_slab))]
    near_edges = spread([after(edge, *far_slabs)])

    state = jax.ShapeDtypeStruct((2, separator, separator), f32)
    scratch = pltpu.VMEM((2 * TILE, TILE), f32)
    cost = pl.CostEstimate(flops=3 * 10**9, bytes_accessed=2**22, transcendentals=0)
    middle = separator // TILE // 2
    half_kernel = functools.partial(corner_kernel, order=separator, count=count, devices=devices)
    state_one, state_two, heads = pl.pallas_call(
        functools.partial(half_kernel, first=0, last=middle),
        out_shape=(state, state, jax.ShapeDtypeStruct((2, SLAB, separator), f32)),
        in_specs=[vmem] * (2 * devices),
        out_specs=(vmem, vmem, vmem),
        scratch_shapes=[scratch],
        compiler_params=small,
        cost_estimate=cost,
        name="corner_first",
    )(kept, *slabs[1:], *other_slabs, *far_slabs, *other_far_slabs)

    far.append(from_sibling(after(bodies[1], heads)))
    far_edges = spread([after(far_edge, heads)])
    inverse = pl.pallas_call(
        functools.partial(half_kernel, first=middle, last=separator // TILE),
        out_shape=state,
        in_specs=[vmem, vmem],
        out_specs=vmem,
        scratch_shapes=[pltpu.VMEM((2, separator, separator), f32), scratch],
        compiler_params=small,
        cost_estimate=cost,
        name="corner_second",
    )(after(state_one, far_edge, far[0]), state_two)
    other_edges = [from_front(after(piece, inverse), 1) for piece in near_edges]
    other_far_edges = [from_front(after(piece, inverse), 1) for piece in far_edges]

    sizes = dict(count=count, skip=skip, devices=devices)
    panel_space = pltpu.VMEM((devices, sent, separator), bf16)
    update_shape = jax.ShapeDtypeStruct((rows, M2 - TILE), f32)
    panel_shape = jax.ShapeDtypeStruct((devices, sent, separator), bf16)
    large = pltpu.CompilerParams(vmem_limit_bytes=VMEM_BYTES // 2)
    leaf_panel, column, total = pl.pallas_call(
        functools.partial(own_kernel, width=width, **sizes),
        out_shape=(
            jax.ShapeDtypeStruct((rows, separator), f32),
            jax.ShapeDtypeStruct((M2, TILE), f32),
            jax.ShapeDtypeStruct((rows + TILE, M2), f32),
        ),
        in_specs=[smem] + [vmem] * (5 + devices),
        out_specs=(vmem, vmem, vmem),
        scratch_shapes=[panel_space, panel_space],
        compiler_params=large,
        cost_estimate=pl.CostEstimate(flops=2 * 10**9, bytes_accessed=2**22, transcendentals=0),
        name="own",
    )(table, heads, weights[None], kept, inverse, matrix, *near_edges, *other_edges)
    parent_panel, update, far_high, far_low = pl.pallas_call(
        functools.partial(parent_kernel, width=width, **sizes),
        out_shape=(jax.ShapeDtypeStruct((rows, TILE), f32), update_shape, panel_shape, panel_shape),
        in_specs=[smem] + [vmem] * (3 + devices),
        out_specs=(vmem, hbm, vmem, vmem),
        scratch_shapes=[
            pltpu.VMEM((M2, TILE), f32),
            pltpu.VMEM((M2, 3 * TILE), bf16),
            pltpu.VMEM((M2, 3 * TILE), bf16),
            pltpu.VMEM(update_shape.shape, f32),
            pltpu.VMEM((TILE, TILE), f32),
            pltpu.SemaphoreType.DMA((M2 // 512,)),
        ],
        compiler_params=large,
        cost_estimate=pl.CostEstimate(flops=3 * 10**9, bytes_accessed=2**22, transcendentals=0),
        name="parent",
    )(table, inverse, column, total, *far_edges, *other_far_edges)
    update = pl.pallas_call(
        functools.partial(far_kernel, cut=cut, **sizes),
        out_shape=update_shape,
        in_specs=[smem] + [vmem] * 4 + [hbm],
        out_specs=hbm,
        scratch_shapes=[
            pltpu.VMEM((devices * (count - skip) ** 2, TILE, TILE), f32),
            pltpu.SemaphoreType.DMA((devices * (count - skip) ** 2,)),
            pltpu.SemaphoreType.DMA((devices * (count - skip) ** 2,)),
        ],
        input_output_aliases={5: 0},
        compiler_params=large,
        cost_estimate=pl.CostEstimate(flops=10**9, bytes_accessed=2**21, transcendentals=0),
        name="far",
    )(table, far_high, far_low, *far, update)
    return leaf_panel, parent_panel, update


def on_device(leaf_fronts, screen_weights, parent_tile_index):
    results = [
        one_front(leaf_fronts[0, g], screen_weights[0, g], parent_tile_index[:, g])
        for g in range(leaf_fronts.shape[1])
    ]
    return tuple(jnp.stack(parts)[None] for parts in zip(*results))


def solution(mesh):
    in_specs = (P("leaf", None, "front", None), P("leaf", None, "front"), P())
    out_specs = (
        P("leaf", None, "front", None),
        P("leaf", None, "front", None),
        P("leaf", None, "front", None),
    )
    return jax.shard_map(
        on_device, mesh=mesh, in_specs=in_specs, out_specs=out_specs, check_vma=False
    )
```

```python
import functools

import jax
import jax.numpy as jnp
from jax import lax
from jax.experimental import pallas as pl
from jax.experimental.pallas import tpu as pltpu
from jax.sharding import PartitionSpec as P

SEP2 = 1024
PANEL_WIDTH = 128
M2 = 4096
GROUP_TILES = 4
SLAB = 8
GROUP = 32
EXACT = lax.Precision.HIGHEST
VMEM_BYTES = 60 * 2**20

TILE = PANEL_WIDTH
LAST = ((1,), (1,))
PLAIN = ((1,), (0,))
FIRST = ((0,), (0,))


def from_front(value, distance):
    pairs = [(source, source ^ distance) for source in range(lax.axis_size("front"))]
    return lax.ppermute(value, "front", pairs)


def from_sibling(value):
    pairs = [(source, source ^ 1) for source in range(lax.axis_size("leaf"))]
    return lax.ppermute(value, "leaf", pairs)


def after(value, *events):
    return lax.optimization_barrier((value, *events))[0]


def slot_of(offset, count):
    slot, bit, weight = 0, 1, count // 2
    while weight:
        slot = slot + jnp.where((offset & bit) != 0, weight, 0)
        bit, weight = bit * 2, weight // 2
    return slot


def offset_of(slot, count):
    offset, bit, weight = 0, 1, count // 2
    while weight:
        offset += bit if slot & weight else 0
        bit, weight = bit * 2, weight // 2
    return offset


def exact_dot(left, right, contract):
    return lax.dot_general(
        left, right, (contract, ((), ())), precision=EXACT, preferred_element_type=jnp.float32
    )


def plain_dot(left, right):
    return lax.dot_general(left, right, (LAST, ((), ())), preferred_element_type=jnp.float32)


def halves(value):
    high = value.astype(jnp.bfloat16)
    return high, (value - high.astype(jnp.float32)).astype(jnp.bfloat16)


def split_dot(left, right):
    return plain_dot(left[0], right[0]) + (plain_dot(left[0], right[1]) + plain_dot(left[1], right[0]))


def lane(row, index):
    return jnp.broadcast_to(row[:, index : index + 1], row.shape)


def sum_tree(terms):
    while len(terms) > 1:
        terms = [sum(terms[i : i + 2]) for i in range(0, len(terms), 2)]
    return terms[0]


def factor_slab(rows, first, inside, lanes):
    entry = {(i, j): lane(rows[i], first + j) for i in range(SLAB) for j in range(i + 1)}
    rows = [jnp.where(inside, jnp.where(lanes == first + i, 1.0, 0.0), row) for i, row in enumerate(rows)]
    done = []
    for p in range(0, SLAB, 2):
        r = p + 1
        one, mixed, two = entry[p, p], entry[r, p], entry[r, r]
        inverse_one = pl.reciprocal(one, approx=True)
        inverse_two = pl.reciprocal(one * two - mixed * mixed, approx=True) * one
        factor = {i: entry[i, p] * inverse_one for i in range(r, SLAB)}
        rows[r] = rows[r] - factor[r] * rows[p]
        for i in range(p + 2, SLAB):
            entry[i, r] = entry[i, r] - factor[i] * mixed
        for i in range(p + 2, SLAB):
            second = entry[i, r] * inverse_two
            for k in range(p + 2, i + 1):
                entry[i, k] = (entry[i, k] - factor[i] * entry[k, p]) - second * entry[k, r]
            rows[i] = (rows[i] - factor[i] * rows[p]) - second * rows[r]
        done.append(rows[p] * lax.rsqrt(one))
        done.append(rows[r] * (inverse_two * lax.rsqrt(inverse_two)))
    return done


def row_of(q):
    return pl.ds(q, TILE, stride=SLAB)


def clear_rows(a):
    row_ids = lax.broadcasted_iota(jnp.int32, a.shape, 0) & -SLAB
    col_ids = lax.broadcasted_iota(jnp.int32, a.shape, 1) * SLAB
    a[...] = (row_ids == col_ids).astype(jnp.float32)


def factor_steps(a, fronts):
    lanes = lax.broadcasted_iota(jnp.int32, (SLAB, TILE), 1)
    columns = lax.broadcasted_iota(jnp.int32, (TILE, TILE), 1)
    settled = (lax.broadcasted_iota(jnp.int32, (GROUP, TILE), 0) & -SLAB) + SLAB

    def at(i):
        return pl.ds(SLAB * i, SLAB)

    for start in range(0, TILE, GROUP):
        stop = start + GROUP
        rows = [a[at(i), :] for i in range(start, stop)]
        for s in range(0, GROUP, SLAB):
            first = start + s
            inside = (lanes >= first) & (lanes < first + SLAB)
            head = factor_slab(rows[s : s + SLAB], first, inside, lanes)
            for i in range(SLAB):
                a[at(first + i), :] = head[i]
            for i in range(s + SLAB, GROUP):
                terms = [lane(row, start + i) * row for row in head]
                rows[i] = jnp.where(inside, 0.0, rows[i]) - sum_tree(terms)
            if s + SLAB < GROUP:
                yield
        if stop < TILE:
            for q in range(fronts):
                upper = a[pl.ds(SLAB * start + q, GROUP, stride=SLAB), :]
                rest = pl.ds(SLAB * stop + q, TILE - stop, stride=SLAB)
                inverse = jnp.where((columns[:GROUP] >= start + settled) & (columns[:GROUP] < stop), 0.0, upper)
                product = exact_dot(upper, inverse, FIRST)[stop:]
                group = columns[stop:]
                kept = jnp.where((group >= start) & (group < stop), 0.0, a[rest, :])
                a[rest, :] = kept - product
        yield


def place():
    leaf, front = lax.axis_index("leaf"), lax.axis_index("front")
    return leaf, front, leaf & 1


def corner_kernel(*refs, order, first, last, count, devices):
    tiles = order // TILE
    pieces = 2 * devices
    if first == 0:
        slabs, (work, out, heads, a) = refs[:pieces], refs[pieces:]
    else:
        old_work, old_out, out, work, a = refs
    fronts = out.shape[0]
    if first == 0:
        front = place()[1]

        def copy(owner, q, take):
            slot = slot_of(front ^ owner, devices)
            for s in range(devices):

                @pl.when(slot == s)
                def _():
                    take(slabs[q * devices + s])

        for q in range(fronts):
            for e in range(tiles):

                def take_tile(slab):
                    work[q, e * TILE : (e + 1) * TILE, :] = slab[:TILE, :]

                copy(e * GROUP_TILES // count, q, take_tile)

            def take_head(slab):
                heads[q] = slab[TILE:, :]

            copy(0, q, take_head)
    else:
        work[...] = old_work[...]
        out[...] = old_out[...]

    clear_rows(a)

    def step(k, carry):
        block = pl.ds(pl.multiple_of(k * TILE, TILE), TILE)
        for q in range(fronts):
            a[row_of(q), :] = work[q, block, block]
        for _ in factor_steps(a, fronts):
            pass
        kept = lax.broadcasted_iota(jnp.int32, (TILE, TILE), 0) >= lax.broadcasted_iota(jnp.int32, (TILE, TILE), 1)
        for q in range(fronts):
            out[q, block, block] = jnp.where(kept, a[row_of(q), :], 0.0)
        for fixed in range(first, last):

            @pl.when(k == fixed)
            def _():
                here = slice(fixed * TILE, (fixed + 1) * TILE)
                low, rest = slice(0, fixed * TILE), slice((fixed + 1) * TILE, order)
                for q in range(fronts):
                    corner = out[q, here, here]
                    if fixed:
                        chain = exact_dot(work[q, here, low], out[q, low, low], PLAIN)
                        out[q, here, low] = -exact_dot(corner, chain, PLAIN)
                    if fixed + 1 < tiles:
                        out[q, here, rest] = jnp.zeros((TILE, order - (fixed + 1) * TILE), jnp.float32)
                        below = exact_dot(work[q, rest, here], corner, LAST)
                        work[q, rest, here] = below
                        work[q, rest, rest] = work[q, rest, rest] - exact_dot(below, below, LAST)

        return carry

    lax.fori_loop(first, last, step, 0)


def at(tile):
    return pl.ds(pl.multiple_of(tile * TILE, TILE), TILE)


def goal_of(table, i, tile):
    entry = 3 * (tile >> 2) + (tile & 3) - 1
    return jnp.where((tile & 3) == 0, -1, table[place()[0] ^ i, jnp.maximum(entry, 0)])


def panel_of(inverse):
    turned = halves(inverse)
    cut = inverse.shape[0] // 2
    top = tuple(part[:cut, :cut] for part in turned)
    bottom = tuple(part[cut:, :] for part in turned)

    def product(block):
        full = halves(block)
        left = split_dot(tuple(part[:, :cut] for part in full), top)
        return jnp.concatenate([left, split_dot(full, bottom)], axis=1)

    return product


def add_columns(table, i, edges, panel_high, panel_low, column, *, count, skip, devices):
    front = place()[1]
    separator = panel_high.shape[2]
    first = slice((1 - skip) * TILE, (2 - skip) * TILE)
    slot = slot_of(front, devices)
    one = panel_high[slot, first, :], panel_low[slot, first, :]
    for s in range(devices):
        piece = edges[s][:, separator:] - split_dot((panel_high[s], panel_low[s]), one)
        owner = front ^ offset_of(s, devices)
        for t in range(count - skip):
            target = goal_of(table, i, owner * count + skip + t)

            @pl.when(target >= 0)
            def _():
                column[at(target), :] += piece[t * TILE : (t + 1) * TILE, :]


def own_kernel(*refs, count, skip, width, devices):
    table, heads, weights, slab, inverse, fronts_here = refs[:6]
    edges = refs[6 : 6 + devices]
    leaf_panel, column, total, panel_high, panel_low = refs[6 + devices :]
    leaf, front, half = place()
    sent = count - skip
    separator = width // GROUP_TILES
    rows = count * TILE
    first_row = (front * 2 + half) * rows

    total[...] = jnp.zeros_like(total)
    column[...] = jnp.zeros_like(column)
    row_ids = lax.broadcasted_iota(jnp.int32, (TILE, TILE), 0)
    col_ids = lax.broadcasted_iota(jnp.int32, (TILE, TILE), 1)
    near = jnp.where(jnp.abs(row_ids - col_ids) == 1, 1.0, 0.0)
    before = jnp.where((row_ids == 0) & (col_ids == TILE - 1), 1.0, 0.0)
    behind = jnp.where((row_ids == TILE - 1) & (col_ids == 0), 1.0, 0.0)
    first_weights = jnp.where(half == 0, heads[0, 0:1, :TILE], heads[1, 0:1, :TILE])
    column[:TILE, :] = jnp.where(row_ids == col_ids, first_weights + 4.0, 0.0) - near
    column[TILE : 2 * TILE, :] = -before
    inside = first_row < SEP2
    weight = jnp.transpose(jnp.broadcast_to(weights[...], (TILE, rows)))
    for j in range(count):
        mine = (front * 2 + half) * count + j
        line = slice(j * TILE, (j + 1) * TILE)
        total[line, at(mine)] = jnp.where(
            row_ids == col_ids, weight[line, :] + jnp.where(inside, 4.0, 0.0), 0.0
        ) - jnp.where(inside, near, 0.0)

        @pl.when((mine > 0) & inside)
        def _():
            total[line, at(mine - 1)] = -before

        @pl.when((mine + 1) * TILE < SEP2)
        def _():
            total[line, at(mine + 1)] = -behind

    panel_from = panel_of(inverse[0])
    if skip:
        leaf_panel[:TILE, :] = panel_from(slab[:TILE, :])
    for s in range(devices):
        panel = panel_from(edges[s][:, :separator])
        if s == 0:
            leaf_panel[skip * TILE :, :] = panel
        panel_high[s], panel_low[s] = halves(panel)
    add_columns(table, 0, edges, panel_high, panel_low, column, count=count, skip=skip, devices=devices)

    for s in range(devices):
        product = split_dot((panel_high[0], panel_low[0]), (panel_high[s], panel_low[s]))
        for c in range(sent):
            tile = (front ^ offset_of(s, devices)) * count + skip + c
            goal = jnp.maximum(goal_of(table, 0, tile), 0)
            for t in range(sent):
                target = goal_of(table, 0, front * count + skip + t) - (front * 2 + half) * count
                target = jnp.where((target >= 0) & (target < count), target, count)
                line = slice(t * TILE, (t + 1) * TILE)
                source = fronts_here[(skip + t) * TILE : (skip + t + 1) * TILE, at(tile)]
                total[at(target), at(goal)] += source - product[line, c * TILE : (c + 1) * TILE]


def parent_kernel(*refs, count, skip, width, devices):
    table, inverse, column_in, total = refs[:4]
    edges = refs[4 : 4 + devices]
    panel_out, update_out, panel_high, panel_low = refs[4 + devices : 8 + devices]
    column, two_left, two_right, update, a, done = refs[8 + devices :]
    leaf, front, half = place()
    separator = width // GROUP_TILES
    rows = count * TILE
    first_row = pl.multiple_of((front * 2 + half) * rows, TILE)

    column[...] = column_in[...]
    panel_from = panel_of(inverse[1])
    for s in range(devices):
        panel_high[s], panel_low[s] = halves(panel_from(edges[s][:, :separator]))
    add_columns(table, 1, edges, panel_high, panel_low, column, count=count, skip=skip, devices=devices)

    clear_rows(a)
    a[row_of(0), :] = column[:TILE, :]
    for _ in factor_steps(a, 1):
        pass
    row_ids = lax.broadcasted_iota(jnp.int32, (TILE, TILE), 0)
    col_ids = lax.broadcasted_iota(jnp.int32, (TILE, TILE), 1)
    turned = halves(jnp.where(row_ids >= col_ids, a[row_of(0), :], 0.0))
    for start in range(0, M2, 1024):
        block = slice(start, start + 1024)
        panel = split_dot(halves(column[block, :]), turned)
        column[block, :] = panel
        high, low = halves(panel)
        two_left[block, :] = jnp.concatenate([high, high, low], axis=1)
        two_right[block, :] = jnp.concatenate([high, low, high], axis=1)
    mine = pl.ds(first_row, rows)
    panel_out[...] = column[mine, :]
    own = two_left[mine, :]
    sends = []
    for start in range(TILE, M2, 512):
        stop = min(start + 512, M2)
        here = slice(start - TILE, stop - TILE)
        update[:, here] = total[:rows, start:stop] - plain_dot(own, two_right[start:stop, :])
        send = pltpu.make_async_copy(update.at[:, here], update_out.at[:, here], done.at[len(sends)])
        send.start()
        sends.append(send)
    for send in sends:
        send.wait()


def far_kernel(table, panel_high, panel_low, *refs, count, skip, devices, cut):
    beyond, (update, out, tiles, got, put) = refs[:2], refs[2:]
    leaf, front, half = place()
    sent = count - skip

    def each(s, t, c):
        tile = (front ^ offset_of(s, devices)) * count + skip + c
        goal = goal_of(table, 1, tile)
        target = goal_of(table, 1, front * count + skip + t) - (front * 2 + half) * count
        valid = (goal > 0) & (target >= 0) & (target < count)
        index = (s * sent + t) * sent + c
        lies = out.at[at(jnp.clip(target, 0, count - 1)), at(jnp.maximum(goal - 1, 0))]
        return tile, index, valid, lies

    def fetch(index, lies):
        return pltpu.make_async_copy(lies, tiles.at[index], got.at[index])

    def store(index, lies):
        return pltpu.make_async_copy(tiles.at[index], lies, put.at[index])

    for s in range(devices):
        for t in range(sent):
            for c in range(sent):
                _, index, valid, lies = each(s, t, c)

                @pl.when(valid)
                def _():
                    fetch(index, lies).start()

    for s in range(devices):
        product = split_dot((panel_high[0], panel_low[0]), (panel_high[s], panel_low[s]))
        for t in range(sent):
            line = slice(t * TILE, (t + 1) * TILE)
            for c in range(sent):
                tile, index, valid, lies = each(s, t, c)

                source = jnp.maximum(tile - (tile >> 2) - 2, 0)

                @pl.when(valid)
                def _():
                    fetch(index, lies).wait()
                    tiles[index] += -product[line, c * TILE : (c + 1) * TILE]

                @pl.when(valid & (source < cut))
                def _():
                    tiles[index] += beyond[0][line, at(jnp.minimum(source, cut - 1))]

                @pl.when(valid & (source >= cut))
                def _():
                    tiles[index] += beyond[1][line, at(jnp.maximum(source - cut, 0))]

                @pl.when(valid)
                def _():
                    store(index, lies).start()

    for s in range(devices):
        for t in range(sent):
            for c in range(sent):
                _, index, valid, lies = each(s, t, c)

                @pl.when(valid)
                def _():
                    store(index, lies).wait()


def slab_kernel(matrix, weights, slab, kept, done, *, chosen):
    copies = [
        pltpu.make_async_copy(
            matrix.at[:TILE, t * TILE : (t + 1) * TILE], slab.at[:TILE, k * TILE : (k + 1) * TILE], done.at[k]
        )
        for k, t in enumerate(chosen)
    ]
    for copy in copies:
        copy.start()
    slab[TILE:, :] = jnp.zeros_like(slab[TILE:, :])
    slab[TILE : TILE + 1, : weights.shape[1]] = weights[...]
    for copy in copies:
        copy.wait()
    kept[...] = slab[...]


def body_kernel(matrix, edge, *refs, skip, chosen, rest):
    parts, done = refs[:-1], refs[-1]
    copies = []
    for target, tiles in ((edge, chosen), *zip(parts, rest)):
        filled = 0
        while filled < len(tiles):
            stop = filled + 1
            while stop < len(tiles) and tiles[stop] == tiles[stop - 1] + 1:
                stop += 1
            copies.append(
                pltpu.make_async_copy(
                    matrix.at[skip * TILE :, tiles[filled] * TILE : (tiles[stop - 1] + 1) * TILE],
                    target.at[:, filled * TILE : stop * TILE],
                    done.at[len(copies)],
                )
            )
            filled = stop
    for copy in copies:
        copy.start()
    for copy in copies:
        copy.wait()


def one_front(matrix, weights, table):
    rows, width = matrix.shape
    devices = lax.axis_size("front")
    count, tiles = rows // TILE, width // TILE
    skip = 1 if count % GROUP_TILES == 0 else 0
    separator = width // GROUP_TILES
    sent = (count - skip) * TILE
    distances = []
    while 2 ** (len(distances) + 1) < devices:
        distances.insert(0, 2 ** (len(distances) + 1))

    def spread(pieces):
        for distance in distances:
            pieces = pieces + [from_front(piece, distance) for piece in pieces]
        return pieces

    vmem = pl.BlockSpec(memory_space=pltpu.VMEM)
    smem = pl.BlockSpec(memory_space=pltpu.SMEM)
    hbm = pl.BlockSpec(memory_space=pl.ANY)
    f32, bf16 = jnp.float32, jnp.bfloat16
    params = pltpu.CompilerParams(vmem_limit_bytes=VMEM_BYTES)
    small = pltpu.CompilerParams(vmem_limit_bytes=VMEM_BYTES // 3)

    corner = list(range(0, tiles, GROUP_TILES))
    rest = [t for t in range(tiles) if t % GROUP_TILES and t != 1]
    slab, kept = pl.pallas_call(
        functools.partial(slab_kernel, chosen=corner),
        out_shape=(jax.ShapeDtypeStruct((TILE + SLAB, separator), f32),) * 2,
        in_specs=[hbm, vmem],
        out_specs=(vmem, vmem),
        scratch_shapes=[pltpu.SemaphoreType.DMA((len(corner),))],
        compiler_params=params,
        cost_estimate=pl.CostEstimate(flops=0, bytes_accessed=2**19, transcendentals=0),
        name="slab",
    )(matrix, weights[None])
    far_slab = from_sibling(slab)
    slabs = spread([slab])
    cut = len(rest) * 3 // 11
    rest = (rest[:cut], rest[cut:])
    edge, *bodies = pl.pallas_call(
        functools.partial(body_kernel, skip=skip, chosen=corner + [1], rest=rest),
        out_shape=(
            jax.ShapeDtypeStruct((sent, (len(corner) + 1) * TILE), f32),
            *(jax.ShapeDtypeStruct((sent, len(part) * TILE), f32) for part in rest),
        ),
        in_specs=[hbm],
        out_specs=(vmem, vmem, vmem),
        scratch_shapes=[pltpu.SemaphoreType.DMA((2 * tiles,))],
        compiler_params=params,
        cost_estimate=pl.CostEstimate(flops=0, bytes_accessed=2**23, transcendentals=0),
        name="body",
    )(after(matrix, slab))
    far_slabs = spread([after(far_slab, edge, *slabs)])
    other_slabs = [from_front(piece, 1) for piece in slabs]
    other_far_slabs = [from_front(piece, 1) for piece in far_slabs]
    far_edge = from_sibling(after(edge, far_slab))
    far = [from_sibling(after(bodies[0], far_slab))]
    near_edges = spread([after(edge, *far_slabs)])

    state = jax.ShapeDtypeStruct((2, separator, separator), f32)
    scratch = pltpu.VMEM((SLAB * TILE, TILE), f32)
    cost = pl.CostEstimate(flops=3 * 10**9, bytes_accessed=2**22, transcendentals=0)
    middle = separator // TILE // 2
    half_kernel = functools.partial(corner_kernel, order=separator, count=count, devices=devices)
    state_one, state_two, heads = pl.pallas_call(
        functools.partial(half_kernel, first=0, last=middle),
        out_shape=(state, state, jax.ShapeDtypeStruct((2, SLAB, separator), f32)),
        in_specs=[vmem] * (2 * devices),
        out_specs=(vmem, vmem, vmem),
        scratch_shapes=[scratch],
        compiler_params=small,
        cost_estimate=cost,
        name="corner_first",
    )(kept, *slabs[1:], *other_slabs, *far_slabs, *other_far_slabs)

    far.append(from_sibling(after(bodies[1], heads)))
    far_edges = spread([after(far_edge, heads)])
    inverse = pl.pallas_call(
        functools.partial(half_kernel, first=middle, last=separator // TILE),
        out_shape=state,
        in_specs=[vmem, vmem],
        out_specs=vmem,
        scratch_shapes=[pltpu.VMEM((2, separator, separator), f32), scratch],
        compiler_params=small,
        cost_estimate=cost,
        name="corner_second",
    )(after(state_one, far_edge), state_two)
    other_edges = [from_front(after(piece, inverse), 1) for piece in near_edges]
    other_far_edges = [from_front(after(piece, inverse), 1) for piece in far_edges]

    sizes = dict(count=count, skip=skip, devices=devices)
    panel_space = pltpu.VMEM((devices, sent, separator), bf16)
    update_shape = jax.ShapeDtypeStruct((rows, M2 - TILE), f32)
    panel_shape = jax.ShapeDtypeStruct((devices, sent, separator), bf16)
    large = pltpu.CompilerParams(vmem_limit_bytes=VMEM_BYTES // 2)
    leaf_panel, column, total = pl.pallas_call(
        functools.partial(own_kernel, width=width, **sizes),
        out_shape=(
            jax.ShapeDtypeStruct((rows, separator), f32),
            jax.ShapeDtypeStruct((M2, TILE), f32),
            jax.ShapeDtypeStruct((rows + TILE, M2), f32),
        ),
        in_specs=[smem] + [vmem] * (5 + devices),
        out_specs=(vmem, vmem, vmem),
        scratch_shapes=[panel_space, panel_space],
        compiler_params=large,
        cost_estimate=pl.CostEstimate(flops=2 * 10**9, bytes_accessed=2**22, transcendentals=0),
        name="own",
    )(table, heads, weights[None], kept, after(inverse, far[0]), matrix, *near_edges, *other_edges)
    parent_panel, update, far_high, far_low = pl.pallas_call(
        functools.partial(parent_kernel, width=width, **sizes),
        out_shape=(jax.ShapeDtypeStruct((rows, TILE), f32), update_shape, panel_shape, panel_shape),
        in_specs=[smem] + [vmem] * (3 + devices),
        out_specs=(vmem, hbm, vmem, vmem),
        scratch_shapes=[
            pltpu.VMEM((M2, TILE), f32),
            pltpu.VMEM((M2, 3 * TILE), bf16),
            pltpu.VMEM((M2, 3 * TILE), bf16),
            pltpu.VMEM(update_shape.shape, f32),
            scratch,
            pltpu.SemaphoreType.DMA((M2 // 512,)),
        ],
        compiler_params=large,
        cost_estimate=pl.CostEstimate(flops=3 * 10**9, bytes_accessed=2**22, transcendentals=0),
        name="parent",
    )(table, inverse, column, total, *far_edges, *other_far_edges)
    update = pl.pallas_call(
        functools.partial(far_kernel, cut=cut, **sizes),
        out_shape=update_shape,
        in_specs=[smem] + [vmem] * 4 + [hbm],
        out_specs=hbm,
        scratch_shapes=[
            pltpu.VMEM((devices * (count - skip) ** 2, TILE, TILE), f32),
            pltpu.SemaphoreType.DMA((devices * (count - skip) ** 2,)),
            pltpu.SemaphoreType.DMA((devices * (count - skip) ** 2,)),
        ],
        input_output_aliases={5: 0},
        compiler_params=large,
        cost_estimate=pl.CostEstimate(flops=10**9, bytes_accessed=2**21, transcendentals=0),
        name="far",
    )(table, far_high, far_low, *far, update)
    return leaf_panel, parent_panel, update


def on_device(leaf_fronts, screen_weights, parent_tile_index):
    results = [
        one_front(leaf_fronts[0, g], screen_weights[0, g], parent_tile_index[:, g])
        for g in range(leaf_fronts.shape[1])
    ]
    return tuple(jnp.stack(parts)[None] for parts in zip(*results))


def solution(mesh):
    in_specs = (P("leaf", None, "front", None), P("leaf", None, "front"), P())
    out_specs = (
        P("leaf", None, "front", None),
        P("leaf", None, "front", None),
        P("leaf", None, "front", None),
    )
    return jax.shard_map(
        on_device, mesh=mesh, in_specs=in_specs, out_specs=out_specs, check_vma=False
    )
```

```python
import functools

import jax
import jax.numpy as jnp
from jax import lax
from jax.experimental import pallas as pl
from jax.experimental.pallas import tpu as pltpu
from jax.sharding import PartitionSpec as P

SEP2 = 1024
PANEL_WIDTH = 128
M2 = 4096
GROUP_TILES = 4
SLAB = 8
GROUP = 32
EXACT = lax.Precision.HIGHEST
VMEM_BYTES = 60 * 2**20

TILE = PANEL_WIDTH
LAST = ((1,), (1,))
PLAIN = ((1,), (0,))
FIRST = ((0,), (0,))


def from_front(value, distance):
    pairs = [(source, source ^ distance) for source in range(lax.axis_size("front"))]
    return lax.ppermute(value, "front", pairs)


def from_sibling(value):
    pairs = [(source, source ^ 1) for source in range(lax.axis_size("leaf"))]
    return lax.ppermute(value, "leaf", pairs)


def after(value, *events):
    return lax.optimization_barrier((value, *events))[0]


def slot_of(offset, count):
    slot, bit, weight = 0, 1, count // 2
    while weight:
        slot = slot + jnp.where((offset & bit) != 0, weight, 0)
        bit, weight = bit * 2, weight // 2
    return slot


def offset_of(slot, count):
    offset, bit, weight = 0, 1, count // 2
    while weight:
        offset += bit if slot & weight else 0
        bit, weight = bit * 2, weight // 2
    return offset


def exact_dot(left, right, contract):
    return lax.dot_general(
        left, right, (contract, ((), ())), precision=EXACT, preferred_element_type=jnp.float32
    )


def plain_dot(left, right):
    return lax.dot_general(left, right, (LAST, ((), ())), preferred_element_type=jnp.float32)


def halves(value):
    high = value.astype(jnp.bfloat16)
    return high, (value - high.astype(jnp.float32)).astype(jnp.bfloat16)


def split_dot(left, right):
    return plain_dot(left[0], right[0]) + (plain_dot(left[0], right[1]) + plain_dot(left[1], right[0]))


def lane(row, index):
    return jnp.broadcast_to(row[:, index : index + 1], row.shape)


def sum_tree(terms):
    while len(terms) > 1:
        terms = [sum(terms[i : i + 2]) for i in range(0, len(terms), 2)]
    return terms[0]


def factor_slab(rows, first, inside, lanes):
    entry = {(i, j): lane(rows[i], first + j) for i in range(SLAB) for j in range(i + 1)}
    rows = [jnp.where(inside, jnp.where(lanes == first + i, 1.0, 0.0), row) for i, row in enumerate(rows)]
    done = []
    for p in range(0, SLAB, 2):
        r = p + 1
        one, mixed, two = entry[p, p], entry[r, p], entry[r, r]
        inverse_one = pl.reciprocal(one, approx=True)
        inverse_two = pl.reciprocal(one * two - mixed * mixed, approx=True) * one
        factor = {i: entry[i, p] * inverse_one for i in range(r, SLAB)}
        rows[r] = rows[r] - factor[r] * rows[p]
        for i in range(p + 2, SLAB):
            entry[i, r] = entry[i, r] - factor[i] * mixed
        for i in range(p + 2, SLAB):
            second = entry[i, r] * inverse_two
            for k in range(p + 2, i + 1):
                entry[i, k] = (entry[i, k] - factor[i] * entry[k, p]) - second * entry[k, r]
            rows[i] = (rows[i] - factor[i] * rows[p]) - second * rows[r]
        done.append(rows[p] * lax.rsqrt(one))
        done.append(rows[r] * (inverse_two * lax.rsqrt(inverse_two)))
    return done


def row_of(q):
    return pl.ds(q, TILE, stride=SLAB)


def clear_rows(a):
    row_ids = lax.broadcasted_iota(jnp.int32, a.shape, 0) & -SLAB
    col_ids = lax.broadcasted_iota(jnp.int32, a.shape, 1) * SLAB
    a[...] = (row_ids == col_ids).astype(jnp.float32)


def factor_steps(a, fronts):
    lanes = lax.broadcasted_iota(jnp.int32, (SLAB, TILE), 1)
    columns = lax.broadcasted_iota(jnp.int32, (TILE, TILE), 1)
    settled = (lax.broadcasted_iota(jnp.int32, (GROUP, TILE), 0) & -SLAB) + SLAB

    def at(i):
        return pl.ds(SLAB * i, SLAB)

    for start in range(0, TILE, GROUP):
        stop = start + GROUP
        rows = [a[at(i), :] for i in range(start, stop)]
        for s in range(0, GROUP, SLAB):
            first = start + s
            inside = (lanes >= first) & (lanes < first + SLAB)
            head = factor_slab(rows[s : s + SLAB], first, inside, lanes)
            for i in range(SLAB):
                a[at(first + i), :] = head[i]
            for i in range(s + SLAB, GROUP):
                terms = [lane(row, start + i) * row for row in head]
                rows[i] = jnp.where(inside, 0.0, rows[i]) - sum_tree(terms)
            if s + SLAB < GROUP:
                yield
        if stop < TILE:
            for q in range(fronts):
                upper = a[pl.ds(SLAB * start + q, GROUP, stride=SLAB), :]
                rest = pl.ds(SLAB * stop + q, TILE - stop, stride=SLAB)
                inverse = jnp.where((columns[:GROUP] >= start + settled) & (columns[:GROUP] < stop), 0.0, upper)
                product = exact_dot(upper, inverse, FIRST)[stop:]
                group = columns[stop:]
                kept = jnp.where((group >= start) & (group < stop), 0.0, a[rest, :])
                a[rest, :] = kept - product
        yield


def factor_blocks(a):
    sublanes = lax.broadcasted_iota(jnp.int32, (SLAB, TILE), 0)
    lanes = lax.broadcasted_iota(jnp.int32, (SLAB, TILE), 1)
    for start in range(0, TILE, SLAB):
        inside = (lanes >= start) & (lanes < start + SLAB)
        block = a[start : start + SLAB, :]
        rows = [jnp.broadcast_to(block[i : i + 1, :], block.shape) for i in range(SLAB)]
        rows = factor_slab(rows, start, inside, lanes)
        for low in range(start + SLAB, TILE, SLAB):
            chosen = sublanes + low
            terms = [jnp.take_along_axis(row, chosen, axis=1) * row for row in rows]
            block = a[low : low + SLAB, :]
            a[low : low + SLAB, :] = jnp.where(inside, 0.0, block) - sum_tree(terms)
        block = rows[0]
        for i in range(1, SLAB):
            block = jnp.where(sublanes == i, rows[i], block)
        a[start : start + SLAB, :] = block
        yield


def place():
    leaf, front = lax.axis_index("leaf"), lax.axis_index("front")
    return leaf, front, leaf & 1


def corner_kernel(*refs, order, first, last, count, devices):
    tiles = order // TILE
    pieces = 2 * devices
    if first == 0:
        slabs, (work, out, heads, a) = refs[:pieces], refs[pieces:]
    else:
        old_work, old_out, out, work, a = refs
    fronts = out.shape[0]
    if first == 0:
        front = place()[1]

        def copy(owner, q, take):
            slot = slot_of(front ^ owner, devices)
            for s in range(devices):

                @pl.when(slot == s)
                def _():
                    take(slabs[q * devices + s])

        for q in range(fronts):
            for e in range(tiles):

                def take_tile(slab):
                    work[q, e * TILE : (e + 1) * TILE, :] = slab[:TILE, :]

                copy(e * GROUP_TILES // count, q, take_tile)

            def take_head(slab):
                heads[q] = slab[TILE:, :]

            copy(0, q, take_head)
    else:
        work[...] = old_work[...]
        out[...] = old_out[...]

    clear_rows(a)

    def step(k, carry):
        block = pl.ds(pl.multiple_of(k * TILE, TILE), TILE)
        for q in range(fronts):
            a[row_of(q), :] = work[q, block, block]
        for _ in factor_steps(a, fronts):
            pass
        kept = lax.broadcasted_iota(jnp.int32, (TILE, TILE), 0) >= lax.broadcasted_iota(jnp.int32, (TILE, TILE), 1)
        for q in range(fronts):
            out[q, block, block] = jnp.where(kept, a[row_of(q), :], 0.0)
        for fixed in range(first, last):

            @pl.when(k == fixed)
            def _():
                here = slice(fixed * TILE, (fixed + 1) * TILE)
                low, rest = slice(0, fixed * TILE), slice((fixed + 1) * TILE, order)
                for q in range(fronts):
                    corner = out[q, here, here]
                    if fixed:
                        chain = exact_dot(work[q, here, low], out[q, low, low], PLAIN)
                        out[q, here, low] = -exact_dot(corner, chain, PLAIN)
                    if fixed + 1 < tiles:
                        out[q, here, rest] = jnp.zeros((TILE, order - (fixed + 1) * TILE), jnp.float32)
                        below = exact_dot(work[q, rest, here], corner, LAST)
                        work[q, rest, here] = below
                        work[q, rest, rest] = work[q, rest, rest] - exact_dot(below, below, LAST)

        return carry

    lax.fori_loop(first, last, step, 0)


def at(tile):
    return pl.ds(pl.multiple_of(tile * TILE, TILE), TILE)


def goal_of(table, i, tile):
    entry = 3 * (tile >> 2) + (tile & 3) - 1
    return jnp.where((tile & 3) == 0, -1, table[place()[0] ^ i, jnp.maximum(entry, 0)])


def panel_of(inverse):
    turned = halves(inverse)
    cut = inverse.shape[0] // 2
    top = tuple(part[:cut, :cut] for part in turned)
    bottom = tuple(part[cut:, :] for part in turned)

    def product(block):
        full = halves(block)
        left = split_dot(tuple(part[:, :cut] for part in full), top)
        return jnp.concatenate([left, split_dot(full, bottom)], axis=1)

    return product


def add_columns(table, i, edges, panel_high, panel_low, column, *, count, skip, devices):
    front = place()[1]
    separator = panel_high.shape[2]
    first = slice((1 - skip) * TILE, (2 - skip) * TILE)
    slot = slot_of(front, devices)
    one = panel_high[slot, first, :], panel_low[slot, first, :]
    for s in range(devices):
        piece = edges[s][:, separator:] - split_dot((panel_high[s], panel_low[s]), one)
        owner = front ^ offset_of(s, devices)
        for t in range(count - skip):
            target = goal_of(table, i, owner * count + skip + t)

            @pl.when(target >= 0)
            def _():
                column[at(target), :] += piece[t * TILE : (t + 1) * TILE, :]


def own_kernel(*refs, count, skip, width, devices):
    table, heads, weights, slab, inverse, fronts_here = refs[:6]
    edges = refs[6 : 6 + devices]
    leaf_panel, column, total, panel_high, panel_low = refs[6 + devices :]
    leaf, front, half = place()
    sent = count - skip
    separator = width // GROUP_TILES
    rows = count * TILE
    first_row = (front * 2 + half) * rows

    total[...] = jnp.zeros_like(total)
    column[...] = jnp.zeros_like(column)
    row_ids = lax.broadcasted_iota(jnp.int32, (TILE, TILE), 0)
    col_ids = lax.broadcasted_iota(jnp.int32, (TILE, TILE), 1)
    near = jnp.where(jnp.abs(row_ids - col_ids) == 1, 1.0, 0.0)
    before = jnp.where((row_ids == 0) & (col_ids == TILE - 1), 1.0, 0.0)
    behind = jnp.where((row_ids == TILE - 1) & (col_ids == 0), 1.0, 0.0)
    first_weights = jnp.where(half == 0, heads[0, 0:1, :TILE], heads[1, 0:1, :TILE])
    column[:TILE, :] = jnp.where(row_ids == col_ids, first_weights + 4.0, 0.0) - near
    column[TILE : 2 * TILE, :] = -before
    inside = first_row < SEP2
    weight = jnp.transpose(jnp.broadcast_to(weights[...], (TILE, rows)))
    for j in range(count):
        mine = (front * 2 + half) * count + j
        line = slice(j * TILE, (j + 1) * TILE)
        total[line, at(mine)] = jnp.where(
            row_ids == col_ids, weight[line, :] + jnp.where(inside, 4.0, 0.0), 0.0
        ) - jnp.where(inside, near, 0.0)

        @pl.when((mine > 0) & inside)
        def _():
            total[line, at(mine - 1)] = -before

        @pl.when((mine + 1) * TILE < SEP2)
        def _():
            total[line, at(mine + 1)] = -behind

    panel_from = panel_of(inverse[0])
    if skip:
        leaf_panel[:TILE, :] = panel_from(slab[:TILE, :])
    for s in range(devices):
        panel = panel_from(edges[s][:, :separator])
        if s == 0:
            leaf_panel[skip * TILE :, :] = panel
        panel_high[s], panel_low[s] = halves(panel)
    add_columns(table, 0, edges, panel_high, panel_low, column, count=count, skip=skip, devices=devices)

    for s in range(devices):
        product = split_dot((panel_high[0], panel_low[0]), (panel_high[s], panel_low[s]))
        for c in range(sent):
            tile = (front ^ offset_of(s, devices)) * count + skip + c
            goal = jnp.maximum(goal_of(table, 0, tile), 0)
            for t in range(sent):
                target = goal_of(table, 0, front * count + skip + t) - (front * 2 + half) * count
                target = jnp.where((target >= 0) & (target < count), target, count)
                line = slice(t * TILE, (t + 1) * TILE)
                source = fronts_here[(skip + t) * TILE : (skip + t + 1) * TILE, at(tile)]
                total[at(target), at(goal)] += source - product[line, c * TILE : (c + 1) * TILE]


def parent_kernel(*refs, count, skip, width, devices):
    table, inverse, column_in, total = refs[:4]
    edges = refs[4 : 4 + devices]
    panel_out, update_out = refs[4 + devices : 6 + devices]
    panel_high, panel_low, column, two_left, two_right, update, a, done = refs[6 + devices :]
    leaf, front, half = place()
    separator = width // GROUP_TILES
    rows = count * TILE
    sent = count - skip
    first_row = pl.multiple_of((front * 2 + half) * rows, TILE)

    column[...] = column_in[...]
    panel_from = panel_of(inverse[1])
    for s in range(devices):
        panel_high[s], panel_low[s] = halves(panel_from(edges[s][:, :separator]))
    add_columns(table, 1, edges, panel_high, panel_low, column, count=count, skip=skip, devices=devices)

    def copy(j):
        line = slice(j * TILE, (j + 1) * TILE)
        update[line, :] = total[line, :]

    def contribution(s):
        product = split_dot((panel_high[0], panel_low[0]), (panel_high[s], panel_low[s]))
        for c in range(sent):
            tile = (front ^ offset_of(s, devices)) * count + skip + c
            goal = jnp.maximum(goal_of(table, 1, tile), 0)
            for t in range(sent):
                target = goal_of(table, 1, front * count + skip + t) - (front * 2 + half) * count
                target = jnp.where((target >= 0) & (target < count), target, count)
                update[at(target), at(goal)] -= product[t * TILE : (t + 1) * TILE, c * TILE : (c + 1) * TILE]

    work = [functools.partial(copy, j) for j in range(count)]
    work += [functools.partial(contribution, s) for s in range(devices)]
    steps, tasks = TILE // SLAB, len(work)
    update[rows:, :] = jnp.zeros_like(update[rows:, :])
    a[...] = column[:TILE, :]
    for k, _ in enumerate(factor_blocks(a)):
        while work and len(work) * steps >= (steps - k) * tasks:
            work.pop(0)()
    for task in work:
        task()
    row_ids = lax.broadcasted_iota(jnp.int32, (TILE, TILE), 0)
    col_ids = lax.broadcasted_iota(jnp.int32, (TILE, TILE), 1)
    turned = halves(jnp.where(row_ids >= col_ids, a[...], 0.0))
    for start in range(0, M2, 1024):
        block = slice(start, start + 1024)
        panel = split_dot(halves(column[block, :]), turned)
        column[block, :] = panel
        high, low = halves(panel)
        two_left[block, :] = jnp.concatenate([high, high, low], axis=1)
        two_right[block, :] = jnp.concatenate([high, low, high], axis=1)
    mine = pl.ds(first_row, rows)
    panel_out[...] = column[mine, :]
    own = two_left[mine, :]
    sends = []
    for start in range(TILE, M2, 512):
        stop = min(start + 512, M2)
        here = slice(start - TILE, stop - TILE)
        update[:rows, start:stop] = update[:rows, start:stop] - plain_dot(own, two_right[start:stop, :])
        send = pltpu.make_async_copy(update.at[:rows, start:stop], update_out.at[:, here], done.at[len(sends)])
        send.start()
        sends.append(send)
    for send in sends:
        send.wait()


def far_kernel(table, *refs, count, skip, devices, cut):
    beyond, (update, out, tiles, got, put) = refs[:2], refs[2:]
    leaf, front, half = place()
    sent = count - skip
    every = [(s, t, c) for s in range(devices) for t in range(sent) for c in range(sent)]

    def place_of(s, t, c):
        tile = (front ^ offset_of(s, devices)) * count + skip + c
        goal = goal_of(table, 1, tile)
        target = goal_of(table, 1, front * count + skip + t) - (front * 2 + half) * count
        valid = (goal > 0) & (target >= 0) & (target < count)
        index = (s * sent + t) * sent + c
        lies = out.at[at(jnp.clip(target, 0, count - 1)), at(jnp.maximum(goal - 1, 0))]
        return tile, index, valid, lies

    def fetch(index, lies):
        return pltpu.make_async_copy(lies, tiles.at[index], got.at[index])

    def store(index, lies):
        return pltpu.make_async_copy(tiles.at[index], lies, put.at[index])

    for s, t, c in every:
        _, index, valid, lies = place_of(s, t, c)

        @pl.when(valid)
        def _():
            fetch(index, lies).start()

    for s, t, c in every:
        tile, index, valid, lies = place_of(s, t, c)
        line = slice(t * TILE, (t + 1) * TILE)
        source = jnp.maximum(tile - (tile >> 2) - 2, 0)

        @pl.when(valid)
        def _():
            fetch(index, lies).wait()

            @pl.when(source < cut)
            def _():
                tiles[index] += beyond[0][line, at(jnp.minimum(source, cut - 1))]

            @pl.when(source >= cut)
            def _():
                tiles[index] += beyond[1][line, at(jnp.maximum(source - cut, 0))]

            store(index, lies).start()

    for s, t, c in every:
        _, index, valid, lies = place_of(s, t, c)

        @pl.when(valid)
        def _():
            store(index, lies).wait()


def slab_kernel(matrix, weights, slab, kept, done, *, chosen):
    copies = [
        pltpu.make_async_copy(
            matrix.at[:TILE, t * TILE : (t + 1) * TILE], slab.at[:TILE, k * TILE : (k + 1) * TILE], done.at[k]
        )
        for k, t in enumerate(chosen)
    ]
    for copy in copies:
        copy.start()
    slab[TILE:, :] = jnp.zeros_like(slab[TILE:, :])
    slab[TILE : TILE + 1, : weights.shape[1]] = weights[...]
    for copy in copies:
        copy.wait()
    kept[...] = slab[...]


def body_kernel(matrix, edge, *refs, skip, chosen, rest):
    parts, done = refs[:-1], refs[-1]
    copies = []
    for target, tiles in ((edge, chosen), *zip(parts, rest)):
        filled = 0
        while filled < len(tiles):
            stop = filled + 1
            while stop < len(tiles) and tiles[stop] == tiles[stop - 1] + 1:
                stop += 1
            copies.append(
                pltpu.make_async_copy(
                    matrix.at[skip * TILE :, tiles[filled] * TILE : (tiles[stop - 1] + 1) * TILE],
                    target.at[:, filled * TILE : stop * TILE],
                    done.at[len(copies)],
                )
            )
            filled = stop
    for copy in copies:
        copy.start()
    for copy in copies:
        copy.wait()


def one_front(matrix, weights, table):
    rows, width = matrix.shape
    devices = lax.axis_size("front")
    count, tiles = rows // TILE, width // TILE
    skip = 1 if count % GROUP_TILES == 0 else 0
    separator = width // GROUP_TILES
    sent = (count - skip) * TILE
    distances = []
    while 2 ** (len(distances) + 1) < devices:
        distances.insert(0, 2 ** (len(distances) + 1))

    def spread(pieces):
        for distance in distances:
            pieces = pieces + [from_front(piece, distance) for piece in pieces]
        return pieces

    vmem = pl.BlockSpec(memory_space=pltpu.VMEM)
    smem = pl.BlockSpec(memory_space=pltpu.SMEM)
    hbm = pl.BlockSpec(memory_space=pl.ANY)
    f32, bf16 = jnp.float32, jnp.bfloat16
    params = pltpu.CompilerParams(vmem_limit_bytes=VMEM_BYTES)
    small = pltpu.CompilerParams(vmem_limit_bytes=VMEM_BYTES // 3)

    corner = list(range(0, tiles, GROUP_TILES))
    rest = [t for t in range(tiles) if t % GROUP_TILES and t != 1]
    slab, kept = pl.pallas_call(
        functools.partial(slab_kernel, chosen=corner),
        out_shape=(jax.ShapeDtypeStruct((TILE + SLAB, separator), f32),) * 2,
        in_specs=[hbm, vmem],
        out_specs=(vmem, vmem),
        scratch_shapes=[pltpu.SemaphoreType.DMA((len(corner),))],
        compiler_params=params,
        cost_estimate=pl.CostEstimate(flops=0, bytes_accessed=2**19, transcendentals=0),
        name="slab",
    )(matrix, weights[None])
    far_slab = from_sibling(slab)
    slabs = spread([slab])
    cut = len(rest) * 3 // 11
    rest = (rest[:cut], rest[cut:])
    edge, *bodies = pl.pallas_call(
        functools.partial(body_kernel, skip=skip, chosen=corner + [1], rest=rest),
        out_shape=(
            jax.ShapeDtypeStruct((sent, (len(corner) + 1) * TILE), f32),
            *(jax.ShapeDtypeStruct((sent, len(part) * TILE), f32) for part in rest),
        ),
        in_specs=[hbm],
        out_specs=(vmem, vmem, vmem),
        scratch_shapes=[pltpu.SemaphoreType.DMA((2 * tiles,))],
        compiler_params=params,
        cost_estimate=pl.CostEstimate(flops=0, bytes_accessed=2**23, transcendentals=0),
        name="body",
    )(after(matrix, slab))
    far_slabs = spread([after(far_slab, edge, *slabs)])
    other_slabs = [from_front(piece, 1) for piece in slabs]
    other_far_slabs = [from_front(piece, 1) for piece in far_slabs]
    far_edge = from_sibling(after(edge, far_slab))
    far = [from_sibling(after(bodies[0], far_slab))]
    near_edges = spread([after(edge, *far_slabs)])

    state = jax.ShapeDtypeStruct((2, separator, separator), f32)
    scratch = pltpu.VMEM((SLAB * TILE, TILE), f32)
    cost = pl.CostEstimate(flops=3 * 10**9, bytes_accessed=2**22, transcendentals=0)
    middle = separator // TILE // 2
    half_kernel = functools.partial(corner_kernel, order=separator, count=count, devices=devices)
    state_one, state_two, heads = pl.pallas_call(
        functools.partial(half_kernel, first=0, last=middle),
        out_shape=(state, state, jax.ShapeDtypeStruct((2, SLAB, separator), f32)),
        in_specs=[vmem] * (2 * devices),
        out_specs=(vmem, vmem, vmem),
        scratch_shapes=[scratch],
        compiler_params=small,
        cost_estimate=cost,
        name="corner_first",
    )(kept, *slabs[1:], *other_slabs, *far_slabs, *other_far_slabs)

    far.append(from_sibling(after(bodies[1], heads)))
    far_edges = spread([after(far_edge, heads)])
    inverse = pl.pallas_call(
        functools.partial(half_kernel, first=middle, last=separator // TILE),
        out_shape=state,
        in_specs=[vmem, vmem],
        out_specs=vmem,
        scratch_shapes=[pltpu.VMEM((2, separator, separator), f32), scratch],
        compiler_params=small,
        cost_estimate=cost,
        name="corner_second",
    )(after(state_one, far_edge), state_two)
    other_edges = [from_front(after(piece, inverse), 1) for piece in near_edges]
    other_far_edges = [from_front(after(piece, inverse), 1) for piece in far_edges]

    sizes = dict(count=count, skip=skip, devices=devices)
    panel_space = pltpu.VMEM((devices, sent, separator), bf16)
    update_shape = jax.ShapeDtypeStruct((rows, M2 - TILE), f32)
    large = pltpu.CompilerParams(vmem_limit_bytes=VMEM_BYTES // 2)
    leaf_panel, column, total = pl.pallas_call(
        functools.partial(own_kernel, width=width, **sizes),
        out_shape=(
            jax.ShapeDtypeStruct((rows, separator), f32),
            jax.ShapeDtypeStruct((M2, TILE), f32),
            jax.ShapeDtypeStruct((rows + TILE, M2), f32),
        ),
        in_specs=[smem] + [vmem] * (5 + devices),
        out_specs=(vmem, vmem, vmem),
        scratch_shapes=[panel_space, panel_space],
        compiler_params=large,
        cost_estimate=pl.CostEstimate(flops=2 * 10**9, bytes_accessed=2**22, transcendentals=0),
        name="own",
    )(table, heads, weights[None], kept, inverse, matrix, *near_edges, *other_edges)
    parent_panel, update = pl.pallas_call(
        functools.partial(parent_kernel, width=width, **sizes),
        out_shape=(jax.ShapeDtypeStruct((rows, TILE), f32), update_shape),
        in_specs=[smem] + [vmem] * (3 + devices),
        out_specs=(vmem, hbm),
        scratch_shapes=[
            panel_space,
            panel_space,
            pltpu.VMEM((M2, TILE), f32),
            pltpu.VMEM((M2, 3 * TILE), bf16),
            pltpu.VMEM((M2, 3 * TILE), bf16),
            pltpu.VMEM((rows + TILE, M2), f32),
            pltpu.VMEM((TILE, TILE), f32),
            pltpu.SemaphoreType.DMA((M2 // 512,)),
        ],
        compiler_params=large,
        cost_estimate=pl.CostEstimate(flops=2 * 10**9, bytes_accessed=2**22, transcendentals=0),
        name="parent",
    )(table, inverse, column, total, *far_edges, *other_far_edges)
    update = pl.pallas_call(
        functools.partial(far_kernel, cut=cut, **sizes),
        out_shape=update_shape,
        in_specs=[smem] + [vmem] * 2 + [hbm],
        out_specs=hbm,
        scratch_shapes=[
            pltpu.VMEM((devices * (count - skip) ** 2, TILE, TILE), f32),
            pltpu.SemaphoreType.DMA((devices * (count - skip) ** 2,)),
            pltpu.SemaphoreType.DMA((devices * (count - skip) ** 2,)),
        ],
        input_output_aliases={3: 0},
        compiler_params=large,
        cost_estimate=pl.CostEstimate(flops=2 * 10**9, bytes_accessed=2**22, transcendentals=0),
        name="far",
    )(table, *far, update)
    return leaf_panel, parent_panel, update


def on_device(leaf_fronts, screen_weights, parent_tile_index):
    results = [
        one_front(leaf_fronts[0, g], screen_weights[0, g], parent_tile_index[:, g])
        for g in range(leaf_fronts.shape[1])
    ]
    return tuple(jnp.stack(parts)[None] for parts in zip(*results))


def solution(mesh):
    in_specs = (P("leaf", None, "front", None), P("leaf", None, "front"), P())
    out_specs = (
        P("leaf", None, "front", None),
        P("leaf", None, "front", None),
        P("leaf", None, "front", None),
    )
    return jax.shard_map(
        on_device, mesh=mesh, in_specs=in_specs, out_specs=out_specs, check_vma=False
    )
```

```python
import functools

import jax
import jax.numpy as jnp
from jax import lax
from jax.experimental import pallas as pl
from jax.experimental.pallas import tpu as pltpu
from jax.sharding import PartitionSpec as P

SEP2 = 1024
PANEL_WIDTH = 128
M2 = 4096
GROUP_TILES = 4
SLAB = 8
GROUP = 32
STEP = 16
EXACT = lax.Precision.HIGHEST
VMEM_BYTES = 60 * 2**20

TILE = PANEL_WIDTH
LAST = ((1,), (1,))
PLAIN = ((1,), (0,))
FIRST = ((0,), (0,))


def from_front(value, distance):
    pairs = [(source, source ^ distance) for source in range(lax.axis_size("front"))]
    return lax.ppermute(value, "front", pairs)


def from_sibling(value):
    pairs = [(source, source ^ 1) for source in range(lax.axis_size("leaf"))]
    return lax.ppermute(value, "leaf", pairs)


def after(value, *events):
    return lax.optimization_barrier((value, *events))[0]


def slot_of(offset, count):
    slot, bit, weight = 0, 1, count // 2
    while weight:
        slot = slot + jnp.where((offset & bit) != 0, weight, 0)
        bit, weight = bit * 2, weight // 2
    return slot


def offset_of(slot, count):
    offset, bit, weight = 0, 1, count // 2
    while weight:
        offset += bit if slot & weight else 0
        bit, weight = bit * 2, weight // 2
    return offset


def exact_dot(left, right, contract):
    return lax.dot_general(
        left, right, (contract, ((), ())), precision=EXACT, preferred_element_type=jnp.float32
    )


def plain_dot(left, right):
    return lax.dot_general(left, right, (LAST, ((), ())), preferred_element_type=jnp.float32)


def halves(value):
    high = value.astype(jnp.bfloat16)
    return high, (value - high.astype(jnp.float32)).astype(jnp.bfloat16)


def split_dot(left, right):
    return plain_dot(left[0], right[0]) + (plain_dot(left[0], right[1]) + plain_dot(left[1], right[0]))


def lane(row, index):
    return jnp.broadcast_to(row[:, index : index + 1], row.shape)


def sum_tree(terms):
    while len(terms) > 1:
        terms = [sum(terms[i : i + 2]) for i in range(0, len(terms), 2)]
    return terms[0]


def factor_slab(rows, first, inside, lanes):
    size = len(rows)
    entry = {(i, j): lane(rows[i], first + j) for i in range(size) for j in range(i + 1)}
    rows = [jnp.where(inside, jnp.where(lanes == first + i, 1.0, 0.0), row) for i, row in enumerate(rows)]
    done = []
    for p in range(0, size, 2):
        r = p + 1
        one, mixed, two = entry[p, p], entry[r, p], entry[r, r]
        inverse_one = pl.reciprocal(one, approx=True)
        inverse_two = pl.reciprocal(one * two - mixed * mixed, approx=True) * one
        factor = {i: entry[i, p] * inverse_one for i in range(r, size)}
        rows[r] = rows[r] - factor[r] * rows[p]
        for i in range(p + 2, size):
            entry[i, r] = entry[i, r] - factor[i] * mixed
        for i in range(p + 2, size):
            second = entry[i, r] * inverse_two
            for k in range(p + 2, i + 1):
                entry[i, k] = (entry[i, k] - factor[i] * entry[k, p]) - second * entry[k, r]
            rows[i] = (rows[i] - factor[i] * rows[p]) - second * rows[r]
        done.append(rows[p] * lax.rsqrt(one))
        done.append(rows[r] * (inverse_two * lax.rsqrt(inverse_two)))
    return done


def row_of(q):
    return pl.ds(q, TILE, stride=SLAB)


def clear_rows(a):
    row_ids = lax.broadcasted_iota(jnp.int32, a.shape, 0) & -SLAB
    col_ids = lax.broadcasted_iota(jnp.int32, a.shape, 1) * SLAB
    a[...] = (row_ids == col_ids).astype(jnp.float32)


def factor_steps(a, fronts):
    lanes = lax.broadcasted_iota(jnp.int32, (SLAB, TILE), 1)
    columns = lax.broadcasted_iota(jnp.int32, (TILE, TILE), 1)
    settled = (lax.broadcasted_iota(jnp.int32, (GROUP, TILE), 0) & -STEP) + STEP

    def at(i):
        return pl.ds(SLAB * i, SLAB)

    for start in range(0, TILE, GROUP):
        stop = start + GROUP
        rows = [a[at(i), :] for i in range(start, stop)]
        for s in range(0, GROUP, STEP):
            first = start + s
            inside = (lanes >= first) & (lanes < first + STEP)
            head = factor_slab(rows[s : s + STEP], first, inside, lanes)
            for i in range(STEP):
                a[at(first + i), :] = head[i]
            for i in range(s + STEP, GROUP):
                terms = [lane(row, start + i) * row for row in head]
                rows[i] = jnp.where(inside, 0.0, rows[i]) - sum_tree(terms)
            if s + STEP < GROUP:
                yield
        if stop < TILE:
            for q in range(fronts):
                upper = a[pl.ds(SLAB * start + q, GROUP, stride=SLAB), :]
                rest = pl.ds(SLAB * stop + q, TILE - stop, stride=SLAB)
                inverse = jnp.where((columns[:GROUP] >= start + settled) & (columns[:GROUP] < stop), 0.0, upper)
                product = exact_dot(upper, inverse, FIRST)[stop:]
                group = columns[stop:]
                kept = jnp.where((group >= start) & (group < stop), 0.0, a[rest, :])
                a[rest, :] = kept - product
        yield


def factor_blocks(a):
    sublanes = lax.broadcasted_iota(jnp.int32, (SLAB, TILE), 0)
    lanes = lax.broadcasted_iota(jnp.int32, (SLAB, TILE), 1)
    for start in range(0, TILE, SLAB):
        inside = (lanes >= start) & (lanes < start + SLAB)
        block = a[start : start + SLAB, :]
        rows = [jnp.broadcast_to(block[i : i + 1, :], block.shape) for i in range(SLAB)]
        rows = factor_slab(rows, start, inside, lanes)
        for low in range(start + SLAB, TILE, SLAB):
            chosen = sublanes + low
            terms = [jnp.take_along_axis(row, chosen, axis=1) * row for row in rows]
            block = a[low : low + SLAB, :]
            a[low : low + SLAB, :] = jnp.where(inside, 0.0, block) - sum_tree(terms)
        block = rows[0]
        for i in range(1, SLAB):
            block = jnp.where(sublanes == i, rows[i], block)
        a[start : start + SLAB, :] = block
        yield


def place():
    leaf, front = lax.axis_index("leaf"), lax.axis_index("front")
    return leaf, front, leaf & 1


def corner_kernel(*refs, order, first, last, count, devices):
    tiles = order // TILE
    pieces = 2 * devices
    if first == 0:
        slabs, (work, out, heads, a) = refs[:pieces], refs[pieces:]
    else:
        old_work, old_out, out, work, a = refs
    fronts = out.shape[0]
    if first == 0:
        front = place()[1]

        def copy(owner, q, take):
            slot = slot_of(front ^ owner, devices)
            for s in range(devices):

                @pl.when(slot == s)
                def _():
                    take(slabs[q * devices + s])

        for q in range(fronts):
            for e in range(tiles):

                def take_tile(slab):
                    work[q, e * TILE : (e + 1) * TILE, :] = slab[:TILE, :]

                copy(e * GROUP_TILES // count, q, take_tile)

            def take_head(slab):
                heads[q] = slab[TILE:, :]

            copy(0, q, take_head)
    else:
        work[...] = old_work[...]
        out[...] = old_out[...]

    clear_rows(a)

    def step(k, carry):
        block = pl.ds(pl.multiple_of(k * TILE, TILE), TILE)
        for q in range(fronts):
            a[row_of(q), :] = work[q, block, block]
        for _ in factor_steps(a, fronts):
            pass
        kept = lax.broadcasted_iota(jnp.int32, (TILE, TILE), 0) >= lax.broadcasted_iota(jnp.int32, (TILE, TILE), 1)
        for q in range(fronts):
            out[q, block, block] = jnp.where(kept, a[row_of(q), :], 0.0)
        for fixed in range(first, last):

            @pl.when(k == fixed)
            def _():
                here = slice(fixed * TILE, (fixed + 1) * TILE)
                low, rest = slice(0, fixed * TILE), slice((fixed + 1) * TILE, order)
                for q in range(fronts):
                    corner = out[q, here, here]
                    if fixed:
                        chain = exact_dot(work[q, here, low], out[q, low, low], PLAIN)
                        out[q, here, low] = -exact_dot(corner, chain, PLAIN)
                    if fixed + 1 < tiles:
                        out[q, here, rest] = jnp.zeros((TILE, order - (fixed + 1) * TILE), jnp.float32)
                        below = exact_dot(work[q, rest, here], corner, LAST)
                        work[q, rest, here] = below
                        work[q, rest, rest] = work[q, rest, rest] - exact_dot(below, below, LAST)

        return carry

    lax.fori_loop(first, last, step, 0)


def at(tile):
    return pl.ds(pl.multiple_of(tile * TILE, TILE), TILE)


def goal_of(table, i, tile):
    entry = 3 * (tile >> 2) + (tile & 3) - 1
    return jnp.where((tile & 3) == 0, -1, table[place()[0] ^ i, jnp.maximum(entry, 0)])


def panel_of(inverse):
    turned = halves(inverse)
    cut = inverse.shape[0] // 2
    top = tuple(part[:cut, :cut] for part in turned)
    bottom = tuple(part[cut:, :] for part in turned)

    def product(block):
        full = halves(block)
        left = split_dot(tuple(part[:, :cut] for part in full), top)
        return jnp.concatenate([left, split_dot(full, bottom)], axis=1)

    return product


def add_columns(table, i, edges, panel_high, panel_low, column, *, count, skip, devices):
    front = place()[1]
    separator = panel_high.shape[2]
    first = slice((1 - skip) * TILE, (2 - skip) * TILE)
    slot = slot_of(front, devices)
    one = panel_high[slot, first, :], panel_low[slot, first, :]
    for s in range(devices):
        piece = edges[s][:, separator:] - split_dot((panel_high[s], panel_low[s]), one)
        owner = front ^ offset_of(s, devices)
        for t in range(count - skip):
            target = goal_of(table, i, owner * count + skip + t)

            @pl.when(target >= 0)
            def _():
                column[at(target), :] += piece[t * TILE : (t + 1) * TILE, :]


def own_kernel(*refs, count, skip, width, devices):
    table, heads, weights, slab, inverse, fronts_here = refs[:6]
    edges = refs[6 : 6 + devices]
    leaf_panel, column, total, panel_high, panel_low = refs[6 + devices :]
    leaf, front, half = place()
    sent = count - skip
    separator = width // GROUP_TILES
    rows = count * TILE
    first_row = (front * 2 + half) * rows

    total[...] = jnp.zeros_like(total)
    column[...] = jnp.zeros_like(column)
    row_ids = lax.broadcasted_iota(jnp.int32, (TILE, TILE), 0)
    col_ids = lax.broadcasted_iota(jnp.int32, (TILE, TILE), 1)
    near = jnp.where(jnp.abs(row_ids - col_ids) == 1, 1.0, 0.0)
    before = jnp.where((row_ids == 0) & (col_ids == TILE - 1), 1.0, 0.0)
    behind = jnp.where((row_ids == TILE - 1) & (col_ids == 0), 1.0, 0.0)
    first_weights = jnp.where(half == 0, heads[0, 0:1, :TILE], heads[1, 0:1, :TILE])
    column[:TILE, :] = jnp.where(row_ids == col_ids, first_weights + 4.0, 0.0) - near
    column[TILE : 2 * TILE, :] = -before
    inside = first_row < SEP2
    weight = jnp.transpose(jnp.broadcast_to(weights[...], (TILE, rows)))
    for j in range(count):
        mine = (front * 2 + half) * count + j
        line = slice(j * TILE, (j + 1) * TILE)
        total[line, at(mine)] = jnp.where(
            row_ids == col_ids, weight[line, :] + jnp.where(inside, 4.0, 0.0), 0.0
        ) - jnp.where(inside, near, 0.0)

        @pl.when((mine > 0) & inside)
        def _():
            total[line, at(mine - 1)] = -before

        @pl.when((mine + 1) * TILE < SEP2)
        def _():
            total[line, at(mine + 1)] = -behind

    panel_from = panel_of(inverse[0])
    if skip:
        leaf_panel[:TILE, :] = panel_from(slab[:TILE, :])
    for s in range(devices):
        panel = panel_from(edges[s][:, :separator])
        if s == 0:
            leaf_panel[skip * TILE :, :] = panel
        panel_high[s], panel_low[s] = halves(panel)
    add_columns(table, 0, edges, panel_high, panel_low, column, count=count, skip=skip, devices=devices)

    for s in range(devices):
        product = split_dot((panel_high[0], panel_low[0]), (panel_high[s], panel_low[s]))
        for c in range(sent):
            tile = (front ^ offset_of(s, devices)) * count + skip + c
            goal = jnp.maximum(goal_of(table, 0, tile), 0)
            for t in range(sent):
                target = goal_of(table, 0, front * count + skip + t) - (front * 2 + half) * count
                target = jnp.where((target >= 0) & (target < count), target, count)
                line = slice(t * TILE, (t + 1) * TILE)
                source = fronts_here[(skip + t) * TILE : (skip + t + 1) * TILE, at(tile)]
                total[at(target), at(goal)] += source - product[line, c * TILE : (c + 1) * TILE]


def parent_kernel(*refs, count, skip, width, devices):
    table, inverse, column_in, total = refs[:4]
    edges = refs[4 : 4 + devices]
    panel_out, update_out = refs[4 + devices : 6 + devices]
    panel_high, panel_low, column, two_left, two_right, update, a, done = refs[6 + devices :]
    leaf, front, half = place()
    separator = width // GROUP_TILES
    rows = count * TILE
    sent = count - skip
    first_row = pl.multiple_of((front * 2 + half) * rows, TILE)

    column[...] = column_in[...]
    panel_from = panel_of(inverse[1])
    for s in range(devices):
        panel_high[s], panel_low[s] = halves(panel_from(edges[s][:, :separator]))
    add_columns(table, 1, edges, panel_high, panel_low, column, count=count, skip=skip, devices=devices)

    def copy(j):
        line = slice(j * TILE, (j + 1) * TILE)
        update[line, :] = total[line, :]

    def contribution(s):
        product = split_dot((panel_high[0], panel_low[0]), (panel_high[s], panel_low[s]))
        for c in range(sent):
            tile = (front ^ offset_of(s, devices)) * count + skip + c
            goal = jnp.maximum(goal_of(table, 1, tile), 0)
            for t in range(sent):
                target = goal_of(table, 1, front * count + skip + t) - (front * 2 + half) * count
                target = jnp.where((target >= 0) & (target < count), target, count)
                update[at(target), at(goal)] -= product[t * TILE : (t + 1) * TILE, c * TILE : (c + 1) * TILE]

    work = [functools.partial(copy, j) for j in range(count)]
    work += [functools.partial(contribution, s) for s in range(devices)]
    steps, tasks = TILE // SLAB, len(work)
    update[rows:, :] = jnp.zeros_like(update[rows:, :])
    a[...] = column[:TILE, :]
    for k, _ in enumerate(factor_blocks(a)):
        while work and len(work) * steps >= (steps - k) * tasks:
            work.pop(0)()
    for task in work:
        task()
    row_ids = lax.broadcasted_iota(jnp.int32, (TILE, TILE), 0)
    col_ids = lax.broadcasted_iota(jnp.int32, (TILE, TILE), 1)
    turned = halves(jnp.where(row_ids >= col_ids, a[...], 0.0))
    for start in range(0, M2, 1024):
        block = slice(start, start + 1024)
        panel = split_dot(halves(column[block, :]), turned)
        column[block, :] = panel
        high, low = halves(panel)
        two_left[block, :] = jnp.concatenate([high, high, low], axis=1)
        two_right[block, :] = jnp.concatenate([high, low, high], axis=1)
    mine = pl.ds(first_row, rows)
    panel_out[...] = column[mine, :]
    own = two_left[mine, :]
    sends = []
    for start in range(TILE, M2, 512):
        stop = min(start + 512, M2)
        here = slice(start - TILE, stop - TILE)
        update[:rows, start:stop] = update[:rows, start:stop] - plain_dot(own, two_right[start:stop, :])
        send = pltpu.make_async_copy(update.at[:rows, start:stop], update_out.at[:, here], done.at[len(sends)])
        send.start()
        sends.append(send)
    for send in sends:
        send.wait()


def far_kernel(table, *refs, count, skip, devices, cuts):
    beyond, (update, out, tiles, got, put) = refs[: len(cuts) - 1], refs[len(cuts) - 1 :]
    leaf, front, half = place()
    sent = count - skip
    every = [(s, t, c) for s in range(devices) for t in range(sent) for c in range(sent)]

    def place_of(s, t, c):
        tile = (front ^ offset_of(s, devices)) * count + skip + c
        goal = goal_of(table, 1, tile)
        target = goal_of(table, 1, front * count + skip + t) - (front * 2 + half) * count
        valid = (goal > 0) & (target >= 0) & (target < count)
        index = (s * sent + t) * sent + c
        lies = out.at[at(jnp.clip(target, 0, count - 1)), at(jnp.maximum(goal - 1, 0))]
        return tile, index, valid, lies

    def fetch(index, lies):
        return pltpu.make_async_copy(lies, tiles.at[index], got.at[index])

    def store(index, lies):
        return pltpu.make_async_copy(tiles.at[index], lies, put.at[index])

    for s, t, c in every:
        _, index, valid, lies = place_of(s, t, c)

        @pl.when(valid)
        def _():
            fetch(index, lies).start()

    for s, t, c in every:
        tile, index, valid, lies = place_of(s, t, c)
        line = slice(t * TILE, (t + 1) * TILE)
        source = jnp.maximum(tile - (tile >> 2) - 2, 0)

        @pl.when(valid)
        def _():
            fetch(index, lies).wait()

            for part, low, high in zip(beyond, cuts, cuts[1:]):

                @pl.when((source >= low) & (source < high))
                def _():
                    tiles[index] += part[line, at(jnp.clip(source - low, 0, high - low - 1))]

            store(index, lies).start()

    for s, t, c in every:
        _, index, valid, lies = place_of(s, t, c)

        @pl.when(valid)
        def _():
            store(index, lies).wait()


def slab_kernel(matrix, weights, slab, kept, done, *, chosen):
    copies = [
        pltpu.make_async_copy(
            matrix.at[:TILE, t * TILE : (t + 1) * TILE], slab.at[:TILE, k * TILE : (k + 1) * TILE], done.at[k]
        )
        for k, t in enumerate(chosen)
    ]
    for copy in copies:
        copy.start()
    slab[TILE:, :] = jnp.zeros_like(slab[TILE:, :])
    slab[TILE : TILE + 1, : weights.shape[1]] = weights[...]
    for copy in copies:
        copy.wait()
    kept[...] = slab[...]


def body_kernel(matrix, edge, *refs, skip, chosen, rest):
    parts, done = refs[:-1], refs[-1]
    copies = []
    for target, tiles in ((edge, chosen), *zip(parts, rest)):
        filled = 0
        while filled < len(tiles):
            stop = filled + 1
            while stop < len(tiles) and tiles[stop] == tiles[stop - 1] + 1:
                stop += 1
            copies.append(
                pltpu.make_async_copy(
                    matrix.at[skip * TILE :, tiles[filled] * TILE : (tiles[stop - 1] + 1) * TILE],
                    target.at[:, filled * TILE : stop * TILE],
                    done.at[len(copies)],
                )
            )
            filled = stop
    for copy in copies:
        copy.start()
    for copy in copies:
        copy.wait()


def one_front(matrix, weights, table):
    rows, width = matrix.shape
    devices = lax.axis_size("front")
    count, tiles = rows // TILE, width // TILE
    skip = 1 if count % GROUP_TILES == 0 else 0
    separator = width // GROUP_TILES
    sent = (count - skip) * TILE
    distances = []
    while 2 ** (len(distances) + 1) < devices:
        distances.insert(0, 2 ** (len(distances) + 1))

    def spread(pieces):
        for distance in distances:
            pieces = pieces + [from_front(piece, distance) for piece in pieces]
        return pieces

    vmem = pl.BlockSpec(memory_space=pltpu.VMEM)
    smem = pl.BlockSpec(memory_space=pltpu.SMEM)
    hbm = pl.BlockSpec(memory_space=pl.ANY)
    f32, bf16 = jnp.float32, jnp.bfloat16
    params = pltpu.CompilerParams(vmem_limit_bytes=VMEM_BYTES)
    small = pltpu.CompilerParams(vmem_limit_bytes=VMEM_BYTES // 3)

    corner = list(range(0, tiles, GROUP_TILES))
    rest = [t for t in range(tiles) if t % GROUP_TILES and t != 1]
    slab, kept = pl.pallas_call(
        functools.partial(slab_kernel, chosen=corner),
        out_shape=(jax.ShapeDtypeStruct((TILE + SLAB, separator), f32),) * 2,
        in_specs=[hbm, vmem],
        out_specs=(vmem, vmem),
        scratch_shapes=[pltpu.SemaphoreType.DMA((len(corner),))],
        compiler_params=params,
        cost_estimate=pl.CostEstimate(flops=0, bytes_accessed=2**19, transcendentals=0),
        name="slab",
    )(matrix, weights[None])
    far_slab = from_sibling(slab)
    slabs = spread([slab])
    cuts = (0, 1 + len(rest) // 2, len(rest))
    rest = [rest[low:high] for low, high in zip(cuts, cuts[1:])]
    edge, *bodies = pl.pallas_call(
        functools.partial(body_kernel, skip=skip, chosen=corner + [1], rest=rest),
        out_shape=(
            jax.ShapeDtypeStruct((sent, (len(corner) + 1) * TILE), f32),
            *(jax.ShapeDtypeStruct((sent, len(part) * TILE), f32) for part in rest),
        ),
        in_specs=[hbm],
        out_specs=(vmem,) * (1 + len(rest)),
        scratch_shapes=[pltpu.SemaphoreType.DMA((2 * tiles,))],
        compiler_params=params,
        cost_estimate=pl.CostEstimate(flops=0, bytes_accessed=2**23, transcendentals=0),
        name="body",
    )(after(matrix, slab))
    far_slabs = spread([after(far_slab, edge, *slabs)])
    other_slabs = [from_front(piece, 1) for piece in slabs]
    other_far_slabs = [from_front(piece, 1) for piece in far_slabs]
    far_edge = from_sibling(after(edge, far_slab))
    near_edges = spread([after(edge, *far_slabs)])

    state = jax.ShapeDtypeStruct((2, separator, separator), f32)
    scratch = pltpu.VMEM((SLAB * TILE, TILE), f32)
    cost = pl.CostEstimate(flops=3 * 10**9, bytes_accessed=2**22, transcendentals=0)
    middle = separator // TILE // 2
    half_kernel = functools.partial(corner_kernel, order=separator, count=count, devices=devices)
    state_one, state_two, heads = pl.pallas_call(
        functools.partial(half_kernel, first=0, last=middle),
        out_shape=(state, state, jax.ShapeDtypeStruct((2, SLAB, separator), f32)),
        in_specs=[vmem] * (2 * devices),
        out_specs=(vmem, vmem, vmem),
        scratch_shapes=[scratch],
        compiler_params=small,
        cost_estimate=cost,
        name="corner_first",
    )(kept, *slabs[1:], *other_slabs, *far_slabs, *other_far_slabs)

    far = [from_sibling(after(body, heads)) for body in bodies]
    far_edges = spread([after(far_edge, heads)])
    inverse = pl.pallas_call(
        functools.partial(half_kernel, first=middle, last=separator // TILE),
        out_shape=state,
        in_specs=[vmem, vmem],
        out_specs=vmem,
        scratch_shapes=[pltpu.VMEM((2, separator, separator), f32), scratch],
        compiler_params=small,
        cost_estimate=cost,
        name="corner_second",
    )(after(state_one, far_edge), state_two)
    other_edges = [from_front(after(piece, inverse), 1) for piece in near_edges]
    other_far_edges = [from_front(after(piece, inverse), 1) for piece in far_edges]

    sizes = dict(count=count, skip=skip, devices=devices)
    panel_space = pltpu.VMEM((devices, sent, separator), bf16)
    update_shape = jax.ShapeDtypeStruct((rows, M2 - TILE), f32)
    large = pltpu.CompilerParams(vmem_limit_bytes=VMEM_BYTES // 2)
    leaf_panel, column, total = pl.pallas_call(
        functools.partial(own_kernel, width=width, **sizes),
        out_shape=(
            jax.ShapeDtypeStruct((rows, separator), f32),
            jax.ShapeDtypeStruct((M2, TILE), f32),
            jax.ShapeDtypeStruct((rows + TILE, M2), f32),
        ),
        in_specs=[smem] + [vmem] * (5 + devices),
        out_specs=(vmem, vmem, vmem),
        scratch_shapes=[panel_space, panel_space],
        compiler_params=large,
        cost_estimate=pl.CostEstimate(flops=2 * 10**9, bytes_accessed=2**22, transcendentals=0),
        name="own",
    )(table, heads, weights[None], kept, after(inverse, far[0]), matrix, *near_edges, *other_edges)
    parent_panel, update = pl.pallas_call(
        functools.partial(parent_kernel, width=width, **sizes),
        out_shape=(jax.ShapeDtypeStruct((rows, TILE), f32), update_shape),
        in_specs=[smem] + [vmem] * (3 + devices),
        out_specs=(vmem, hbm),
        scratch_shapes=[
            panel_space,
            panel_space,
            pltpu.VMEM((M2, TILE), f32),
            pltpu.VMEM((M2, 3 * TILE), bf16),
            pltpu.VMEM((M2, 3 * TILE), bf16),
            pltpu.VMEM((rows + TILE, M2), f32),
            pltpu.VMEM((TILE, TILE), f32),
            pltpu.SemaphoreType.DMA((M2 // 512,)),
        ],
        compiler_params=large,
        cost_estimate=pl.CostEstimate(flops=2 * 10**9, bytes_accessed=2**22, transcendentals=0),
        name="parent",
    )(table, inverse, column, total, *far_edges, *other_far_edges)
    update = pl.pallas_call(
        functools.partial(far_kernel, cuts=cuts, **sizes),
        out_shape=update_shape,
        in_specs=[smem] + [vmem] * len(far) + [hbm],
        out_specs=hbm,
        scratch_shapes=[
            pltpu.VMEM((devices * (count - skip) ** 2, TILE, TILE), f32),
            pltpu.SemaphoreType.DMA((devices * (count - skip) ** 2,)),
            pltpu.SemaphoreType.DMA((devices * (count - skip) ** 2,)),
        ],
        input_output_aliases={1 + len(far): 0},
        compiler_params=large,
        cost_estimate=pl.CostEstimate(flops=2 * 10**9, bytes_accessed=2**22, transcendentals=0),
        name="far",
    )(table, *far, update)
    return leaf_panel, parent_panel, update


def on_device(leaf_fronts, screen_weights, parent_tile_index):
    results = [
        one_front(leaf_fronts[0, g], screen_weights[0, g], parent_tile_index[:, g])
        for g in range(leaf_fronts.shape[1])
    ]
    return tuple(jnp.stack(parts)[None] for parts in zip(*results))


def solution(mesh):
    in_specs = (P("leaf", None, "front", None), P("leaf", None, "front"), P())
    out_specs = (
        P("leaf", None, "front", None),
        P("leaf", None, "front", None),
        P("leaf", None, "front", None),
    )
    return jax.shard_map(
        on_device, mesh=mesh, in_specs=in_specs, out_specs=out_specs, check_vma=False
    )
```

```python
import functools

import jax
import jax.numpy as jnp
from jax import lax
from jax.experimental import pallas as pl
from jax.experimental.pallas import tpu as pltpu
from jax.sharding import PartitionSpec as P

SEP2 = 1024
PANEL_WIDTH = 128
M2 = 4096
GROUP_TILES = 4
SLAB = 8
GROUP = 32
STEP = 16
VMEM_BYTES = 60 * 2**20

TILE = PANEL_WIDTH
LAST = ((1,), (1,))
PLAIN = ((1,), (0,))
FIRST = ((0,), (0,))


def from_front(value, distance):
    pairs = [(source, source ^ distance) for source in range(lax.axis_size("front"))]
    return lax.ppermute(value, "front", pairs)


def from_sibling(value):
    pairs = [(source, source ^ 1) for source in range(lax.axis_size("leaf"))]
    return lax.ppermute(value, "leaf", pairs)


def after(value, *events):
    return lax.optimization_barrier((value, *events))[0]


def slot_of(offset, count):
    slot, bit, weight = 0, 1, count // 2
    while weight:
        slot = slot + jnp.where((offset & bit) != 0, weight, 0)
        bit, weight = bit * 2, weight // 2
    return slot


def offset_of(slot, count):
    offset, bit, weight = 0, 1, count // 2
    while weight:
        offset += bit if slot & weight else 0
        bit, weight = bit * 2, weight // 2
    return offset


def exact_dot(left, right, contract):
    def parts(value):
        high = value.astype(jnp.bfloat16)
        value = value - high.astype(jnp.float32)
        middle = value.astype(jnp.bfloat16)
        return high, middle, (value - middle.astype(jnp.float32)).astype(jnp.bfloat16)

    left, right = parts(left), parts(right)
    left = jnp.concatenate([left[k] for k in (0, 0, 1, 0, 1, 2)], axis=contract[0][0])
    right = jnp.concatenate([right[k] for k in (0, 1, 0, 2, 1, 0)], axis=contract[1][0])
    return lax.dot_general(left, right, (contract, ((), ())), preferred_element_type=jnp.float32)


def plain_dot(left, right):
    return lax.dot_general(left, right, (LAST, ((), ())), preferred_element_type=jnp.float32)


def halves(value):
    high = value.astype(jnp.bfloat16)
    return high, (value - high.astype(jnp.float32)).astype(jnp.bfloat16)


def split_dot(left, right):
    return plain_dot(left[0], right[0]) + (plain_dot(left[0], right[1]) + plain_dot(left[1], right[0]))


def lane(row, index):
    return jnp.broadcast_to(row[:, index : index + 1], row.shape)


def sum_tree(terms):
    while len(terms) > 1:
        terms = [sum(terms[i : i + 2]) for i in range(0, len(terms), 2)]
    return terms[0]


def factor_slab(rows, first, inside, lanes):
    size = len(rows)
    entry = {(i, j): lane(rows[i], first + j) for i in range(size) for j in range(i + 1)}
    rows = [jnp.where(inside, jnp.where(lanes == first + i, 1.0, 0.0), row) for i, row in enumerate(rows)]
    done = []
    for p in range(0, size, 2):
        r = p + 1
        one, mixed, two = entry[p, p], entry[r, p], entry[r, r]
        inverse_one = pl.reciprocal(one, approx=True)
        inverse_two = pl.reciprocal(one * two - mixed * mixed, approx=True) * one
        factor = {i: entry[i, p] * inverse_one for i in range(r, size)}
        rows[r] = rows[r] - factor[r] * rows[p]
        for i in range(p + 2, size):
            entry[i, r] = entry[i, r] - factor[i] * mixed
        for i in range(p + 2, size):
            second = entry[i, r] * inverse_two
            for k in range(p + 2, i + 1):
                entry[i, k] = (entry[i, k] - factor[i] * entry[k, p]) - second * entry[k, r]
            rows[i] = (rows[i] - factor[i] * rows[p]) - second * rows[r]
        done.append(rows[p] * lax.rsqrt(one))
        done.append(rows[r] * (inverse_two * lax.rsqrt(inverse_two)))
    return done


def row_of(q):
    return pl.ds(q, TILE, stride=SLAB)


def clear_rows(a):
    row_ids = lax.broadcasted_iota(jnp.int32, a.shape, 0) & -SLAB
    col_ids = lax.broadcasted_iota(jnp.int32, a.shape, 1) * SLAB
    a[...] = (row_ids == col_ids).astype(jnp.float32)


def factor_steps(a, fronts):
    lanes = lax.broadcasted_iota(jnp.int32, (SLAB, TILE), 1)
    columns = lax.broadcasted_iota(jnp.int32, (TILE, TILE), 1)
    settled = (lax.broadcasted_iota(jnp.int32, (GROUP, TILE), 0) & -STEP) + STEP

    def at(i):
        return pl.ds(SLAB * i, SLAB)

    for start in range(0, TILE, GROUP):
        stop = start + GROUP
        rows = [a[at(i), :] for i in range(start, stop)]
        for s in range(0, GROUP, STEP):
            first = start + s
            inside = (lanes >= first) & (lanes < first + STEP)
            head = factor_slab(rows[s : s + STEP], first, inside, lanes)
            for i in range(STEP):
                a[at(first + i), :] = head[i]
            for i in range(s + STEP, GROUP):
                terms = [lane(row, start + i) * row for row in head]
                rows[i] = jnp.where(inside, 0.0, rows[i]) - sum_tree(terms)
            if s + STEP < GROUP:
                yield
        if stop < TILE:
            for q in range(fronts):
                upper = a[pl.ds(SLAB * start + q, GROUP, stride=SLAB), :]
                rest = pl.ds(SLAB * stop + q, TILE - stop, stride=SLAB)
                inverse = jnp.where((columns[:GROUP] >= start + settled) & (columns[:GROUP] < stop), 0.0, upper)
                product = exact_dot(upper, inverse, FIRST)[stop:]
                group = columns[stop:]
                kept = jnp.where((group >= start) & (group < stop), 0.0, a[rest, :])
                a[rest, :] = kept - product
        yield


def factor_blocks(a):
    sublanes = lax.broadcasted_iota(jnp.int32, (SLAB, TILE), 0)
    lanes = lax.broadcasted_iota(jnp.int32, (SLAB, TILE), 1)
    for start in range(0, TILE, SLAB):
        inside = (lanes >= start) & (lanes < start + SLAB)
        block = a[start : start + SLAB, :]
        rows = [jnp.broadcast_to(block[i : i + 1, :], block.shape) for i in range(SLAB)]
        rows = factor_slab(rows, start, inside, lanes)
        for low in range(start + SLAB, TILE, SLAB):
            chosen = sublanes + low
            terms = [jnp.take_along_axis(row, chosen, axis=1) * row for row in rows]
            block = a[low : low + SLAB, :]
            a[low : low + SLAB, :] = jnp.where(inside, 0.0, block) - sum_tree(terms)
        block = rows[0]
        for i in range(1, SLAB):
            block = jnp.where(sublanes == i, rows[i], block)
        a[start : start + SLAB, :] = block
        yield


def place():
    leaf, front = lax.axis_index("leaf"), lax.axis_index("front")
    return leaf, front, leaf & 1


def corner_kernel(*refs, order, first, last, count, devices):
    tiles = order // TILE
    pieces = 2 * devices
    if first == 0:
        slabs, (work, out, heads, a) = refs[:pieces], refs[pieces:]
    else:
        old_work, old_out, out, work, a = refs
    fronts = out.shape[0]
    if first == 0:
        front = place()[1]

        def copy(owner, q, take):
            slot = slot_of(front ^ owner, devices)
            for s in range(devices):

                @pl.when(slot == s)
                def _():
                    take(slabs[q * devices + s])

        for q in range(fronts):
            for e in range(tiles):

                def take_tile(slab):
                    work[q, e * TILE : (e + 1) * TILE, :] = slab[:TILE, :]

                copy(e * GROUP_TILES // count, q, take_tile)

            def take_head(slab):
                heads[q] = slab[TILE:, :]

            copy(0, q, take_head)
    else:
        work[...] = old_work[...]
        out[...] = old_out[...]

    clear_rows(a)

    def step(k, carry):
        block = pl.ds(pl.multiple_of(k * TILE, TILE), TILE)
        for q in range(fronts):
            a[row_of(q), :] = work[q, block, block]
        for _ in factor_steps(a, fronts):
            pass
        kept = lax.broadcasted_iota(jnp.int32, (TILE, TILE), 0) >= lax.broadcasted_iota(jnp.int32, (TILE, TILE), 1)
        for q in range(fronts):
            out[q, block, block] = jnp.where(kept, a[row_of(q), :], 0.0)
        for fixed in range(first, last):

            @pl.when(k == fixed)
            def _():
                here = slice(fixed * TILE, (fixed + 1) * TILE)
                low, rest = slice(0, fixed * TILE), slice((fixed + 1) * TILE, order)
                for q in range(fronts):
                    corner = out[q, here, here]
                    if fixed:
                        chain = exact_dot(work[q, here, low], out[q, low, low], PLAIN)
                        out[q, here, low] = -exact_dot(corner, chain, PLAIN)
                    if fixed + 1 < tiles:
                        out[q, here, rest] = jnp.zeros((TILE, order - (fixed + 1) * TILE), jnp.float32)
                        below = exact_dot(work[q, rest, here], corner, LAST)
                        work[q, rest, here] = below
                        work[q, rest, rest] = work[q, rest, rest] - exact_dot(below, below, LAST)

        return carry

    lax.fori_loop(first, last, step, 0)


def at(tile):
    return pl.ds(pl.multiple_of(tile * TILE, TILE), TILE)


def goal_of(table, i, tile):
    entry = 3 * (tile >> 2) + (tile & 3) - 1
    return jnp.where((tile & 3) == 0, -1, table[place()[0] ^ i, jnp.maximum(entry, 0)])


def panel_of(inverse):
    turned = halves(inverse)
    cut = inverse.shape[0] // 2
    top = tuple(part[:cut, :cut] for part in turned)
    bottom = tuple(part[cut:, :] for part in turned)

    def product(block):
        full = halves(block)
        left = split_dot(tuple(part[:, :cut] for part in full), top)
        return jnp.concatenate([left, split_dot(full, bottom)], axis=1)

    return product


def add_columns(table, i, edges, panel_high, panel_low, column, *, count, skip, devices):
    front = place()[1]
    separator = panel_high.shape[2]
    first = slice((1 - skip) * TILE, (2 - skip) * TILE)
    slot = slot_of(front, devices)
    one = panel_high[slot, first, :], panel_low[slot, first, :]
    for s in range(devices):
        piece = edges[s][:, separator:] - split_dot((panel_high[s], panel_low[s]), one)
        owner = front ^ offset_of(s, devices)
        for t in range(count - skip):
            target = goal_of(table, i, owner * count + skip + t)

            @pl.when(target >= 0)
            def _():
                column[at(target), :] += piece[t * TILE : (t + 1) * TILE, :]


def own_kernel(*refs, count, skip, width, devices):
    table, heads, weights, slab, inverse, fronts_here = refs[:6]
    edges = refs[6 : 6 + devices]
    leaf_panel, column, total, panel_high, panel_low = refs[6 + devices :]
    leaf, front, half = place()
    sent = count - skip
    separator = width // GROUP_TILES
    rows = count * TILE
    first_row = (front * 2 + half) * rows

    total[...] = jnp.zeros_like(total)
    column[...] = jnp.zeros_like(column)
    row_ids = lax.broadcasted_iota(jnp.int32, (TILE, TILE), 0)
    col_ids = lax.broadcasted_iota(jnp.int32, (TILE, TILE), 1)
    near = jnp.where(jnp.abs(row_ids - col_ids) == 1, 1.0, 0.0)
    before = jnp.where((row_ids == 0) & (col_ids == TILE - 1), 1.0, 0.0)
    behind = jnp.where((row_ids == TILE - 1) & (col_ids == 0), 1.0, 0.0)
    first_weights = jnp.where(half == 0, heads[0, 0:1, :TILE], heads[1, 0:1, :TILE])
    column[:TILE, :] = jnp.where(row_ids == col_ids, first_weights + 4.0, 0.0) - near
    column[TILE : 2 * TILE, :] = -before
    inside = first_row < SEP2
    weight = jnp.transpose(jnp.broadcast_to(weights[...], (TILE, rows)))
    for j in range(count):
        mine = (front * 2 + half) * count + j
        line = slice(j * TILE, (j + 1) * TILE)
        total[line, at(mine)] = jnp.where(
            row_ids == col_ids, weight[line, :] + jnp.where(inside, 4.0, 0.0), 0.0
        ) - jnp.where(inside, near, 0.0)

        @pl.when((mine > 0) & inside)
        def _():
            total[line, at(mine - 1)] = -before

        @pl.when((mine + 1) * TILE < SEP2)
        def _():
            total[line, at(mine + 1)] = -behind

    panel_from = panel_of(inverse[0])
    if skip:
        leaf_panel[:TILE, :] = panel_from(slab[:TILE, :])
    for s in range(devices):
        panel = panel_from(edges[s][:, :separator])
        if s == 0:
            leaf_panel[skip * TILE :, :] = panel
        panel_high[s], panel_low[s] = halves(panel)
    add_columns(table, 0, edges, panel_high, panel_low, column, count=count, skip=skip, devices=devices)

    for s in range(devices):
        product = split_dot((panel_high[0], panel_low[0]), (panel_high[s], panel_low[s]))
        for c in range(sent):
            tile = (front ^ offset_of(s, devices)) * count + skip + c
            goal = jnp.maximum(goal_of(table, 0, tile), 0)
            for t in range(sent):
                target = goal_of(table, 0, front * count + skip + t) - (front * 2 + half) * count
                target = jnp.where((target >= 0) & (target < count), target, count)
                line = slice(t * TILE, (t + 1) * TILE)
                source = fronts_here[(skip + t) * TILE : (skip + t + 1) * TILE, at(tile)]
                total[at(target), at(goal)] += source - product[line, c * TILE : (c + 1) * TILE]


def parent_kernel(*refs, count, skip, width, devices):
    table, inverse, column_in, total = refs[:4]
    edges = refs[4 : 4 + devices]
    panel_out, update_out = refs[4 + devices : 6 + devices]
    panel_high, panel_low, column, two_left, two_right, update, a, done = refs[6 + devices :]
    leaf, front, half = place()
    separator = width // GROUP_TILES
    rows = count * TILE
    sent = count - skip
    first_row = pl.multiple_of((front * 2 + half) * rows, TILE)

    column[...] = column_in[...]
    panel_from = panel_of(inverse[1])
    for s in range(devices):
        panel_high[s], panel_low[s] = halves(panel_from(edges[s][:, :separator]))
    add_columns(table, 1, edges, panel_high, panel_low, column, count=count, skip=skip, devices=devices)

    def copy(j):
        line = slice(j * TILE, (j + 1) * TILE)
        update[line, :] = total[line, :]

    def contribution(s):
        product = split_dot((panel_high[0], panel_low[0]), (panel_high[s], panel_low[s]))
        for c in range(sent):
            tile = (front ^ offset_of(s, devices)) * count + skip + c
            goal = jnp.maximum(goal_of(table, 1, tile), 0)
            for t in range(sent):
                target = goal_of(table, 1, front * count + skip + t) - (front * 2 + half) * count
                target = jnp.where((target >= 0) & (target < count), target, count)
                update[at(target), at(goal)] -= product[t * TILE : (t + 1) * TILE, c * TILE : (c + 1) * TILE]

    work = [functools.partial(copy, j) for j in range(count)]
    work += [functools.partial(contribution, s) for s in range(devices)]
    steps, tasks = TILE // SLAB, len(work)
    update[rows:, :] = jnp.zeros_like(update[rows:, :])
    a[...] = column[:TILE, :]
    for k, _ in enumerate(factor_blocks(a)):
        while work and len(work) * steps >= (steps - k) * tasks:
            work.pop(0)()
    for task in work:
        task()
    row_ids = lax.broadcasted_iota(jnp.int32, (TILE, TILE), 0)
    col_ids = lax.broadcasted_iota(jnp.int32, (TILE, TILE), 1)
    turned = halves(jnp.where(row_ids >= col_ids, a[...], 0.0))
    for start in range(0, M2, 1024):
        block = slice(start, start + 1024)
        panel = split_dot(halves(column[block, :]), turned)
        column[block, :] = panel
        high, low = halves(panel)
        two_left[block, :] = jnp.concatenate([high, high, low], axis=1)
        two_right[block, :] = jnp.concatenate([high, low, high], axis=1)
    mine = pl.ds(first_row, rows)
    panel_out[...] = column[mine, :]
    own = two_left[mine, :]
    sends = []
    for start in range(TILE, M2, 512):
        stop = min(start + 512, M2)
        here = slice(start - TILE, stop - TILE)
        update[:rows, start:stop] = update[:rows, start:stop] - plain_dot(own, two_right[start:stop, :])
        send = pltpu.make_async_copy(update.at[:rows, start:stop], update_out.at[:, here], done.at[len(sends)])
        send.start()
        sends.append(send)
    for send in sends:
        send.wait()


def far_kernel(table, *refs, count, skip, devices, cuts):
    beyond, (update, out, tiles, got, put) = refs[: len(cuts) - 1], refs[len(cuts) - 1 :]
    leaf, front, half = place()
    sent = count - skip
    every = [(s, t, c) for s in range(devices) for t in range(sent) for c in range(sent)]

    def place_of(s, t, c):
        tile = (front ^ offset_of(s, devices)) * count + skip + c
        goal = goal_of(table, 1, tile)
        target = goal_of(table, 1, front * count + skip + t) - (front * 2 + half) * count
        valid = (goal > 0) & (target >= 0) & (target < count)
        index = (s * sent + t) * sent + c
        lies = out.at[at(jnp.clip(target, 0, count - 1)), at(jnp.maximum(goal - 1, 0))]
        return tile, index, valid, lies

    def fetch(index, lies):
        return pltpu.make_async_copy(lies, tiles.at[index], got.at[index])

    def store(index, lies):
        return pltpu.make_async_copy(tiles.at[index], lies, put.at[index])

    for s, t, c in every:
        _, index, valid, lies = place_of(s, t, c)

        @pl.when(valid)
        def _():
            fetch(index, lies).start()

    for s, t, c in every:
        tile, index, valid, lies = place_of(s, t, c)
        line = slice(t * TILE, (t + 1) * TILE)
        source = jnp.maximum(tile - (tile >> 2) - 2, 0)

        @pl.when(valid)
        def _():
            fetch(index, lies).wait()

            for part, low, high in zip(beyond, cuts, cuts[1:]):

                @pl.when((source >= low) & (source < high))
                def _():
                    tiles[index] += part[line, at(jnp.clip(source - low, 0, high - low - 1))]

            store(index, lies).start()

    for s, t, c in every:
        _, index, valid, lies = place_of(s, t, c)

        @pl.when(valid)
        def _():
            store(index, lies).wait()


def slab_kernel(matrix, weights, slab, kept, done, *, chosen):
    copies = [
        pltpu.make_async_copy(
            matrix.at[:TILE, t * TILE : (t + 1) * TILE], slab.at[:TILE, k * TILE : (k + 1) * TILE], done.at[k]
        )
        for k, t in enumerate(chosen)
    ]
    for copy in copies:
        copy.start()
    slab[TILE:, :] = jnp.zeros_like(slab[TILE:, :])
    slab[TILE : TILE + 1, : weights.shape[1]] = weights[...]
    for copy in copies:
        copy.wait()
    kept[...] = slab[...]


def body_kernel(matrix, *refs, skip, wanted):
    targets, done = refs[:-1], refs[-1]
    copies = []
    for target, tiles in zip(targets, wanted):
        filled = 0
        while filled < len(tiles):
            stop = filled + 1
            while stop < len(tiles) and tiles[stop] == tiles[stop - 1] + 1:
                stop += 1
            copies.append(
                pltpu.make_async_copy(
                    matrix.at[skip * TILE :, tiles[filled] * TILE : (tiles[stop - 1] + 1) * TILE],
                    target.at[:, filled * TILE : stop * TILE],
                    done.at[len(copies)],
                )
            )
            filled = stop
    for copy in copies:
        copy.start()
    for copy in copies:
        copy.wait()


def one_front(matrix, weights, table):
    rows, width = matrix.shape
    devices = lax.axis_size("front")
    count, tiles = rows // TILE, width // TILE
    skip = 1 if count % GROUP_TILES == 0 else 0
    separator = width // GROUP_TILES
    sent = (count - skip) * TILE
    distances = []
    while 2 ** (len(distances) + 1) < devices:
        distances.insert(0, 2 ** (len(distances) + 1))

    def spread(pieces):
        for distance in distances:
            pieces = pieces + [from_front(piece, distance) for piece in pieces]
        return pieces

    vmem = pl.BlockSpec(memory_space=pltpu.VMEM)
    smem = pl.BlockSpec(memory_space=pltpu.SMEM)
    hbm = pl.BlockSpec(memory_space=pl.ANY)
    f32, bf16 = jnp.float32, jnp.bfloat16
    params = pltpu.CompilerParams(vmem_limit_bytes=VMEM_BYTES)
    small = pltpu.CompilerParams(vmem_limit_bytes=VMEM_BYTES // 3)

    corner = list(range(0, tiles, GROUP_TILES))
    rest = [t for t in range(tiles) if t % GROUP_TILES and t != 1]
    slab, kept = pl.pallas_call(
        functools.partial(slab_kernel, chosen=corner),
        out_shape=(jax.ShapeDtypeStruct((TILE + SLAB, separator), f32),) * 2,
        in_specs=[hbm, vmem],
        out_specs=(vmem, vmem),
        scratch_shapes=[pltpu.SemaphoreType.DMA((len(corner),))],
        compiler_params=params,
        cost_estimate=pl.CostEstimate(flops=0, bytes_accessed=2**19, transcendentals=0),
        name="slab",
    )(matrix, weights[None])
    far_slab = from_sibling(slab)
    slabs = spread([slab])
    cuts = (0, 3, 5, 7, len(rest))
    rest = [rest[low:high] for low, high in zip(cuts, cuts[1:])]
    chosen = corner + [1]
    wanted = [chosen, chosen + rest[0], *rest[1:]]
    edge, wide, *bodies = pl.pallas_call(
        functools.partial(body_kernel, skip=skip, wanted=wanted),
        out_shape=tuple(jax.ShapeDtypeStruct((sent, len(part) * TILE), f32) for part in wanted),
        in_specs=[hbm],
        out_specs=(vmem,) * len(wanted),
        scratch_shapes=[pltpu.SemaphoreType.DMA((4 * tiles,))],
        compiler_params=params,
        cost_estimate=pl.CostEstimate(flops=0, bytes_accessed=2**23, transcendentals=0),
        name="body",
    )(after(matrix, slab))
    far_slabs = spread([after(far_slab, edge, *slabs)])
    other_slabs = [from_front(piece, 1) for piece in slabs]
    other_far_slabs = [from_front(piece, 1) for piece in far_slabs]
    far_wide = from_sibling(after(wide, far_slab))
    far_edge = far_wide[:, : len(chosen) * TILE]
    near_edges = spread([after(edge, *far_slabs)])

    state = jax.ShapeDtypeStruct((2, separator, separator), f32)
    scratch = pltpu.VMEM((SLAB * TILE, TILE), f32)
    cost = pl.CostEstimate(flops=3 * 10**9, bytes_accessed=2**22, transcendentals=0)
    middle = separator // TILE - 1
    half_kernel = functools.partial(corner_kernel, order=separator, count=count, devices=devices)
    state_one, state_two, heads = pl.pallas_call(
        functools.partial(half_kernel, first=0, last=middle),
        out_shape=(state, state, jax.ShapeDtypeStruct((2, SLAB, separator), f32)),
        in_specs=[vmem] * (2 * devices),
        out_specs=(vmem, vmem, vmem),
        scratch_shapes=[scratch],
        compiler_params=small,
        cost_estimate=cost,
        name="corner_first",
    )(kept, *slabs[1:], *other_slabs, *far_slabs, *other_far_slabs)

    other_edges = [from_front(after(piece, heads), 1) for piece in near_edges]
    far = [far_wide[:, len(chosen) * TILE :]]
    far += [from_sibling(after(body, heads)) for body in bodies]
    far_edges = spread([after(far_edge, heads)])
    inverse = pl.pallas_call(
        functools.partial(half_kernel, first=middle, last=separator // TILE),
        out_shape=state,
        in_specs=[vmem, vmem],
        out_specs=vmem,
        scratch_shapes=[pltpu.VMEM((2, separator, separator), f32), scratch],
        compiler_params=small,
        cost_estimate=cost,
        name="corner_second",
    )(after(state_one, far_edge, *other_edges), state_two)

    sizes = dict(count=count, skip=skip, devices=devices)
    panel_space = pltpu.VMEM((devices, sent, separator), bf16)
    update_shape = jax.ShapeDtypeStruct((rows, M2 - TILE), f32)
    large = pltpu.CompilerParams(vmem_limit_bytes=VMEM_BYTES // 2)
    leaf_panel, column, total = pl.pallas_call(
        functools.partial(own_kernel, width=width, **sizes),
        out_shape=(
            jax.ShapeDtypeStruct((rows, separator), f32),
            jax.ShapeDtypeStruct((M2, TILE), f32),
            jax.ShapeDtypeStruct((rows + TILE, M2), f32),
        ),
        in_specs=[smem] + [vmem] * (5 + devices),
        out_specs=(vmem, vmem, vmem),
        scratch_shapes=[panel_space, panel_space],
        compiler_params=large,
        cost_estimate=pl.CostEstimate(flops=2 * 10**9, bytes_accessed=2**22, transcendentals=0),
        name="own",
    )(table, heads, weights[None], kept, after(inverse, far[1]), matrix, *near_edges, *other_edges)
    other_far_edges = [from_front(after(piece, column, far[2]), 1) for piece in far_edges]
    parent_panel, update = pl.pallas_call(
        functools.partial(parent_kernel, width=width, **sizes),
        out_shape=(jax.ShapeDtypeStruct((rows, TILE), f32), update_shape),
        in_specs=[smem] + [vmem] * (3 + devices),
        out_specs=(vmem, hbm),
        scratch_shapes=[
            panel_space,
            panel_space,
            pltpu.VMEM((M2, TILE), f32),
            pltpu.VMEM((M2, 3 * TILE), bf16),
            pltpu.VMEM((M2, 3 * TILE), bf16),
            pltpu.VMEM((rows + TILE, M2), f32),
            pltpu.VMEM((TILE, TILE), f32),
            pltpu.SemaphoreType.DMA((M2 // 512,)),
        ],
        compiler_params=large,
        cost_estimate=pl.CostEstimate(flops=2 * 10**9, bytes_accessed=2**22, transcendentals=0),
        name="parent",
    )(table, inverse, column, total, *far_edges, *other_far_edges)
    update = pl.pallas_call(
        functools.partial(far_kernel, cuts=cuts, **sizes),
        out_shape=update_shape,
        in_specs=[smem] + [vmem] * len(far) + [hbm],
        out_specs=hbm,
        scratch_shapes=[
            pltpu.VMEM((devices * (count - skip) ** 2, TILE, TILE), f32),
            pltpu.SemaphoreType.DMA((devices * (count - skip) ** 2,)),
            pltpu.SemaphoreType.DMA((devices * (count - skip) ** 2,)),
        ],
        input_output_aliases={1 + len(far): 0},
        compiler_params=large,
        cost_estimate=pl.CostEstimate(flops=2 * 10**9, bytes_accessed=2**22, transcendentals=0),
        name="far",
    )(table, *far, update)
    return leaf_panel, parent_panel, update


def on_device(leaf_fronts, screen_weights, parent_tile_index):
    results = [
        one_front(leaf_fronts[0, g], screen_weights[0, g], parent_tile_index[:, g])
        for g in range(leaf_fronts.shape[1])
    ]
    return tuple(jnp.stack(parts)[None] for parts in zip(*results))


def solution(mesh):
    in_specs = (P("leaf", None, "front", None), P("leaf", None, "front"), P())
    out_specs = (
        P("leaf", None, "front", None),
        P("leaf", None, "front", None),
        P("leaf", None, "front", None),
    )
    return jax.shard_map(
        on_device, mesh=mesh, in_specs=in_specs, out_specs=out_specs, check_vma=False
    )
```

```python
import functools

import jax
import jax.numpy as jnp
from jax import lax
from jax.experimental import pallas as pl
from jax.experimental.pallas import tpu as pltpu
from jax.sharding import PartitionSpec as P

SEP2 = 1024
PANEL_WIDTH = 128
M2 = 4096
GROUP_TILES = 4
SLAB = 8
GROUP = 32
STEP = 16
VMEM_BYTES = 60 * 2**20

TILE = PANEL_WIDTH
LAST = ((1,), (1,))
PLAIN = ((1,), (0,))
FIRST = ((0,), (0,))


def from_front(value, distance):
    pairs = [(source, source ^ distance) for source in range(lax.axis_size("front"))]
    return lax.ppermute(value, "front", pairs)


def from_sibling(value):
    pairs = [(source, source ^ 1) for source in range(lax.axis_size("leaf"))]
    return lax.ppermute(value, "leaf", pairs)


def after(value, *events):
    return lax.optimization_barrier((value, *events))[0]


def slot_of(offset, count):
    slot, bit, weight = 0, 1, count // 2
    while weight:
        slot = slot + jnp.where((offset & bit) != 0, weight, 0)
        bit, weight = bit * 2, weight // 2
    return slot


def offset_of(slot, count):
    offset, bit, weight = 0, 1, count // 2
    while weight:
        offset += bit if slot & weight else 0
        bit, weight = bit * 2, weight // 2
    return offset


def exact_dot(left, right, contract):
    def parts(value):
        high = value.astype(jnp.bfloat16)
        value = value - high.astype(jnp.float32)
        middle = value.astype(jnp.bfloat16)
        return high, middle, (value - middle.astype(jnp.float32)).astype(jnp.bfloat16)

    left, right = parts(left), parts(right)
    left = jnp.concatenate([left[k] for k in (0, 0, 1, 0, 1, 2)], axis=contract[0][0])
    right = jnp.concatenate([right[k] for k in (0, 1, 0, 2, 1, 0)], axis=contract[1][0])
    return lax.dot_general(left, right, (contract, ((), ())), preferred_element_type=jnp.float32)


def plain_dot(left, right):
    return lax.dot_general(left, right, (LAST, ((), ())), preferred_element_type=jnp.float32)


def halves(value):
    high = value.astype(jnp.bfloat16)
    return high, (value - high.astype(jnp.float32)).astype(jnp.bfloat16)


def split_dot(left, right):
    return plain_dot(left[0], right[0]) + (plain_dot(left[0], right[1]) + plain_dot(left[1], right[0]))


def lane(row, index):
    return jnp.broadcast_to(row[:, index : index + 1], row.shape)


def sum_tree(terms):
    while len(terms) > 1:
        terms = [sum(terms[i : i + 2]) for i in range(0, len(terms), 2)]
    return terms[0]


def factor_slab(rows, first, inside, lanes):
    size = len(rows)
    entry = {(i, j): lane(rows[i], first + j) for i in range(size) for j in range(i + 1)}
    rows = [jnp.where(inside, jnp.where(lanes == first + i, 1.0, 0.0), row) for i, row in enumerate(rows)]
    done = []
    for p in range(0, size, 2):
        r = p + 1
        one, mixed, two = entry[p, p], entry[r, p], entry[r, r]
        inverse_one = pl.reciprocal(one, approx=True)
        inverse_two = pl.reciprocal(one * two - mixed * mixed, approx=True) * one
        factor = {i: entry[i, p] * inverse_one for i in range(r, size)}
        rows[r] = rows[r] - factor[r] * rows[p]
        for i in range(p + 2, size):
            entry[i, r] = entry[i, r] - factor[i] * mixed
        for i in range(p + 2, size):
            second = entry[i, r] * inverse_two
            for k in range(p + 2, i + 1):
                entry[i, k] = (entry[i, k] - factor[i] * entry[k, p]) - second * entry[k, r]
            rows[i] = (rows[i] - factor[i] * rows[p]) - second * rows[r]
        done.append(rows[p] * lax.rsqrt(one))
        done.append(rows[r] * (inverse_two * lax.rsqrt(inverse_two)))
    return done


def row_of(q):
    return pl.ds(q, TILE, stride=SLAB)


def clear_rows(a):
    row_ids = lax.broadcasted_iota(jnp.int32, a.shape, 0) & -SLAB
    col_ids = lax.broadcasted_iota(jnp.int32, a.shape, 1) * SLAB
    a[...] = (row_ids == col_ids).astype(jnp.float32)


def factor_steps(a, fronts):
    lanes = lax.broadcasted_iota(jnp.int32, (SLAB, TILE), 1)
    columns = lax.broadcasted_iota(jnp.int32, (TILE, TILE), 1)
    settled = (lax.broadcasted_iota(jnp.int32, (GROUP, TILE), 0) & -STEP) + STEP

    def at(i):
        return pl.ds(SLAB * i, SLAB)

    for start in range(0, TILE, GROUP):
        stop = start + GROUP
        rows = [a[at(i), :] for i in range(start, stop)]
        for s in range(0, GROUP, STEP):
            first = start + s
            inside = (lanes >= first) & (lanes < first + STEP)
            head = factor_slab(rows[s : s + STEP], first, inside, lanes)
            for i in range(STEP):
                a[at(first + i), :] = head[i]
            for i in range(s + STEP, GROUP):
                terms = [lane(row, start + i) * row for row in head]
                rows[i] = jnp.where(inside, 0.0, rows[i]) - sum_tree(terms)
            if s + STEP < GROUP:
                yield
        if stop < TILE:
            for q in range(fronts):
                upper = a[pl.ds(SLAB * start + q, GROUP, stride=SLAB), :]
                rest = pl.ds(SLAB * stop + q, TILE - stop, stride=SLAB)
                inverse = jnp.where((columns[:GROUP] >= start + settled) & (columns[:GROUP] < stop), 0.0, upper)
                product = exact_dot(upper, inverse, FIRST)[stop:]
                group = columns[stop:]
                kept = jnp.where((group >= start) & (group < stop), 0.0, a[rest, :])
                a[rest, :] = kept - product
        yield


def factor_blocks(a):
    sublanes = lax.broadcasted_iota(jnp.int32, (SLAB, TILE), 0)
    lanes = lax.broadcasted_iota(jnp.int32, (SLAB, TILE), 1)
    for start in range(0, TILE, SLAB):
        inside = (lanes >= start) & (lanes < start + SLAB)
        block = a[start : start + SLAB, :]
        rows = [jnp.broadcast_to(block[i : i + 1, :], block.shape) for i in range(SLAB)]
        rows = factor_slab(rows, start, inside, lanes)
        for low in range(start + SLAB, TILE, SLAB):
            chosen = sublanes + low
            terms = [jnp.take_along_axis(row, chosen, axis=1) * row for row in rows]
            block = a[low : low + SLAB, :]
            a[low : low + SLAB, :] = jnp.where(inside, 0.0, block) - sum_tree(terms)
        block = rows[0]
        for i in range(1, SLAB):
            block = jnp.where(sublanes == i, rows[i], block)
        a[start : start + SLAB, :] = block
        yield


def place():
    leaf, front = lax.axis_index("leaf"), lax.axis_index("front")
    return leaf, front, leaf & 1


def corner_kernel(*refs, order, first, last, count, devices):
    tiles = order // TILE
    pieces = 2 * devices
    if first == 0:
        slabs, (work, out, heads, a) = refs[:pieces], refs[pieces:]
    else:
        old_work, old_out, out, work, a = refs
    fronts = out.shape[0]
    if first == 0:
        front = place()[1]

        def copy(owner, q, take):
            slot = slot_of(front ^ owner, devices)
            for s in range(devices):

                @pl.when(slot == s)
                def _():
                    take(slabs[q * devices + s])

        for q in range(fronts):
            for e in range(tiles):

                def take_tile(slab):
                    work[q, e * TILE : (e + 1) * TILE, :] = slab[:TILE, :]

                copy(e * GROUP_TILES // count, q, take_tile)

            def take_head(slab):
                heads[q] = slab[TILE:, :]

            copy(0, q, take_head)
    else:
        work[...] = old_work[...]
        out[...] = old_out[...]

    clear_rows(a)

    def step(k, carry):
        block = pl.ds(pl.multiple_of(k * TILE, TILE), TILE)
        for q in range(fronts):
            a[row_of(q), :] = work[q, block, block]
        for _ in factor_steps(a, fronts):
            pass
        kept = lax.broadcasted_iota(jnp.int32, (TILE, TILE), 0) >= lax.broadcasted_iota(jnp.int32, (TILE, TILE), 1)
        for q in range(fronts):
            out[q, block, block] = jnp.where(kept, a[row_of(q), :], 0.0)
        for fixed in range(first, last):

            @pl.when(k == fixed)
            def _():
                here = slice(fixed * TILE, (fixed + 1) * TILE)
                low, rest = slice(0, fixed * TILE), slice((fixed + 1) * TILE, order)
                for q in range(fronts):
                    corner = out[q, here, here]
                    if fixed:
                        chain = exact_dot(work[q, here, low], out[q, low, low], PLAIN)
                        out[q, here, low] = -exact_dot(corner, chain, PLAIN)
                    if fixed + 1 < tiles:
                        out[q, here, rest] = jnp.zeros((TILE, order - (fixed + 1) * TILE), jnp.float32)
                        below = exact_dot(work[q, rest, here], corner, LAST)
                        work[q, rest, here] = below
                        work[q, rest, rest] = work[q, rest, rest] - exact_dot(below, below, LAST)

        return carry

    lax.fori_loop(first, last, step, 0)


def at(tile):
    return pl.ds(pl.multiple_of(tile * TILE, TILE), TILE)


def goal_of(table, i, tile):
    entry = 3 * (tile >> 2) + (tile & 3) - 1
    return jnp.where((tile & 3) == 0, -1, table[place()[0] ^ i, jnp.maximum(entry, 0)])


def panel_of(inverse):
    turned = halves(inverse)
    cut = inverse.shape[0] // 2
    top = tuple(part[:cut, :cut] for part in turned)
    bottom = tuple(part[cut:, :] for part in turned)

    def product(block):
        full = halves(block)
        left = split_dot(tuple(part[:, :cut] for part in full), top)
        return jnp.concatenate([left, split_dot(full, bottom)], axis=1)

    return product


def add_columns(table, i, edges, panel_high, panel_low, column, *, count, skip, devices):
    front = place()[1]
    separator = panel_high.shape[2]
    first = slice((1 - skip) * TILE, (2 - skip) * TILE)
    slot = slot_of(front, devices)
    one = panel_high[slot, first, :], panel_low[slot, first, :]
    for s in range(devices):
        piece = edges[s][:, separator:] - split_dot((panel_high[s], panel_low[s]), one)
        owner = front ^ offset_of(s, devices)
        for t in range(count - skip):
            target = goal_of(table, i, owner * count + skip + t)

            @pl.when(target >= 0)
            def _():
                column[at(target), :] += piece[t * TILE : (t + 1) * TILE, :]


def own_kernel(*refs, count, skip, width, devices):
    table, heads, weights, slab, inverse, fronts_here = refs[:6]
    edges = refs[6 : 6 + devices]
    leaf_panel, column, total, panel_high, panel_low = refs[6 + devices :]
    leaf, front, half = place()
    sent = count - skip
    separator = width // GROUP_TILES
    rows = count * TILE
    first_row = (front * 2 + half) * rows

    total[...] = jnp.zeros_like(total)
    column[...] = jnp.zeros_like(column)
    row_ids = lax.broadcasted_iota(jnp.int32, (TILE, TILE), 0)
    col_ids = lax.broadcasted_iota(jnp.int32, (TILE, TILE), 1)
    near = jnp.where(jnp.abs(row_ids - col_ids) == 1, 1.0, 0.0)
    before = jnp.where((row_ids == 0) & (col_ids == TILE - 1), 1.0, 0.0)
    behind = jnp.where((row_ids == TILE - 1) & (col_ids == 0), 1.0, 0.0)
    first_weights = jnp.where(half == 0, heads[0, 0:1, :TILE], heads[1, 0:1, :TILE])
    column[:TILE, :] = jnp.where(row_ids == col_ids, first_weights + 4.0, 0.0) - near
    column[TILE : 2 * TILE, :] = -before
    inside = first_row < SEP2
    weight = jnp.transpose(jnp.broadcast_to(weights[...], (TILE, rows)))
    for j in range(count):
        mine = (front * 2 + half) * count + j
        line = slice(j * TILE, (j + 1) * TILE)
        total[line, at(mine)] = jnp.where(
            row_ids == col_ids, weight[line, :] + jnp.where(inside, 4.0, 0.0), 0.0
        ) - jnp.where(inside, near, 0.0)

        @pl.when((mine > 0) & inside)
        def _():
            total[line, at(mine - 1)] = -before

        @pl.when((mine + 1) * TILE < SEP2)
        def _():
            total[line, at(mine + 1)] = -behind

    panel_from = panel_of(inverse[0])
    if skip:
        leaf_panel[:TILE, :] = panel_from(slab[:TILE, :])
    for s in range(devices):
        panel = panel_from(edges[s][:, :separator])
        if s == 0:
            leaf_panel[skip * TILE :, :] = panel
        panel_high[s], panel_low[s] = halves(panel)
    add_columns(table, 0, edges, panel_high, panel_low, column, count=count, skip=skip, devices=devices)

    for s in range(devices):
        product = split_dot((panel_high[0], panel_low[0]), (panel_high[s], panel_low[s]))
        for c in range(sent):
            tile = (front ^ offset_of(s, devices)) * count + skip + c
            goal = jnp.maximum(goal_of(table, 0, tile), 0)
            for t in range(sent):
                target = goal_of(table, 0, front * count + skip + t) - (front * 2 + half) * count
                target = jnp.where((target >= 0) & (target < count), target, count)
                line = slice(t * TILE, (t + 1) * TILE)
                source = fronts_here[(skip + t) * TILE : (skip + t + 1) * TILE, at(tile)]
                total[at(target), at(goal)] += source - product[line, c * TILE : (c + 1) * TILE]


def parent_kernel(*refs, count, skip, width, devices):
    table, inverse, column_in, total = refs[:4]
    edges = refs[4 : 4 + devices]
    panel_out, update_out = refs[4 + devices : 6 + devices]
    panel_high, panel_low, column, two_left, two_right, update, a, done = refs[6 + devices :]
    leaf, front, half = place()
    separator = width // GROUP_TILES
    rows = count * TILE
    sent = count - skip
    first_row = pl.multiple_of((front * 2 + half) * rows, TILE)

    column[...] = column_in[...]
    panel_from = panel_of(inverse[1])
    for s in range(devices):
        panel_high[s], panel_low[s] = halves(panel_from(edges[s][:, :separator]))
    add_columns(table, 1, edges, panel_high, panel_low, column, count=count, skip=skip, devices=devices)

    def copy(j):
        line = slice(j * TILE, (j + 1) * TILE)
        update[line, :] = total[line, :]

    def contribution(s):
        product = split_dot((panel_high[0], panel_low[0]), (panel_high[s], panel_low[s]))
        for c in range(sent):
            tile = (front ^ offset_of(s, devices)) * count + skip + c
            goal = jnp.maximum(goal_of(table, 1, tile), 0)
            for t in range(sent):
                target = goal_of(table, 1, front * count + skip + t) - (front * 2 + half) * count
                target = jnp.where((target >= 0) & (target < count), target, count)
                update[at(target), at(goal)] -= product[t * TILE : (t + 1) * TILE, c * TILE : (c + 1) * TILE]

    work = [functools.partial(copy, j) for j in range(count)]
    work += [functools.partial(contribution, s) for s in range(devices)]
    steps, tasks = TILE // SLAB, len(work)
    update[rows:, :] = jnp.zeros_like(update[rows:, :])
    a[...] = column[:TILE, :]
    for k, _ in enumerate(factor_blocks(a)):
        while work and len(work) * steps >= (steps - k) * tasks:
            work.pop(0)()
    for task in work:
        task()
    row_ids = lax.broadcasted_iota(jnp.int32, (TILE, TILE), 0)
    col_ids = lax.broadcasted_iota(jnp.int32, (TILE, TILE), 1)
    turned = halves(jnp.where(row_ids >= col_ids, a[...], 0.0))
    for start in range(0, M2, 1024):
        block = slice(start, start + 1024)
        panel = split_dot(halves(column[block, :]), turned)
        column[block, :] = panel
        high, low = halves(panel)
        two_left[block, :] = jnp.concatenate([high, high, low], axis=1)
        two_right[block, :] = jnp.concatenate([high, low, high], axis=1)
    mine = pl.ds(first_row, rows)
    panel_out[...] = column[mine, :]
    own = two_left[mine, :]
    sends = []
    for start in range(TILE, M2, 512):
        stop = min(start + 512, M2)
        here = slice(start - TILE, stop - TILE)
        update[:rows, start:stop] = update[:rows, start:stop] - plain_dot(own, two_right[start:stop, :])
        send = pltpu.make_async_copy(update.at[:rows, start:stop], update_out.at[:, here], done.at[len(sends)])
        send.start()
        sends.append(send)
    for send in sends:
        send.wait()


def far_kernel(table, *refs, count, skip, devices, cuts):
    beyond, (update, out, tiles, got, put) = refs[: len(cuts) - 1], refs[len(cuts) - 1 :]
    leaf, front, half = place()
    sent = count - skip
    every = [(s, t, c) for s in range(devices) for t in range(sent) for c in range(sent)]

    def place_of(s, t, c):
        tile = (front ^ offset_of(s, devices)) * count + skip + c
        goal = goal_of(table, 1, tile)
        target = goal_of(table, 1, front * count + skip + t) - (front * 2 + half) * count
        valid = (goal > 0) & (target >= 0) & (target < count)
        index = (s * sent + t) * sent + c
        lies = out.at[at(jnp.clip(target, 0, count - 1)), at(jnp.maximum(goal - 1, 0))]
        return tile, index, valid, lies

    def fetch(index, lies):
        return pltpu.make_async_copy(lies, tiles.at[index], got.at[index])

    def store(index, lies):
        return pltpu.make_async_copy(tiles.at[index], lies, put.at[index])

    for s, t, c in every:
        _, index, valid, lies = place_of(s, t, c)

        @pl.when(valid)
        def _():
            fetch(index, lies).start()

    for s, t, c in every:
        tile, index, valid, lies = place_of(s, t, c)
        line = slice(t * TILE, (t + 1) * TILE)
        source = jnp.maximum(tile - (tile >> 2) - 2, 0)

        @pl.when(valid)
        def _():
            fetch(index, lies).wait()

            for part, low, high in zip(beyond, cuts, cuts[1:]):

                @pl.when((source >= low) & (source < high))
                def _():
                    tiles[index] += part[line, at(jnp.clip(source - low, 0, high - low - 1))]

            store(index, lies).start()

    for s, t, c in every:
        _, index, valid, lies = place_of(s, t, c)

        @pl.when(valid)
        def _():
            store(index, lies).wait()


def slab_kernel(matrix, weights, slab, kept, done, *, chosen):
    copies = [
        pltpu.make_async_copy(
            matrix.at[:TILE, t * TILE : (t + 1) * TILE], slab.at[:TILE, k * TILE : (k + 1) * TILE], done.at[k]
        )
        for k, t in enumerate(chosen)
    ]
    for copy in copies:
        copy.start()
    slab[TILE:, :] = jnp.zeros_like(slab[TILE:, :])
    slab[TILE : TILE + 1, : weights.shape[1]] = weights[...]
    for copy in copies:
        copy.wait()
    kept[...] = slab[...]


def body_kernel(matrix, *refs, skip, wanted):
    targets, done = refs[:-1], refs[-1]
    copies = []
    for target, tiles in zip(targets, wanted):
        filled = 0
        while filled < len(tiles):
            stop = filled + 1
            while stop < len(tiles) and tiles[stop] == tiles[stop - 1] + 1:
                stop += 1
            copies.append(
                pltpu.make_async_copy(
                    matrix.at[skip * TILE :, tiles[filled] * TILE : (tiles[stop - 1] + 1) * TILE],
                    target.at[:, filled * TILE : stop * TILE],
                    done.at[len(copies)],
                )
            )
            filled = stop
    for copy in copies:
        copy.start()
    for copy in copies:
        copy.wait()


def one_front(matrix, weights, table):
    rows, width = matrix.shape
    devices = lax.axis_size("front")
    count, tiles = rows // TILE, width // TILE
    skip = 1 if count % GROUP_TILES == 0 else 0
    separator = width // GROUP_TILES
    sent = (count - skip) * TILE
    distances = []
    while 2 ** (len(distances) + 1) < devices:
        distances.insert(0, 2 ** (len(distances) + 1))

    def spread(pieces):
        for distance in distances:
            pieces = pieces + [from_front(piece, distance) for piece in pieces]
        return pieces

    vmem = pl.BlockSpec(memory_space=pltpu.VMEM)
    smem = pl.BlockSpec(memory_space=pltpu.SMEM)
    hbm = pl.BlockSpec(memory_space=pl.ANY)
    f32, bf16 = jnp.float32, jnp.bfloat16
    params = pltpu.CompilerParams(vmem_limit_bytes=VMEM_BYTES)
    small = pltpu.CompilerParams(vmem_limit_bytes=VMEM_BYTES // 3)

    corner = list(range(0, tiles, GROUP_TILES))
    rest = [t for t in range(tiles) if t % GROUP_TILES and t != 1]
    slab, kept = pl.pallas_call(
        functools.partial(slab_kernel, chosen=corner),
        out_shape=(jax.ShapeDtypeStruct((TILE + SLAB, separator), f32),) * 2,
        in_specs=[hbm, vmem],
        out_specs=(vmem, vmem),
        scratch_shapes=[pltpu.SemaphoreType.DMA((len(corner),))],
        compiler_params=params,
        cost_estimate=pl.CostEstimate(flops=0, bytes_accessed=2**19, transcendentals=0),
        name="slab",
    )(matrix, weights[None])
    far_slab = from_sibling(slab)
    slabs = spread([slab])
    cuts = (0, 2, 7, len(rest))
    rest = [rest[low:high] for low, high in zip(cuts, cuts[1:])]
    chosen = corner + [1]
    wanted = [chosen, chosen + rest[0], *rest[1:]]
    edge, wide, *bodies = pl.pallas_call(
        functools.partial(body_kernel, skip=skip, wanted=wanted),
        out_shape=tuple(jax.ShapeDtypeStruct((sent, len(part) * TILE), f32) for part in wanted),
        in_specs=[hbm],
        out_specs=(vmem,) * len(wanted),
        scratch_shapes=[pltpu.SemaphoreType.DMA((4 * tiles,))],
        compiler_params=params,
        cost_estimate=pl.CostEstimate(flops=0, bytes_accessed=2**23, transcendentals=0),
        name="body",
    )(after(matrix, slab))
    far_slabs = spread([after(far_slab, edge, *slabs)])
    other_slabs = [from_front(piece, 1) for piece in slabs]
    other_far_slabs = [from_front(piece, 1) for piece in far_slabs]
    far_wide = from_sibling(after(wide, far_slab))
    far_edge = far_wide[:, : len(chosen) * TILE]
    near_edges = spread([after(edge, *far_slabs)])

    state = jax.ShapeDtypeStruct((2, separator, separator), f32)
    scratch = pltpu.VMEM((SLAB * TILE, TILE), f32)
    cost = pl.CostEstimate(flops=3 * 10**9, bytes_accessed=2**22, transcendentals=0)
    middle = separator // TILE - 1
    half_kernel = functools.partial(corner_kernel, order=separator, count=count, devices=devices)
    state_one, state_two, heads = pl.pallas_call(
        functools.partial(half_kernel, first=0, last=middle),
        out_shape=(state, state, jax.ShapeDtypeStruct((2, SLAB, separator), f32)),
        in_specs=[vmem] * (2 * devices),
        out_specs=(vmem, vmem, vmem),
        scratch_shapes=[scratch],
        compiler_params=small,
        cost_estimate=cost,
        name="corner_first",
    )(kept, *slabs[1:], *other_slabs, *far_slabs, *other_far_slabs)

    other_edges = [from_front(after(piece, heads), 1) for piece in near_edges]
    far = [far_wide[:, len(chosen) * TILE :]]
    far += [from_sibling(after(body, heads)) for body in bodies]
    far_edges = spread([after(far_edge, heads)])
    inverse = pl.pallas_call(
        functools.partial(half_kernel, first=middle, last=separator // TILE),
        out_shape=state,
        in_specs=[vmem, vmem],
        out_specs=vmem,
        scratch_shapes=[pltpu.VMEM((2, separator, separator), f32), scratch],
        compiler_params=small,
        cost_estimate=cost,
        name="corner_second",
    )(after(state_one, far_edge, *other_edges), state_two)

    sizes = dict(count=count, skip=skip, devices=devices)
    panel_space = pltpu.VMEM((devices, sent, separator), bf16)
    update_shape = jax.ShapeDtypeStruct((rows, M2 - TILE), f32)
    large = pltpu.CompilerParams(vmem_limit_bytes=VMEM_BYTES // 2)
    leaf_panel, column, total = pl.pallas_call(
        functools.partial(own_kernel, width=width, **sizes),
        out_shape=(
            jax.ShapeDtypeStruct((rows, separator), f32),
            jax.ShapeDtypeStruct((M2, TILE), f32),
            jax.ShapeDtypeStruct((rows + TILE, M2), f32),
        ),
        in_specs=[smem] + [vmem] * (5 + devices),
        out_specs=(vmem, vmem, vmem),
        scratch_shapes=[panel_space, panel_space],
        compiler_params=large,
        cost_estimate=pl.CostEstimate(flops=2 * 10**9, bytes_accessed=2**22, transcendentals=0),
        name="own",
    )(table, heads, weights[None], kept, inverse, matrix, *near_edges, *other_edges)
    other_far_edges = [from_front(after(piece, column, far[1]), 1) for piece in far_edges]
    parent_panel, update = pl.pallas_call(
        functools.partial(parent_kernel, width=width, **sizes),
        out_shape=(jax.ShapeDtypeStruct((rows, TILE), f32), update_shape),
        in_specs=[smem] + [vmem] * (3 + devices),
        out_specs=(vmem, hbm),
        scratch_shapes=[
            panel_space,
            panel_space,
            pltpu.VMEM((M2, TILE), f32),
            pltpu.VMEM((M2, 3 * TILE), bf16),
            pltpu.VMEM((M2, 3 * TILE), bf16),
            pltpu.VMEM((rows + TILE, M2), f32),
            pltpu.VMEM((TILE, TILE), f32),
            pltpu.SemaphoreType.DMA((M2 // 512,)),
        ],
        compiler_params=large,
        cost_estimate=pl.CostEstimate(flops=2 * 10**9, bytes_accessed=2**22, transcendentals=0),
        name="parent",
    )(table, inverse, column, total, *far_edges, *other_far_edges)
    update = pl.pallas_call(
        functools.partial(far_kernel, cuts=cuts, **sizes),
        out_shape=update_shape,
        in_specs=[smem] + [vmem] * len(far) + [hbm],
        out_specs=hbm,
        scratch_shapes=[
            pltpu.VMEM((devices * (count - skip) ** 2, TILE, TILE), f32),
            pltpu.SemaphoreType.DMA((devices * (count - skip) ** 2,)),
            pltpu.SemaphoreType.DMA((devices * (count - skip) ** 2,)),
        ],
        input_output_aliases={1 + len(far): 0},
        compiler_params=large,
        cost_estimate=pl.CostEstimate(flops=2 * 10**9, bytes_accessed=2**22, transcendentals=0),
        name="far",
    )(table, *far, update)
    return leaf_panel, parent_panel, update


def on_device(leaf_fronts, screen_weights, parent_tile_index):
    results = [
        one_front(leaf_fronts[0, g], screen_weights[0, g], parent_tile_index[:, g])
        for g in range(leaf_fronts.shape[1])
    ]
    return tuple(jnp.stack(parts)[None] for parts in zip(*results))


def solution(mesh):
    in_specs = (P("leaf", None, "front", None), P("leaf", None, "front"), P())
    out_specs = (
        P("leaf", None, "front", None),
        P("leaf", None, "front", None),
        P("leaf", None, "front", None),
    )
    return jax.shard_map(
        on_device, mesh=mesh, in_specs=in_specs, out_specs=out_specs, check_vma=False
    )
```

```python
import functools

import jax
import jax.numpy as jnp
from jax import lax
from jax.experimental import pallas as pl
from jax.experimental.pallas import tpu as pltpu
from jax.sharding import PartitionSpec as P

SEP2 = 1024
PANEL_WIDTH = 128
M2 = 4096
GROUP_TILES = 4
SLAB = 8
GROUP = 32
STEP = 16
VMEM_BYTES = 60 * 2**20

TILE = PANEL_WIDTH
LAST = ((1,), (1,))
PLAIN = ((1,), (0,))
FIRST = ((0,), (0,))


def from_front(value, distance):
    pairs = [(source, source ^ distance) for source in range(lax.axis_size("front"))]
    return lax.ppermute(value, "front", pairs)


def from_sibling(value):
    pairs = [(source, source ^ 1) for source in range(lax.axis_size("leaf"))]
    return lax.ppermute(value, "leaf", pairs)


def after(value, *events):
    return lax.optimization_barrier((value, *events))[0]


def slot_of(offset, count):
    slot, bit, weight = 0, 1, count // 2
    while weight:
        slot = slot + jnp.where((offset & bit) != 0, weight, 0)
        bit, weight = bit * 2, weight // 2
    return slot


def offset_of(slot, count):
    offset, bit, weight = 0, 1, count // 2
    while weight:
        offset += bit if slot & weight else 0
        bit, weight = bit * 2, weight // 2
    return offset


def exact_dot(left, right, contract):
    def parts(value):
        high = value.astype(jnp.bfloat16)
        value = value - high.astype(jnp.float32)
        middle = value.astype(jnp.bfloat16)
        return high, middle, (value - middle.astype(jnp.float32)).astype(jnp.bfloat16)

    left, right = parts(left), parts(right)
    left = jnp.concatenate([left[k] for k in (0, 0, 1, 0, 1, 2)], axis=contract[0][0])
    right = jnp.concatenate([right[k] for k in (0, 1, 0, 2, 1, 0)], axis=contract[1][0])
    return lax.dot_general(left, right, (contract, ((), ())), preferred_element_type=jnp.float32)


def plain_dot(left, right):
    return lax.dot_general(left, right, (LAST, ((), ())), preferred_element_type=jnp.float32)


def halves(value):
    high = value.astype(jnp.bfloat16)
    return high, (value - high.astype(jnp.float32)).astype(jnp.bfloat16)


def split_dot(left, right):
    return plain_dot(left[0], right[0]) + (plain_dot(left[0], right[1]) + plain_dot(left[1], right[0]))


def lane(row, index):
    return jnp.broadcast_to(row[:, index : index + 1], row.shape)


def sum_tree(terms):
    while len(terms) > 1:
        terms = [sum(terms[i : i + 2]) for i in range(0, len(terms), 2)]
    return terms[0]


def factor_slab(rows, first, inside, lanes):
    size = len(rows)
    entry = {(i, j): lane(rows[i], first + j) for i in range(size) for j in range(i + 1)}
    rows = [jnp.where(inside, jnp.where(lanes == first + i, 1.0, 0.0), row) for i, row in enumerate(rows)]
    done = []
    for p in range(0, size, 2):
        r = p + 1
        one, mixed, two = entry[p, p], entry[r, p], entry[r, r]
        inverse_one = pl.reciprocal(one, approx=True)
        inverse_two = pl.reciprocal(one * two - mixed * mixed, approx=True) * one
        factor = {i: entry[i, p] * inverse_one for i in range(r, size)}
        rows[r] = rows[r] - factor[r] * rows[p]
        for i in range(p + 2, size):
            entry[i, r] = entry[i, r] - factor[i] * mixed
        for i in range(p + 2, size):
            second = entry[i, r] * inverse_two
            for k in range(p + 2, i + 1):
                entry[i, k] = (entry[i, k] - factor[i] * entry[k, p]) - second * entry[k, r]
            rows[i] = (rows[i] - factor[i] * rows[p]) - second * rows[r]
        done.append(rows[p] * lax.rsqrt(one))
        done.append(rows[r] * (inverse_two * lax.rsqrt(inverse_two)))
    return done


def row_of(q):
    return pl.ds(q, TILE, stride=SLAB)


def clear_rows(a):
    row_ids = lax.broadcasted_iota(jnp.int32, a.shape, 0) & -SLAB
    col_ids = lax.broadcasted_iota(jnp.int32, a.shape, 1) * SLAB
    a[...] = (row_ids == col_ids).astype(jnp.float32)


def factor_steps(a, fronts):
    lanes = lax.broadcasted_iota(jnp.int32, (SLAB, TILE), 1)
    columns = lax.broadcasted_iota(jnp.int32, (TILE, TILE), 1)
    settled = (lax.broadcasted_iota(jnp.int32, (GROUP, TILE), 0) & -STEP) + STEP

    def at(i):
        return pl.ds(SLAB * i, SLAB)

    for start in range(0, TILE, GROUP):
        stop = start + GROUP
        rows = [a[at(i), :] for i in range(start, stop)]
        for s in range(0, GROUP, STEP):
            first = start + s
            inside = (lanes >= first) & (lanes < first + STEP)
            head = factor_slab(rows[s : s + STEP], first, inside, lanes)
            for i in range(STEP):
                a[at(first + i), :] = head[i]
            for i in range(s + STEP, GROUP):
                terms = [lane(row, start + i) * row for row in head]
                rows[i] = jnp.where(inside, 0.0, rows[i]) - sum_tree(terms)
            if s + STEP < GROUP:
                yield
        if stop < TILE:
            for q in range(fronts):
                upper = a[pl.ds(SLAB * start + q, GROUP, stride=SLAB), :]
                rest = pl.ds(SLAB * stop + q, TILE - stop, stride=SLAB)
                inverse = jnp.where((columns[:GROUP] >= start + settled) & (columns[:GROUP] < stop), 0.0, upper)
                product = exact_dot(upper, inverse, FIRST)[stop:]
                group = columns[stop:]
                kept = jnp.where((group >= start) & (group < stop), 0.0, a[rest, :])
                a[rest, :] = kept - product
        yield


def factor_blocks(a):
    sublanes = lax.broadcasted_iota(jnp.int32, (SLAB, TILE), 0)
    lanes = lax.broadcasted_iota(jnp.int32, (SLAB, TILE), 1)
    for start in range(0, TILE, SLAB):
        inside = (lanes >= start) & (lanes < start + SLAB)
        block = a[start : start + SLAB, :]
        rows = [jnp.broadcast_to(block[i : i + 1, :], block.shape) for i in range(SLAB)]
        rows = factor_slab(rows, start, inside, lanes)
        for low in range(start + SLAB, TILE, SLAB):
            chosen = sublanes + low
            terms = [jnp.take_along_axis(row, chosen, axis=1) * row for row in rows]
            block = a[low : low + SLAB, :]
            a[low : low + SLAB, :] = jnp.where(inside, 0.0, block) - sum_tree(terms)
        block = rows[0]
        for i in range(1, SLAB):
            block = jnp.where(sublanes == i, rows[i], block)
        a[start : start + SLAB, :] = block
        yield


def place():
    leaf, front = lax.axis_index("leaf"), lax.axis_index("front")
    return leaf, front, leaf & 1


def corner_kernel(*refs, order, first, last, count, devices):
    tiles = order // TILE
    pieces = 2 * devices
    if first == 0:
        slabs, (work, out, heads, a) = refs[:pieces], refs[pieces:]
    else:
        old_work, old_out, out, work, a = refs
    fronts = out.shape[0]
    if first == 0:
        front = place()[1]

        def copy(owner, q, take):
            slot = slot_of(front ^ owner, devices)
            for s in range(devices):

                @pl.when(slot == s)
                def _():
                    take(slabs[q * devices + s])

        for q in range(fronts):
            for e in range(tiles):

                def take_tile(slab):
                    work[q, e * TILE : (e + 1) * TILE, :] = slab[:TILE, :]

                copy(e * GROUP_TILES // count, q, take_tile)

            def take_head(slab):
                heads[q] = slab[TILE:, :]

            copy(0, q, take_head)
    else:
        work[...] = old_work[...]
        out[...] = old_out[...]

    clear_rows(a)

    def step(k, carry):
        block = pl.ds(pl.multiple_of(k * TILE, TILE), TILE)
        for q in range(fronts):
            a[row_of(q), :] = work[q, block, block]
        for _ in factor_steps(a, fronts):
            pass
        kept = lax.broadcasted_iota(jnp.int32, (TILE, TILE), 0) >= lax.broadcasted_iota(jnp.int32, (TILE, TILE), 1)
        for q in range(fronts):
            out[q, block, block] = jnp.where(kept, a[row_of(q), :], 0.0)
        for fixed in range(first, last):

            @pl.when(k == fixed)
            def _():
                here = slice(fixed * TILE, (fixed + 1) * TILE)
                low, rest = slice(0, fixed * TILE), slice((fixed + 1) * TILE, order)
                for q in range(fronts):
                    corner = out[q, here, here]
                    if fixed:
                        chain = exact_dot(work[q, here, low], out[q, low, low], PLAIN)
                        out[q, here, low] = -exact_dot(corner, chain, PLAIN)
                    if fixed + 1 < tiles:
                        out[q, here, rest] = jnp.zeros((TILE, order - (fixed + 1) * TILE), jnp.float32)
                        below = exact_dot(work[q, rest, here], corner, LAST)
                        work[q, rest, here] = below
                        work[q, rest, rest] = work[q, rest, rest] - exact_dot(below, below, LAST)

        return carry

    lax.fori_loop(first, last, step, 0)


def at(tile):
    return pl.ds(pl.multiple_of(tile * TILE, TILE), TILE)


def goal_of(table, i, tile):
    entry = 3 * (tile >> 2) + (tile & 3) - 1
    return jnp.where((tile & 3) == 0, -1, table[place()[0] ^ i, jnp.maximum(entry, 0)])


def panel_of(inverse):
    turned = halves(inverse)
    cut = inverse.shape[0] // 2
    top = tuple(part[:cut, :cut] for part in turned)
    bottom = tuple(part[cut:, :] for part in turned)

    def product(block):
        full = halves(block)
        left = split_dot(tuple(part[:, :cut] for part in full), top)
        return jnp.concatenate([left, split_dot(full, bottom)], axis=1)

    return product


def add_columns(table, i, edges, panel_high, panel_low, column, *, count, skip, devices):
    front = place()[1]
    separator = panel_high.shape[2]
    first = slice((1 - skip) * TILE, (2 - skip) * TILE)
    slot = slot_of(front, devices)
    one = panel_high[slot, first, :], panel_low[slot, first, :]
    for s in range(devices):
        piece = edges[s][:, separator:] - split_dot((panel_high[s], panel_low[s]), one)
        owner = front ^ offset_of(s, devices)
        for t in range(count - skip):
            target = goal_of(table, i, owner * count + skip + t)

            @pl.when(target >= 0)
            def _():
                column[at(target), :] += piece[t * TILE : (t + 1) * TILE, :]


def own_kernel(*refs, count, skip, width, devices):
    table, heads, weights, slab, inverse, fronts_here = refs[:6]
    edges = refs[6 : 6 + devices]
    leaf_panel, column, total, panel_high, panel_low = refs[6 + devices :]
    leaf, front, half = place()
    sent = count - skip
    separator = width // GROUP_TILES
    rows = count * TILE
    first_row = (front * 2 + half) * rows

    total[...] = jnp.zeros_like(total)
    column[...] = jnp.zeros_like(column)
    row_ids = lax.broadcasted_iota(jnp.int32, (TILE, TILE), 0)
    col_ids = lax.broadcasted_iota(jnp.int32, (TILE, TILE), 1)
    near = jnp.where(jnp.abs(row_ids - col_ids) == 1, 1.0, 0.0)
    before = jnp.where((row_ids == 0) & (col_ids == TILE - 1), 1.0, 0.0)
    behind = jnp.where((row_ids == TILE - 1) & (col_ids == 0), 1.0, 0.0)
    first_weights = jnp.where(half == 0, heads[0, 0:1, :TILE], heads[1, 0:1, :TILE])
    column[:TILE, :] = jnp.where(row_ids == col_ids, first_weights + 4.0, 0.0) - near
    column[TILE : 2 * TILE, :] = -before
    inside = first_row < SEP2
    weight = jnp.transpose(jnp.broadcast_to(weights[...], (TILE, rows)))
    for j in range(count):
        mine = (front * 2 + half) * count + j
        line = slice(j * TILE, (j + 1) * TILE)
        total[line, at(mine)] = jnp.where(
            row_ids == col_ids, weight[line, :] + jnp.where(inside, 4.0, 0.0), 0.0
        ) - jnp.where(inside, near, 0.0)

        @pl.when((mine > 0) & inside)
        def _():
            total[line, at(mine - 1)] = -before

        @pl.when((mine + 1) * TILE < SEP2)
        def _():
            total[line, at(mine + 1)] = -behind

    panel_from = panel_of(inverse[0])
    if skip:
        leaf_panel[:TILE, :] = panel_from(slab[:TILE, :])
    for s in range(devices):
        panel = panel_from(edges[s][:, :separator])
        if s == 0:
            leaf_panel[skip * TILE :, :] = panel
        panel_high[s], panel_low[s] = halves(panel)
    add_columns(table, 0, edges, panel_high, panel_low, column, count=count, skip=skip, devices=devices)

    for s in range(devices):
        product = split_dot((panel_high[0], panel_low[0]), (panel_high[s], panel_low[s]))
        for c in range(sent):
            tile = (front ^ offset_of(s, devices)) * count + skip + c
            goal = jnp.maximum(goal_of(table, 0, tile), 0)
            for t in range(sent):
                target = goal_of(table, 0, front * count + skip + t) - (front * 2 + half) * count
                target = jnp.where((target >= 0) & (target < count), target, count)
                line = slice(t * TILE, (t + 1) * TILE)
                source = fronts_here[(skip + t) * TILE : (skip + t + 1) * TILE, at(tile)]
                total[at(target), at(goal)] += source - product[line, c * TILE : (c + 1) * TILE]


def parent_kernel(*refs, count, skip, width, devices):
    table, inverse, column_in, total = refs[:4]
    edges = refs[4 : 4 + devices]
    panel_out, update_out = refs[4 + devices : 6 + devices]
    panel_high, panel_low, column, two_left, two_right, update, a, done = refs[6 + devices :]
    leaf, front, half = place()
    separator = width // GROUP_TILES
    rows = count * TILE
    sent = count - skip
    first_row = pl.multiple_of((front * 2 + half) * rows, TILE)

    column[...] = column_in[...]
    panel_from = panel_of(inverse[1])
    for s in range(devices):
        panel_high[s], panel_low[s] = halves(panel_from(edges[s][:, :separator]))
    add_columns(table, 1, edges, panel_high, panel_low, column, count=count, skip=skip, devices=devices)

    def copy(j):
        line = slice(j * TILE, (j + 1) * TILE)
        update[line, :] = total[line, :]

    def contribution(s):
        product = split_dot((panel_high[0], panel_low[0]), (panel_high[s], panel_low[s]))
        for c in range(sent):
            tile = (front ^ offset_of(s, devices)) * count + skip + c
            goal = jnp.maximum(goal_of(table, 1, tile), 0)
            for t in range(sent):
                target = goal_of(table, 1, front * count + skip + t) - (front * 2 + half) * count
                target = jnp.where((target >= 0) & (target < count), target, count)
                update[at(target), at(goal)] -= product[t * TILE : (t + 1) * TILE, c * TILE : (c + 1) * TILE]

    work = [functools.partial(copy, j) for j in range(count)]
    work += [functools.partial(contribution, s) for s in range(devices)]
    steps, tasks = TILE // SLAB, len(work)
    update[rows:, :] = jnp.zeros_like(update[rows:, :])
    a[...] = column[:TILE, :]
    for k, _ in enumerate(factor_blocks(a)):
        while work and len(work) * steps >= (steps - k) * tasks:
            work.pop(0)()
    for task in work:
        task()
    row_ids = lax.broadcasted_iota(jnp.int32, (TILE, TILE), 0)
    col_ids = lax.broadcasted_iota(jnp.int32, (TILE, TILE), 1)
    turned = halves(jnp.where(row_ids >= col_ids, a[...], 0.0))
    for start in range(0, M2, 1024):
        block = slice(start, start + 1024)
        panel = split_dot(halves(column[block, :]), turned)
        column[block, :] = panel
        high, low = halves(panel)
        two_left[block, :] = jnp.concatenate([high, high, low], axis=1)
        two_right[block, :] = jnp.concatenate([high, low, high], axis=1)
    mine = pl.ds(first_row, rows)
    panel_out[...] = column[mine, :]
    own = two_left[mine, :]
    sends = []
    for start in range(TILE, M2, 512):
        stop = min(start + 512, M2)
        here = slice(start - TILE, stop - TILE)
        update[:rows, start:stop] = update[:rows, start:stop] - plain_dot(own, two_right[start:stop, :])
        send = pltpu.make_async_copy(update.at[:rows, start:stop], update_out.at[:, here], done.at[len(sends)])
        send.start()
        sends.append(send)
    for send in sends:
        send.wait()


def far_kernel(table, *refs, count, skip, devices, cuts):
    beyond, (update, out, tiles, got, put) = refs[: len(cuts) - 1], refs[len(cuts) - 1 :]
    leaf, front, half = place()
    sent = count - skip
    every = [(s, t, c) for s in range(devices) for t in range(sent) for c in range(sent)]

    def place_of(s, t, c):
        tile = (front ^ offset_of(s, devices)) * count + skip + c
        goal = goal_of(table, 1, tile)
        target = goal_of(table, 1, front * count + skip + t) - (front * 2 + half) * count
        valid = (goal > 0) & (target >= 0) & (target < count)
        index = (s * sent + t) * sent + c
        lies = out.at[at(jnp.clip(target, 0, count - 1)), at(jnp.maximum(goal - 1, 0))]
        return tile, index, valid, lies

    def fetch(index, lies):
        return pltpu.make_async_copy(lies, tiles.at[index], got.at[index])

    def store(index, lies):
        return pltpu.make_async_copy(tiles.at[index], lies, put.at[index])

    for s, t, c in every:
        _, index, valid, lies = place_of(s, t, c)

        @pl.when(valid)
        def _():
            fetch(index, lies).start()

    for s, t, c in every:
        tile, index, valid, lies = place_of(s, t, c)
        line = slice(t * TILE, (t + 1) * TILE)
        source = jnp.maximum(tile - (tile >> 2) - 2, 0)

        @pl.when(valid)
        def _():
            fetch(index, lies).wait()

            for part, low, high in zip(beyond, cuts, cuts[1:]):

                @pl.when((source >= low) & (source < high))
                def _():
                    tiles[index] += part[line, at(jnp.clip(source - low, 0, high - low - 1))]

            store(index, lies).start()

    for s, t, c in every:
        _, index, valid, lies = place_of(s, t, c)

        @pl.when(valid)
        def _():
            store(index, lies).wait()


def slab_kernel(matrix, weights, slab, kept, done, *, chosen):
    copies = [
        pltpu.make_async_copy(
            matrix.at[:TILE, t * TILE : (t + 1) * TILE], slab.at[:TILE, k * TILE : (k + 1) * TILE], done.at[k]
        )
        for k, t in enumerate(chosen)
    ]
    for copy in copies:
        copy.start()
    slab[TILE:, :] = jnp.zeros_like(slab[TILE:, :])
    slab[TILE : TILE + 1, : weights.shape[1]] = weights[...]
    for copy in copies:
        copy.wait()
    kept[...] = slab[...]


def body_kernel(matrix, *refs, skip, wanted):
    targets, done = refs[:-1], refs[-1]
    copies = []
    for target, tiles in zip(targets, wanted):
        filled = 0
        while filled < len(tiles):
            stop = filled + 1
            while stop < len(tiles) and tiles[stop] == tiles[stop - 1] + 1:
                stop += 1
            copies.append(
                pltpu.make_async_copy(
                    matrix.at[skip * TILE :, tiles[filled] * TILE : (tiles[stop - 1] + 1) * TILE],
                    target.at[:, filled * TILE : stop * TILE],
                    done.at[len(copies)],
                )
            )
            filled = stop
    for copy in copies:
        copy.start()
    for copy in copies:
        copy.wait()


def one_front(matrix, weights, table):
    rows, width = matrix.shape
    devices = lax.axis_size("front")
    count, tiles = rows // TILE, width // TILE
    skip = 1 if count % GROUP_TILES == 0 else 0
    separator = width // GROUP_TILES
    sent = (count - skip) * TILE
    distances = []
    while 2 ** (len(distances) + 1) < devices:
        distances.insert(0, 2 ** (len(distances) + 1))

    def spread(pieces):
        for distance in distances:
            pieces = pieces + [from_front(piece, distance) for piece in pieces]
        return pieces

    vmem = pl.BlockSpec(memory_space=pltpu.VMEM)
    smem = pl.BlockSpec(memory_space=pltpu.SMEM)
    hbm = pl.BlockSpec(memory_space=pl.ANY)
    f32, bf16 = jnp.float32, jnp.bfloat16
    params = pltpu.CompilerParams(vmem_limit_bytes=VMEM_BYTES)
    small = pltpu.CompilerParams(vmem_limit_bytes=VMEM_BYTES // 3)

    corner = list(range(0, tiles, GROUP_TILES))
    rest = [t for t in range(tiles) if t % GROUP_TILES and t != 1]
    slab, kept = pl.pallas_call(
        functools.partial(slab_kernel, chosen=corner),
        out_shape=(jax.ShapeDtypeStruct((TILE + SLAB, separator), f32),) * 2,
        in_specs=[hbm, vmem],
        out_specs=(vmem, vmem),
        scratch_shapes=[pltpu.SemaphoreType.DMA((len(corner),))],
        compiler_params=params,
        cost_estimate=pl.CostEstimate(flops=0, bytes_accessed=2**19, transcendentals=0),
        name="slab",
    )(matrix, weights[None])
    far_slab = from_sibling(slab)
    slabs = spread([slab])
    cuts = (0, 3, 7, len(rest))
    rest = [rest[low:high] for low, high in zip(cuts, cuts[1:])]
    chosen = corner + [1]
    wanted = [chosen, chosen + rest[0], *rest[1:]]
    edge, wide, *bodies = pl.pallas_call(
        functools.partial(body_kernel, skip=skip, wanted=wanted),
        out_shape=tuple(jax.ShapeDtypeStruct((sent, len(part) * TILE), f32) for part in wanted),
        in_specs=[hbm],
        out_specs=(vmem,) * len(wanted),
        scratch_shapes=[pltpu.SemaphoreType.DMA((4 * tiles,))],
        compiler_params=params,
        cost_estimate=pl.CostEstimate(flops=0, bytes_accessed=2**23, transcendentals=0),
        name="body",
    )(after(matrix, slab))
    far_slabs = spread([after(far_slab, edge, *slabs)])
    other_slabs = [from_front(piece, 1) for piece in slabs]
    other_far_slabs = [from_front(piece, 1) for piece in far_slabs]
    far_wide = from_sibling(after(wide, far_slab))
    far_edge = far_wide[:, : len(chosen) * TILE]
    near_edges = spread([after(edge, *far_slabs)])

    state = jax.ShapeDtypeStruct((2, separator, separator), f32)
    scratch = pltpu.VMEM((SLAB * TILE, TILE), f32)
    cost = pl.CostEstimate(flops=3 * 10**9, bytes_accessed=2**22, transcendentals=0)
    middle = separator // TILE - 1
    half_kernel = functools.partial(corner_kernel, order=separator, count=count, devices=devices)
    state_one, state_two, heads = pl.pallas_call(
        functools.partial(half_kernel, first=0, last=middle),
        out_shape=(state, state, jax.ShapeDtypeStruct((2, SLAB, separator), f32)),
        in_specs=[vmem] * (2 * devices),
        out_specs=(vmem, vmem, vmem),
        scratch_shapes=[scratch],
        compiler_params=small,
        cost_estimate=cost,
        name="corner_first",
    )(kept, *slabs[1:], *other_slabs, *far_slabs, *other_far_slabs)

    other_edges = [from_front(after(piece, heads), 1) for piece in near_edges]
    far = [far_wide[:, len(chosen) * TILE :]]
    far += [from_sibling(after(body, heads)) for body in bodies]
    far_edges = spread([after(far_edge, heads)])
    inverse = pl.pallas_call(
        functools.partial(half_kernel, first=middle, last=separator // TILE),
        out_shape=state,
        in_specs=[vmem, vmem],
        out_specs=vmem,
        scratch_shapes=[pltpu.VMEM((2, separator, separator), f32), scratch],
        compiler_params=small,
        cost_estimate=cost,
        name="corner_second",
    )(after(state_one, far_edge, *other_edges), state_two)

    sizes = dict(count=count, skip=skip, devices=devices)
    panel_space = pltpu.VMEM((devices, sent, separator), bf16)
    update_shape = jax.ShapeDtypeStruct((rows, M2 - TILE), f32)
    large = pltpu.CompilerParams(vmem_limit_bytes=VMEM_BYTES // 2)
    leaf_panel, column, total = pl.pallas_call(
        functools.partial(own_kernel, width=width, **sizes),
        out_shape=(
            jax.ShapeDtypeStruct((rows, separator), f32),
            jax.ShapeDtypeStruct((M2, TILE), f32),
            jax.ShapeDtypeStruct((rows + TILE, M2), f32),
        ),
        in_specs=[smem] + [vmem] * (5 + devices),
        out_specs=(vmem, vmem, vmem),
        scratch_shapes=[panel_space, panel_space],
        compiler_params=large,
        cost_estimate=pl.CostEstimate(flops=2 * 10**9, bytes_accessed=2**22, transcendentals=0),
        name="own",
    )(table, heads, weights[None], kept, inverse, matrix, *near_edges, *other_edges)
    other_far_edges = [from_front(after(piece, column, far[1]), 1) for piece in far_edges]
    parent_panel, update = pl.pallas_call(
        functools.partial(parent_kernel, width=width, **sizes),
        out_shape=(jax.ShapeDtypeStruct((rows, TILE), f32), update_shape),
        in_specs=[smem] + [vmem] * (3 + devices),
        out_specs=(vmem, hbm),
        scratch_shapes=[
            panel_space,
            panel_space,
            pltpu.VMEM((M2, TILE), f32),
            pltpu.VMEM((M2, 3 * TILE), bf16),
            pltpu.VMEM((M2, 3 * TILE), bf16),
            pltpu.VMEM((rows + TILE, M2), f32),
            pltpu.VMEM((TILE, TILE), f32),
            pltpu.SemaphoreType.DMA((M2 // 512,)),
        ],
        compiler_params=large,
        cost_estimate=pl.CostEstimate(flops=2 * 10**9, bytes_accessed=2**22, transcendentals=0),
        name="parent",
    )(table, inverse, column, total, *far_edges, *other_far_edges)
    update = pl.pallas_call(
        functools.partial(far_kernel, cuts=cuts, **sizes),
        out_shape=update_shape,
        in_specs=[smem] + [vmem] * len(far) + [hbm],
        out_specs=hbm,
        scratch_shapes=[
            pltpu.VMEM((devices * (count - skip) ** 2, TILE, TILE), f32),
            pltpu.SemaphoreType.DMA((devices * (count - skip) ** 2,)),
            pltpu.SemaphoreType.DMA((devices * (count - skip) ** 2,)),
        ],
        input_output_aliases={1 + len(far): 0},
        compiler_params=large,
        cost_estimate=pl.CostEstimate(flops=2 * 10**9, bytes_accessed=2**22, transcendentals=0),
        name="far",
    )(table, *far, update)
    return leaf_panel, parent_panel, update


def on_device(leaf_fronts, screen_weights, parent_tile_index):
    results = [
        one_front(leaf_fronts[0, g], screen_weights[0, g], parent_tile_index[:, g])
        for g in range(leaf_fronts.shape[1])
    ]
    return tuple(jnp.stack(parts)[None] for parts in zip(*results))


def solution(mesh):
    in_specs = (P("leaf", None, "front", None), P("leaf", None, "front"), P())
    out_specs = (
        P("leaf", None, "front", None),
        P("leaf", None, "front", None),
        P("leaf", None, "front", None),
    )
    return jax.shard_map(
        on_device, mesh=mesh, in_specs=in_specs, out_specs=out_specs, check_vma=False
    )
```
